256 devices in a mesh: dp: 32 (over z_hi, y, core), tensor: 8 (over z_lo, x).
Axes of the slice: x: 4, y: 4, z: 8 (z_hi: 4, z_lo: 2; z = z_hi * 2 + z_lo), core: 2. Of those that a mesh axis runs over, the one named last changes fastest.
Arguments:
- noisy_sample: float32 [4096, 28], P('dp'), may hold values from -5 to 5
- timestep: int32 [4096], P('dp'), may hold values from 0 to 99
- noise: float32 [4096, 28], P('dp'), may hold values from -5 to 5
- obs_feat: bfloat16 [4096, 1024], P('dp'), may hold values from -6 to 6
- step_w1: bfloat16 [256, 1024], replicated, may hold values from -0.75 to 0.75
- step_w2: bfloat16 [1024, 256], replicated, may hold values from -0.25 to 0.25
- film_weight: bfloat16 [1280, 2, 4096], P('dp', None, 'tensor'), may hold values from -0.25 to 0.25
- conv_in_w: bfloat16 [5, 7, 4096], P(None, None, 'tensor'), may hold values from -1 to 1
- residual_w: bfloat16 [7, 4096], P(None, 'tensor'), may hold values from -2 to 2
- conv_mid_w: bfloat16 [5, 4096, 4096], P(None, 'dp', 'tensor'), may hold values from -0.0390625 to 0.0390625
- out_w: bfloat16 [4096, 7], P('tensor'), may hold values from -0.1875 to 0.1875
- gain_one: float32 [4096], P('tensor'), may hold values from 0.4 to 1.6
- gain_two: float32 [4096], P('tensor'), may hold values from 0.4 to 1.6
Outputs:
- predicted_noise: float32 [4096, 28], P('dp')
- denoised: float32 [4096, 28], P('dp')
The draws below stay inside these ranges and needn't reach their ends.
All inputs are finite; a program needn't handle non-finite values.
Results may differ from the reference program's by a relative error of at most 0.0046.
Values may be sent and summed in bfloat16 or wider, within the bound.
No kernel may reach another device: no remote copies, remote signals or barrier semaphores. Data moves between devices by JAX's collectives and lax.ppermute only.
A program may use at most 192 MiB of HBM per device.

```python
import math
import jax
import jax.numpy as jnp
from jax import lax

C = 4096
ACT = 7
HORIZON = 4
TAPS = 5
GROUPS = 8
STEP = 256
STEP_HID = 1024
OBS_FEAT = 1024
TRAIN_STEPS = 100
COND = 1280
OBS = 4096


def set_ends(result, rng, smallest, largest):
    longest = result.shape.index(max(result.shape))
    spots = []
    for shift in (0, 1):
        where = [jax.random.randint(jax.random.fold_in(rng, axis), (), 0, length) for axis, length in enumerate(result.shape)]
        where[longest] = (where[longest] + shift) % result.shape[longest]
        spots.append(tuple(where))
    return result.at[spots[0]].set(smallest).at[spots[1]].set(largest)


def levels(key, shape, shards, smallest, largest):
    loudness, own = 1.0, jax.random.fold_in(key, 6)
    for axis_at, blocks in shards:
        heights = jnp.exp(jax.random.uniform(jax.random.fold_in(own, axis_at), (blocks,), jnp.float32, smallest / len(shards), largest / len(shards)))
        loudness = loudness * jnp.repeat(heights, shape[axis_at] // blocks).reshape([-1 if axis == axis_at else 1 for axis in range(len(shape))])
    return loudness


def scatter_about(own_key, dims, scale, bound, cuts=(), kind=jnp.bfloat16):
    values = scale * jax.random.normal(own_key, dims, jnp.float32)
    if cuts:
        values = values * levels(own_key, dims, cuts, -0.22, 0.18)
    return jnp.clip(values, -bound, bound).astype(kind)


def setup_inputs(seed: int = 0) -> dict:
    streams_of = jax.random.split(jax.random.key(seed), 14)
    noisy_sample = scatter_about(streams_of[0], (OBS, HORIZON * ACT), 1.0, 5.0, ((0, 32),), jnp.float32)
    timestep = set_ends(jax.random.randint(streams_of[1], (OBS,), 0, TRAIN_STEPS), jax.random.fold_in(streams_of[1], 1), 0, TRAIN_STEPS - 1).astype(jnp.int32)
    noise = scatter_about(streams_of[2], (OBS, HORIZON * ACT), 1.0, 5.0, ((0, 32),), jnp.float32)
    obs_feat = scatter_about(streams_of[3], (OBS, OBS_FEAT), 1.0, 6.0, ((0, 32),))
    step_w1 = scatter_about(streams_of[4], (STEP, STEP_HID), (STEP // 4) ** -0.5, 0.75)
    step_w2 = scatter_about(streams_of[5], (STEP_HID, STEP), (STEP_HID // 2) ** -0.5, 0.25)
    film_weight = scatter_about(streams_of[6], (COND, 2, C), (COND // 2) ** -0.5, 0.25, ((0, 32), (2, 8)))
    conv_in_w = scatter_about(streams_of[7], (TAPS, ACT, C), (TAPS * ACT) ** -0.5, 1.0, ((2, 8),))
    residual_w = scatter_about(streams_of[8], (ACT, C), ACT ** -0.5, 2.0, ((1, 8),))
    conv_mid_w = scatter_about(streams_of[9], (TAPS, C, C), (TAPS * C) ** -0.5, 0.0390625, ((1, 32), (2, 8)))
    out_w = scatter_about(streams_of[10], (C, ACT), (C // 4) ** -0.5, 0.1875, ((0, 8),))
    gain_one = jnp.clip(0.4 + 1.2 * jax.random.uniform(streams_of[11], (C,), jnp.float32) ** levels(streams_of[11], (C,), ((0, 8),), -0.2, 0.2), 0.4, 1.6)
    gain_two = jnp.clip(0.4 + 1.2 * jax.random.uniform(streams_of[12], (C,), jnp.float32) ** levels(streams_of[12], (C,), ((0, 8),), -0.2, 0.2), 0.4, 1.6)
    return dict(noisy_sample=noisy_sample, timestep=timestep, noise=noise, obs_feat=obs_feat, step_w1=step_w1, step_w2=step_w2, film_weight=film_weight, conv_in_w=conv_in_w, residual_w=residual_w, conv_mid_w=conv_mid_w, out_w=out_w, gain_one=gain_one, gain_two=gain_two)


def plan():
    pos = jnp.arange(TRAIN_STEPS + 1, dtype=jnp.float32) / TRAIN_STEPS
    curve = jnp.cos((pos + 0.008) / 1.008 * (math.pi / 2)) ** 2
    betas = jnp.minimum(1.0 - curve[1:] / curve[:-1], 0.999)
    return jnp.cumprod(1.0 - betas)

def lookup(table, steps):
    onehot = (steps[:, None] == jnp.arange(table.shape[0], dtype=jnp.int32)[None, :]).astype(jnp.float32)
    return lax.optimization_barrier(jnp.sum(onehot * table[None, :], axis=1))

def mish(value):
    return value * jnp.tanh(jax.nn.softplus(value))

def sinusoid(steps):
    half = STEP // 2
    freqs = jnp.exp(jnp.arange(half, dtype=jnp.float32) * (-math.log(10000.0) / (half - 1)))
    angles = steps.astype(jnp.float32)[:, None] * freqs[None, :]
    return jnp.concatenate([jnp.sin(angles), jnp.cos(angles)], axis=1)

def convolve(acts, weight):
    count, length, inner = acts.shape
    padded = jnp.pad(acts, ((0, 0), (2, 2), (0, 0)))
    total = jnp.zeros((count * length, weight.shape[2]), jnp.float32)
    for shift in range(TAPS):
        window = padded[:, shift:shift + length, :].reshape(count * length, inner)
        total = total + jnp.dot(window, weight[shift], preferred_element_type=jnp.float32)
    return total.reshape(count, length, weight.shape[2])

def group_norm(hidden, gain, groups):
    count, length, width = hidden.shape
    split = hidden.reshape(count, length, groups, width // groups)
    mean = lax.optimization_barrier(jnp.mean(split, axis=(1, 3), keepdims=True))
    var = lax.optimization_barrier(jnp.mean((split - mean) ** 2, axis=(1, 3), keepdims=True))
    normed = ((split - mean) / jnp.sqrt(var + 1e-05)).reshape(count, length, width)
    return normed * gain[None, None, :]

def denoise_step(sample, eps, noise, steps):
    alpha_bar = plan()
    now = lookup(alpha_bar, steps)[:, None]
    before = jnp.where(steps > 0, lookup(alpha_bar, jnp.maximum(steps - 1, 0)), 1.0)[:, None]
    beta_prod = 1.0 - now
    cur_alpha = now / before
    cur_beta = 1.0 - cur_alpha
    start = jnp.clip((sample - jnp.sqrt(beta_prod) * eps) / jnp.sqrt(now), -1.0, 1.0)
    mean = jnp.sqrt(before) * cur_beta / beta_prod * start + jnp.sqrt(cur_alpha) * (1.0 - before) / beta_prod * sample
    spread = jnp.sqrt((1.0 - before) / beta_prod * cur_beta)
    return mean + spread * noise

def reference(noisy_sample, timestep, noise, obs_feat, step_w1, step_w2, film_weight, conv_in_w, residual_w, conv_mid_w, out_w, gain_one, gain_two):
    count = noisy_sample.shape[0]
    sample_b = noisy_sample.reshape(count, HORIZON, ACT).astype(jnp.bfloat16)
    sinus = sinusoid(timestep).astype(jnp.bfloat16)
    step_hidden = mish(jnp.dot(sinus, step_w1, preferred_element_type=jnp.float32)).astype(jnp.bfloat16)
    step_feat = jnp.dot(step_hidden, step_w2, preferred_element_type=jnp.float32)
    cond = mish(jnp.concatenate([step_feat, obs_feat.astype(jnp.float32)], axis=1)).astype(jnp.bfloat16)
    film = jnp.dot(cond, film_weight.reshape(COND, 2 * C), preferred_element_type=jnp.float32)
    scale = film[:, :C]
    shift = film[:, C:]
    first = mish(group_norm(convolve(sample_b, conv_in_w), gain_one, GROUPS))
    act_one = (scale[:, None, :] * first + shift[:, None, :]).astype(jnp.bfloat16)
    skip = jnp.dot(sample_b.reshape(count * HORIZON, ACT), residual_w, preferred_element_type=jnp.float32).reshape(count, HORIZON, C)
    act_two = (mish(group_norm(convolve(act_one, conv_mid_w), gain_two, GROUPS)) + skip).astype(jnp.bfloat16)
    eps = jnp.dot(act_two.reshape(count * HORIZON, C), out_w, preferred_element_type=jnp.float32).reshape(count, HORIZON * ACT)
    denoised = denoise_step(noisy_sample, eps, noise, timestep)
    return (eps, denoised)
```

```python
import math

import jax
import jax.numpy as jnp
import numpy as np
from jax import lax
from jax.experimental import pallas as pl
from jax.experimental.pallas import tpu as pltpu
from jax.sharding import Mesh, PartitionSpec as P

C = 4096
ACT = 7
HORIZON = 4
TAPS = 5
GROUPS = 8
STEP = 256
TRAIN_STEPS = 100
COND = 1280

AXES = ("zq", "zp", "y", "core", "zl", "x")
SIZES = (2, 2, 4, 2, 2, 4)
DP = ("zq", "zp", "y", "core")
TENSOR = ("zl", "x")

OWN = 128
PAIR = 256
ROWS = HORIZON * PAIR
WIDE = 512
HALF = 256
WIN = 48
FILM_ROWS = 2 * PAIR + WIN

f32, bf16 = jnp.float32, jnp.bfloat16


def moves(where):
    pairs = []
    for here in np.ndindex(*SIZES):
        zq, zp, y, core, zl, x = here
        zh, y, core, zl, x = where(2 * zq + zp, y, core, zl, x)
        there = ((zh % 4) // 2, zh % 2, y % 4, core % 2, zl % 2, x % 4)
        pairs.append(
            (int(np.ravel_multi_index(here, SIZES)), int(np.ravel_multi_index(there, SIZES)))
        )
    return pairs


def mover(where):
    pairs = moves(where)
    return lambda array: lax.ppermute(array, AXES, pairs)


z_up = mover(lambda zh, y, core, zl, x: (zh + 1, y, core, zl, x))
z_down = mover(lambda zh, y, core, zl, x: (zh - 1, y, core, zl, x))
z_two = mover(lambda zh, y, core, zl, x: (zh + 2, y, core, zl, x))
z_pair = mover(lambda zh, y, core, zl, x: (zh ^ 1, y, core, zl, x))
y_up = mover(lambda zh, y, core, zl, x: (zh, y + 1, core, zl, x))
y_down = mover(lambda zh, y, core, zl, x: (zh, y - 1, core, zl, x))
cores = mover(lambda zh, y, core, zl, x: (zh, y, 1 - core, zl, x))
zl_swap = mover(lambda zh, y, core, zl, x: (zh, y, core, 1 - zl, x))
x_ring = mover(lambda zh, y, core, zl, x: (zh, y, core, zl, x + 1 - 2 * core))


def plan():
    pos = np.arange(TRAIN_STEPS + 1, dtype=np.float64) / TRAIN_STEPS
    curve = np.cos((pos + 0.008) / 1.008 * (math.pi / 2)) ** 2
    betas = np.minimum(1.0 - curve[1:] / curve[:-1], 0.999)
    return jnp.asarray(np.cumprod(1.0 - betas), f32)


def lookup(table, steps):
    onehot = (steps[:, None] == jnp.arange(table.shape[0], dtype=jnp.int32)[None, :]).astype(f32)
    return jnp.sum(onehot * table[None, :], axis=1)


def mish(value):
    return value * jnp.tanh(jax.nn.softplus(value))


def mish_by_exp(value):
    u = jnp.exp(jnp.minimum(value, 20.0))
    w = u * (u + 2.0)
    return value * (w / (w + 2.0))


def sinusoid(steps):
    half = STEP // 2
    freqs = jnp.exp(jnp.arange(half, dtype=f32) * (-math.log(10000.0) / (half - 1)))
    angles = steps.astype(f32)[:, None] * freqs[None, :]
    return jnp.concatenate([jnp.sin(angles), jnp.cos(angles)], axis=1)


def denoise_coefficients(steps):
    alpha_bar = plan()
    now = lookup(alpha_bar, steps)[:, None]
    before = jnp.where(steps > 0, lookup(alpha_bar, jnp.maximum(steps - 1, 0)), 1.0)[:, None]
    beta_prod = 1.0 - now
    cur_alpha = now / before
    cur_beta = 1.0 - cur_alpha
    return (
        jnp.sqrt(beta_prod),
        jnp.sqrt(now),
        jnp.sqrt(before) * cur_beta / beta_prod,
        jnp.sqrt(cur_alpha) * (1.0 - before) / beta_prod,
        jnp.sqrt((1.0 - before) / beta_prod * cur_beta),
    )


def params(mib, **more):
    return pltpu.CompilerParams(vmem_limit_bytes=mib * 2**20, **more)


def film_kernel(order_ref, cond_ref, mine_ref, sibling_ref, small_ref, out_ref):
    core = order_ref[16]
    mine = jnp.zeros((PAIR, WIDE), f32)
    other = jnp.zeros((PAIR, WIDE), f32)
    for r in range(16):
        rows = cond_ref[order_ref[r]]
        mine += jnp.dot(rows, mine_ref[r], preferred_element_type=f32)
        other += jnp.dot(rows, sibling_ref[r], preferred_element_type=f32)
    out_ref[pl.ds(pl.multiple_of(core * PAIR, PAIR), PAIR), :] = mine.astype(bf16)
    out_ref[pl.ds(pl.multiple_of((1 - core) * PAIR, PAIR), PAIR), :] = other.astype(bf16)
    out_ref[2 * PAIR :, :] = small_ref[...]


def film_of(order, cond_blocks, mine, sibling, small):
    return pl.pallas_call(
        film_kernel,
        out_shape=jax.ShapeDtypeStruct((FILM_ROWS, WIDE), bf16),
        in_specs=[pl.BlockSpec(memory_space=pltpu.SMEM)]
        + [pl.BlockSpec(memory_space=pltpu.VMEM)] * 4,
        out_specs=pl.BlockSpec(memory_space=pltpu.VMEM),
        compiler_params=params(24),
        cost_estimate=pl.CostEstimate(
            flops=2 * PAIR * COND * 2 * WIDE, bytes_accessed=4 * 2**20, transcendentals=0
        ),
        name="film",
    )(order, cond_blocks, mine, sibling, small)


def first_kernel(place_ref, window_ref, film_ref, *rest):
    out_ref, hidden_ref = rest[-2:]
    hidden_ref[...] = jnp.dot(
        window_ref[...], film_ref[2 * PAIR :, :], preferred_element_type=f32
    )
    gain = (
        film_ref[2 * PAIR + 35 : 2 * PAIR + 36, :].astype(f32)
        + film_ref[2 * PAIR + 36 : 2 * PAIR + 37, :].astype(f32)
    )
    some = 16

    @pl.loop(0, PAIR // some)
    def _(step):
        at = [pl.multiple_of(p * PAIR + step * some, some) for p in range(HORIZON)]
        hidden = [hidden_ref[pl.ds(a, some), :] for a in at]
        mean = jnp.sum(sum(hidden), axis=1, keepdims=True) * (1.0 / (HORIZON * WIDE))
        off = [h - mean for h in hidden]
        var = jnp.sum(sum(o * o for o in off), axis=1, keepdims=True) * (1.0 / (HORIZON * WIDE))
        inv = lax.rsqrt(var + 1e-05)
        scale = film_ref[pl.ds(at[0], some), :].astype(f32)
        shift = film_ref[pl.ds(at[1], some), :].astype(f32)
        for a, o in zip(at, off):
            out_ref[0, pl.ds(a, some), :] = (
                scale * mish_by_exp(o * inv * gain) + shift
            ).astype(bf16)


def first_of(place, window, film, before):
    more = [] if before is None else [before]
    return pl.pallas_call(
        first_kernel,
        out_shape=jax.ShapeDtypeStruct((8, ROWS, WIDE), bf16),
        grid_spec=pltpu.PrefetchScalarGridSpec(
            num_scalar_prefetch=1,
            grid=(1,),
            in_specs=[
                pl.BlockSpec((ROWS, WIN), lambda i, place: (0, 0)),
                pl.BlockSpec((FILM_ROWS, WIDE), lambda i, place: (0, 0)),
            ]
            + [pl.BlockSpec(memory_space=pl.ANY)] * len(more),
            out_specs=pl.BlockSpec((1, ROWS, WIDE), lambda i, place: (place[0], 0, 0)),
            scratch_shapes=[pltpu.VMEM((ROWS, WIDE), f32)],
        ),
        input_output_aliases={3: 0} if more else {},
        compiler_params=params(24),
        cost_estimate=pl.CostEstimate(
            flops=2 * ROWS * WIN * WIDE, bytes_accessed=2 * 2**20, transcendentals=ROWS * WIDE
        ),
        name="first",
    )(place, window, film, *more)


def mid_kernel(stats, place_ref, act_ref, weight_ref, *rest):
    rest = list(rest)
    stats_ref = rest.pop() if stats else None
    out_ref = rest.pop()
    j, q = pl.program_id(0), pl.program_id(1)

    @pl.when(jnp.logical_and(j == 0, q == 0))
    def _():
        out_ref[...] = rest[0][...] if rest else jnp.zeros_like(out_ref)

    for h in range(HORIZON):
        total = out_ref[h * PAIR : (h + 1) * PAIR, :]
        for p in range(HORIZON):
            k = p - h + 2
            if 0 <= k < TAPS:
                total += jnp.dot(
                    act_ref[0, p * PAIR : (p + 1) * PAIR, :],
                    weight_ref[:, 0, k].reshape(WIDE, HALF),
                    preferred_element_type=f32,
                )
        out_ref[h * PAIR : (h + 1) * PAIR, :] = total

    if stats:

        @pl.when(jnp.logical_and(j == pl.num_programs(0) - 1, q == 1))
        def _():
            parts = [out_ref[h * PAIR : (h + 1) * PAIR, :] for h in range(HORIZON)]
            mean = jnp.sum(sum(parts), axis=1, keepdims=True) * (1.0 / (HORIZON * HALF))
            spread = jnp.sum(sum((o - mean) ** 2 for o in parts), axis=1, keepdims=True)
            lane = lax.broadcasted_iota(jnp.int32, (PAIR, 128), 1)
            both = jnp.where(lane == 0, mean, jnp.where(lane == 1, spread, 0.0))
            stats_ref[...] = both.T[:8, :]


def mid_of(place, acts, weights, before, stats):
    pieces = weights.shape[1]
    more = [] if before is None else [before]
    whole = pl.BlockSpec((ROWS, HALF), lambda j, q, place: (0, 0))
    out_shape = [jax.ShapeDtypeStruct((ROWS, HALF), f32)]
    out_specs = [whole]
    if stats:
        out_shape.append(jax.ShapeDtypeStruct((8, PAIR), f32))
        out_specs.append(pl.BlockSpec((8, PAIR), lambda j, q, place: (0, 0)))

    def kernel(*refs):
        mid_kernel(stats, *refs)

    return pl.pallas_call(
        kernel,
        out_shape=out_shape,
        grid_spec=pltpu.PrefetchScalarGridSpec(
            num_scalar_prefetch=1,
            grid=(pieces, 2),
            in_specs=[
                pl.BlockSpec((1, ROWS, WIDE), lambda j, q, place: (place[2 * j + q], 0, 0)),
                pl.BlockSpec(
                    (4, 1, TAPS, OWN, HALF), lambda j, q, place: (q, j, 0, 0, 0)
                ),
            ]
            + [whole] * len(more),
            out_specs=out_specs,
        ),
        compiler_params=params(28),
        cost_estimate=pl.CostEstimate(
            flops=2 * pieces * 2 * 14 * PAIR * WIDE * HALF,
            bytes_accessed=pieces * 5 * 2**20,
            transcendentals=0,
        ),
        name="mid",
    )(place, acts, weights, *more)


def last_kernel(conv_ref, own_ref, other_ref, gain_ref, window_ref, res_ref, out_w_ref, eps_ref):
    rows = jnp.concatenate([own_ref[...], other_ref[...], jnp.zeros((112, PAIR), f32)], axis=0).T
    mean_a, spread_a = rows[:, 0:1], rows[:, 1:2]
    mean_b, spread_b = rows[:, 8:9], rows[:, 9:10]
    each = HORIZON * HALF
    mean = 0.5 * (mean_a + mean_b)
    var = (spread_a + spread_b + (mean_a - mean_b) ** 2 * (0.5 * each)) * (0.5 / each)
    inv = lax.rsqrt(var + 1e-05)
    total = jnp.zeros((32, PAIR), f32)
    for h in range(HORIZON):
        at = slice(h * PAIR, (h + 1) * PAIR)
        normed = (conv_ref[at, :] - mean) * inv * gain_ref[...]
        skip = jnp.dot(window_ref[at, :], res_ref[...], preferred_element_type=f32)
        act = (mish_by_exp(normed) + skip).astype(bf16)
        total += lax.dot_general(
            out_w_ref[h], act, (((1,), (1,)), ((), ())), preferred_element_type=f32
        )
    eps_ref[0] = total[:, :OWN]
    eps_ref[1] = total[:, OWN:]


def last_of(conv, own, other, gain, window, res, out_w):
    return pl.pallas_call(
        last_kernel,
        out_shape=jax.ShapeDtypeStruct((2, 32, OWN), f32),
        in_specs=[pl.BlockSpec(memory_space=pltpu.VMEM)] * 7,
        out_specs=pl.BlockSpec(memory_space=pltpu.VMEM),
        compiler_params=params(24),
        cost_estimate=pl.CostEstimate(
            flops=2 * ROWS * HALF * 80, bytes_accessed=2 * 2**20, transcendentals=ROWS * HALF
        ),
        name="last",
    )(conv, own, other, gain, window, res, out_w)


def body(
    noisy_sample,
    timestep,
    noise,
    obs_feat,
    step_w1,
    step_w2,
    film_weight,
    conv_in_w,
    residual_w,
    conv_mid_w,
    out_w,
    gain_one,
    gain_two,
):
    zq, zp, y, core, zl, x = (lax.axis_index(a) for a in AXES)
    zh = 2 * zq + zp

    keep = lax.dynamic_slice_in_dim(conv_mid_w, zp * HALF, HALF, 2)
    give = lax.dynamic_slice_in_dim(conv_mid_w, (1 - zp) * HALF, HALF, 2)
    w_own = lax.all_gather(keep[None], ("y", "core"), axis=0, tiled=False)
    w_rest = jnp.stack([z_up(give), z_down(give), z_two(keep)])
    w_rest = lax.all_gather(w_rest, ("y", "core"), axis=0, tiled=False)

    stay = lax.dynamic_index_in_dim(film_weight, core, 1, keepdims=False)
    go = lax.dynamic_index_in_dim(film_weight, 1 - core, 1, keepdims=False)
    come = cores(go)
    chip = jnp.where(
        core == 0, jnp.concatenate([stay, come]), jnp.concatenate([come, stay])
    )
    line = jnp.stack([chip, z_up(chip), z_down(chip), z_two(chip)])
    from_down, from_up = y_up(line), y_down(line)
    far_a, far_b = y_up(from_down[:2]), y_down(from_up[2:])
    mine = jnp.concatenate([line, from_down, from_up, far_a, far_b])
    sibling = cores(mine)
    dz = (0, -1, 1, 2)
    order = [((zh + dz[r % 4]) % 4) * 4 + (y + dy) % 4 for dy in (0, -1, 1, 2) for r in range(4)]
    order = jnp.stack(order + [core]).astype(jnp.int32)

    sample_b = noisy_sample.astype(bf16)
    sinus = sinusoid(timestep).astype(bf16)
    step_hidden = mish(jnp.dot(sinus, step_w1, preferred_element_type=f32)).astype(bf16)
    step_feat = jnp.dot(step_hidden, step_w2, preferred_element_type=f32)
    cond = mish(jnp.concatenate([step_feat, obs_feat.astype(f32)], axis=1)).astype(bf16)
    packed = jnp.concatenate([cond, jnp.pad(sample_b, ((0, 0), (0, 100)))], axis=1)
    partner = z_pair(packed)
    both = jnp.where(
        zp == 0, jnp.concatenate([packed, partner]), jnp.concatenate([partner, packed])
    )
    cond_blocks = both[:, :COND].reshape(PAIR, 16, 80).transpose(1, 0, 2)
    samples = jnp.pad(both[:, COND : COND + 28], ((0, 0), (14, 14)))
    window = jnp.concatenate([samples[:, 7 * p : 7 * p + 35] for p in range(HORIZON)])
    window = jnp.pad(window, ((0, 0), (0, WIN - 35)))

    coarse = lax.reduce_precision(gain_one, 8, 7)
    small = jnp.concatenate(
        [
            conv_in_w.reshape(TAPS * ACT, WIDE),
            coarse[None].astype(bf16),
            (gain_one - coarse)[None].astype(bf16),
            jnp.zeros((WIN - 37, WIDE), bf16),
        ]
    )
    film = film_of(order, cond_blocks, mine, sibling, small)

    a, b = [film], [zl_swap(film)]
    for _ in range(3):
        a.append(x_ring(a[-1]))
        b.append(x_ring(b[-1]))
    acts = None
    for side, step in ((0, 0), (0, 1), (1, 0), (0, 2), (1, 1), (0, 3), (1, 2), (1, 3)):
        owner = (x + step * (2 * core - 1)) % 4
        block = jnp.where(side == 0, zl, 1 - zl) * 4 + owner
        acts = first_of(
            block.reshape(1).astype(jnp.int32), window, (a if side == 0 else b)[step], acts
        )

    def blocks(*shifts):
        return jnp.stack([((zh + s) % 4) * 2 + q for s in shifts for q in range(2)]).astype(jnp.int32)

    [conv] = mid_of(blocks(0), acts, w_own, None, False)
    conv, stats = mid_of(blocks(-1, 1, 2), acts, w_rest, conv, True)
    other = z_pair(stats)

    out_h = lax.dynamic_slice_in_dim(out_w, zp * HALF, HALF, 0).T
    out_h = jnp.stack([jnp.pad(out_h, ((7 * h, 25 - 7 * h), (0, 0))) for h in range(HORIZON)])
    res_h = lax.dynamic_slice_in_dim(residual_w, zp * HALF, HALF, 1)
    res_h = jnp.pad(res_h, ((14, WIN - 21), (0, 0)))
    gain_h = lax.dynamic_slice_in_dim(gain_two, zp * HALF, HALF, 0)[None]
    part = last_of(conv, stats, other, gain_h, window, res_h, out_h)

    sent = jnp.broadcast_to(part[:, None], (2, 8, 32, OWN)).reshape(16, 32, OWN)
    got = lax.all_to_all(sent, ("zp", "zl", "x"), split_axis=0, concat_axis=0, tiled=True)
    eps = jnp.sum(got, axis=0).T[:, :28]

    root_b, root_a, of_start, of_sample, of_noise = denoise_coefficients(timestep)
    start = jnp.clip((noisy_sample - root_b * eps) / root_a, -1.0, 1.0)
    denoised = of_start * start + of_sample * noisy_sample + of_noise * noise
    return (eps, denoised)


def solution(mesh):
    fine = Mesh(mesh.devices.reshape(SIZES), AXES)
    return jax.shard_map(
        body,
        mesh=fine,
        in_specs=(
            P(DP, None),
            P(DP),
            P(DP, None),
            P(DP, None),
            P(),
            P(),
            P(DP, None, TENSOR),
            P(None, None, TENSOR),
            P(None, TENSOR),
            P(None, DP, TENSOR),
            P(TENSOR, None),
            P(TENSOR),
            P(TENSOR),
        ),
        out_specs=(P(DP, None), P(DP, None)),
        check_vma=False,
    )
```

```python
import math

import jax
import jax.numpy as jnp
import numpy as np
from jax import lax
from jax.experimental import pallas as pl
from jax.experimental.pallas import tpu as pltpu
from jax.sharding import Mesh, PartitionSpec as P

C = 4096
ACT = 7
HORIZON = 4
TAPS = 5
GROUPS = 8
STEP = 256
TRAIN_STEPS = 100
COND = 1280

AXES = ("zq", "zp", "y", "core", "zl", "x")
SIZES = (2, 2, 4, 2, 2, 4)
DP = ("zq", "zp", "y", "core")
TENSOR = ("zl", "x")

OWN = 128
PAIR = 256
ROWS = HORIZON * PAIR
WIDE = 512
HALF = 256
WIN = 48
FILM_ROWS = 2 * PAIR + WIN

f32, bf16 = jnp.float32, jnp.bfloat16


def moves(where):
    pairs = []
    for here in np.ndindex(*SIZES):
        zq, zp, y, core, zl, x = here
        zh, y, core, zl, x = where(2 * zq + zp, y, core, zl, x)
        there = ((zh % 4) // 2, zh % 2, y % 4, core % 2, zl % 2, x % 4)
        pairs.append(
            (int(np.ravel_multi_index(here, SIZES)), int(np.ravel_multi_index(there, SIZES)))
        )
    return pairs


def mover(where):
    pairs = moves(where)
    return lambda array: lax.ppermute(array, AXES, pairs)


z_up = mover(lambda zh, y, core, zl, x: (zh + 1, y, core, zl, x))
z_down = mover(lambda zh, y, core, zl, x: (zh - 1, y, core, zl, x))
z_two = mover(lambda zh, y, core, zl, x: (zh + 2, y, core, zl, x))
z_pair = mover(lambda zh, y, core, zl, x: (zh ^ 1, y, core, zl, x))
y_up = mover(lambda zh, y, core, zl, x: (zh, y + 1, core, zl, x))
y_down = mover(lambda zh, y, core, zl, x: (zh, y - 1, core, zl, x))
cores = mover(lambda zh, y, core, zl, x: (zh, y, 1 - core, zl, x))
zl_swap = mover(lambda zh, y, core, zl, x: (zh, y, core, 1 - zl, x))
y_ring = mover(lambda zh, y, core, zl, x: (zh, y + 1 - 2 * core, core, zl, x))
x_ring = mover(lambda zh, y, core, zl, x: (zh, y, core, zl, x + 1 - 2 * core))


def plan():
    pos = np.arange(TRAIN_STEPS + 1, dtype=np.float64) / TRAIN_STEPS
    curve = np.cos((pos + 0.008) / 1.008 * (math.pi / 2)) ** 2
    betas = np.minimum(1.0 - curve[1:] / curve[:-1], 0.999)
    return jnp.asarray(np.cumprod(1.0 - betas), f32)


def lookup(table, steps):
    onehot = (steps[:, None] == jnp.arange(table.shape[0], dtype=jnp.int32)[None, :]).astype(f32)
    return jnp.sum(onehot * table[None, :], axis=1)


def mish(value):
    return value * jnp.tanh(jax.nn.softplus(value))


def mish_by_exp(value):
    u = jnp.exp(jnp.minimum(value, 20.0))
    w = u * (u + 2.0)
    below = w + 2.0
    inv = pl.reciprocal(below, approx=True)
    inv = inv * (2.0 - below * inv)
    return value * (w * inv)


def tie(*arrays):
    return lax.optimization_barrier(arrays)


def sinusoid(steps):
    half = STEP // 2
    freqs = jnp.exp(jnp.arange(half, dtype=f32) * (-math.log(10000.0) / (half - 1)))
    angles = steps.astype(f32)[:, None] * freqs[None, :]
    return jnp.concatenate([jnp.sin(angles), jnp.cos(angles)], axis=1)


def denoise_coefficients(steps):
    alpha_bar = plan()
    now = lookup(alpha_bar, steps)[:, None]
    before = jnp.where(steps > 0, lookup(alpha_bar, jnp.maximum(steps - 1, 0)), 1.0)[:, None]
    beta_prod = 1.0 - now
    cur_alpha = now / before
    cur_beta = 1.0 - cur_alpha
    return (
        jnp.sqrt(beta_prod),
        jnp.sqrt(now),
        jnp.sqrt(before) * cur_beta / beta_prod,
        jnp.sqrt(cur_alpha) * (1.0 - before) / beta_prod,
        jnp.sqrt((1.0 - before) / beta_prod * cur_beta),
    )


def params(mib, **more):
    return pltpu.CompilerParams(vmem_limit_bytes=mib * 2**20, **more)


def film_kernel(order_ref, cond_ref, mine_ref, sibling_ref, small_ref, out_ref):
    core = order_ref[16]
    mine = jnp.zeros((PAIR, WIDE), f32)
    other = jnp.zeros((PAIR, WIDE), f32)
    for r in range(16):
        rows = cond_ref[order_ref[r]]
        mine += jnp.dot(rows, mine_ref[r], preferred_element_type=f32)
        other += jnp.dot(rows, sibling_ref[r], preferred_element_type=f32)
    out_ref[pl.ds(pl.multiple_of(core * PAIR, PAIR), PAIR), :] = mine.astype(bf16)
    out_ref[pl.ds(pl.multiple_of((1 - core) * PAIR, PAIR), PAIR), :] = other.astype(bf16)
    out_ref[2 * PAIR :, :] = small_ref[...]


def film_of(order, cond_blocks, mine, sibling, small):
    return pl.pallas_call(
        film_kernel,
        out_shape=jax.ShapeDtypeStruct((FILM_ROWS, WIDE), bf16),
        in_specs=[pl.BlockSpec(memory_space=pltpu.SMEM)]
        + [pl.BlockSpec(memory_space=pltpu.VMEM)] * 4,
        out_specs=pl.BlockSpec(memory_space=pltpu.VMEM),
        compiler_params=params(24),
        cost_estimate=pl.CostEstimate(
            flops=2 * PAIR * COND * 2 * WIDE, bytes_accessed=4 * 2**20, transcendentals=0
        ),
        name="film",
    )(order, cond_blocks, mine, sibling, small)


def first_kernel(slot, window_ref, film_ref, *rest):
    out_ref, hidden_ref = rest[-2:]
    hidden_ref[...] = jnp.dot(
        window_ref[...], film_ref[2 * PAIR :, :], preferred_element_type=f32
    )
    gain = (
        film_ref[2 * PAIR + 35 : 2 * PAIR + 36, :].astype(f32)
        + film_ref[2 * PAIR + 36 : 2 * PAIR + 37, :].astype(f32)
    )

    def lanes(value):
        return sum(value[:, c : c + 128] for c in range(0, WIDE, 128))

    some, few = 64, 16

    @pl.loop(0, PAIR // some)
    def _(step):
        at = [pl.multiple_of(p * PAIR + step * some, some) for p in range(HORIZON)]
        total = sum(lanes(hidden_ref[pl.ds(a, some), :]) for a in at)
        mean = jnp.sum(total, axis=1, keepdims=True) * (1.0 / (HORIZON * WIDE))
        total = sum(lanes((hidden_ref[pl.ds(a, some), :] - mean) ** 2) for a in at)
        var = jnp.sum(total, axis=1, keepdims=True) * (1.0 / (HORIZON * WIDE))
        inv = lax.rsqrt(var + 1e-05)
        for r in range(0, some, few):
            base = step * some + r
            scale = film_ref[pl.ds(pl.multiple_of(base, few), few), :].astype(f32)
            shift = film_ref[pl.ds(pl.multiple_of(PAIR + base, few), few), :].astype(f32)
            for p in range(HORIZON):
                a = pl.multiple_of(p * PAIR + base, few)
                normed = (hidden_ref[pl.ds(a, few), :] - mean[r : r + few]) * inv[r : r + few]
                out_ref[0, pl.ds(a, few), :] = (
                    scale * mish_by_exp(normed * gain) + shift
                ).astype(bf16)


def first_of(slot, window, film, before):
    more = [] if before is None else [before]
    return pl.pallas_call(
        lambda *refs: first_kernel(slot, *refs),
        out_shape=jax.ShapeDtypeStruct((8, ROWS, WIDE), bf16),
        grid=(1,),
        in_specs=[
            pl.BlockSpec((ROWS, WIN), lambda i: (0, 0)),
            pl.BlockSpec((FILM_ROWS, WIDE), lambda i: (0, 0)),
        ]
        + [pl.BlockSpec(memory_space=pl.ANY)] * len(more),
        out_specs=pl.BlockSpec((1, ROWS, WIDE), lambda i: (slot, 0, 0)),
        scratch_shapes=[pltpu.VMEM((ROWS, WIDE), f32)],
        input_output_aliases={2: 0} if more else {},
        compiler_params=params(56),
        cost_estimate=pl.CostEstimate(
            flops=2 * ROWS * WIN * WIDE, bytes_accessed=2 * 2**20, transcendentals=ROWS * WIDE
        ),
        name="first",
    )(window, film, *more)


def mid_kernel(count, stats, place_ref, act_ref, own_ref, near_ref, mine_ref, theirs_ref, *rest):
    rest = list(rest)
    sems, held = rest.pop(), rest.pop()
    stats_ref = rest.pop() if stats else None
    out_ref = rest.pop()
    i = pl.program_id(0)
    zh, y, core = place_ref[0], place_ref[1], place_ref[2]

    def fetch(step, slot):
        block = place_ref[3 + step]
        q, apart = block % 2, (block // 2 + 4 - zh) % 4
        into, sem = held.at[slot], sems.at[slot]

        @pl.when(apart == 0)
        def _():
            pltpu.make_async_copy(own_ref.at[pl.ds(4 * q, 4)], into, sem).start()

        for way, side in ((3, 0), (1, 1)):

            @pl.when(apart == way)
            def _():
                pltpu.make_async_copy(near_ref.at[pl.ds(4 * q, 4), side], into, sem).start()

        @pl.when(apart == 2)
        def _():
            for odd in range(2):
                for ref, its in ((mine_ref, core), (theirs_ref, 1 - core)):
                    steps = (1 - 2 * its) * (y - 2 * q - odd)
                    source = ref.at[(steps + 8) % 4]
                    pltpu.make_async_copy(source, into.at[2 * odd + its], sem).start()

    @pl.when(i == 0)
    def _():
        fetch(0, 0)

    @pl.when(i + 1 < count)
    def _():
        fetch(i + 1, (i + 1) % 2)

    @pl.when(i == 0)
    def _():
        out_ref[...] = rest[0][...] if rest else jnp.zeros_like(out_ref)

    slot = i % 2
    pltpu.make_async_copy(own_ref.at[pl.ds(0, 4)], held.at[slot], sems.at[slot]).wait()
    for k in (2, 1, 3, 0, 4):
        low, high = max(0, k - 2), min(HORIZON, HORIZON + k - 2)
        rows = jnp.dot(
            act_ref[0, low * PAIR : high * PAIR, :],
            held[slot, :, k].reshape(WIDE, HALF),
            preferred_element_type=f32,
        )
        out_ref[(low - k + 2) * PAIR : (high - k + 2) * PAIR, :] += rows

    if stats:

        @pl.when(i == count - 1)
        def _():
            parts = [out_ref[h * PAIR : (h + 1) * PAIR, :] for h in range(HORIZON)]
            mean = jnp.sum(sum(parts), axis=1, keepdims=True) * (1.0 / (HORIZON * HALF))
            spread = jnp.sum(sum((o - mean) ** 2 for o in parts), axis=1, keepdims=True)
            lane = lax.broadcasted_iota(jnp.int32, (PAIR, 128), 1)
            both = jnp.where(lane == 0, mean, jnp.where(lane == 1, spread, 0.0))
            stats_ref[...] = both.T[:8, :]


def mid_of(place, start, count, acts, weights, before, stats):
    more = [] if before is None else [before]
    whole = pl.BlockSpec((ROWS, HALF), lambda i: (0, 0))
    out_shape = [jax.ShapeDtypeStruct((ROWS, HALF), f32)]
    out_specs = [whole]
    if stats:
        out_shape.append(jax.ShapeDtypeStruct((8, PAIR), f32))
        out_specs.append(pl.BlockSpec((8, PAIR), lambda i: (0, 0)))
    return pl.pallas_call(
        lambda *refs: mid_kernel(count, stats, *refs),
        out_shape=out_shape,
        grid=(count,),
        in_specs=[
            pl.BlockSpec(memory_space=pltpu.SMEM),
            pl.BlockSpec((1, ROWS, WIDE), lambda i: (start + i, 0, 0)),
        ]
        + [pl.BlockSpec(memory_space=pl.ANY)] * 4
        + [whole] * len(more),
        out_specs=out_specs,
        scratch_shapes=[
            pltpu.VMEM((2, 4, TAPS, OWN, HALF), bf16),
            pltpu.SemaphoreType.DMA((2,)),
        ],
        compiler_params=params(56),
        cost_estimate=pl.CostEstimate(
            flops=2 * count * 14 * PAIR * WIDE * HALF,
            bytes_accessed=count * 5 * 2**19,
            transcendentals=0,
        ),
        name="mid",
    )(place, acts, *weights, *more)


def last_kernel(conv_ref, own_ref, other_ref, gain_ref, window_ref, res_ref, out_w_ref, eps_ref):
    rows = jnp.concatenate([own_ref[...], other_ref[...], jnp.zeros((112, PAIR), f32)], axis=0).T
    mean_a, spread_a = rows[:, 0:1], rows[:, 1:2]
    mean_b, spread_b = rows[:, 8:9], rows[:, 9:10]
    each = HORIZON * HALF
    mean = 0.5 * (mean_a + mean_b)
    var = (spread_a + spread_b + (mean_a - mean_b) ** 2 * (0.5 * each)) * (0.5 / each)
    inv = lax.rsqrt(var + 1e-05)
    total = jnp.zeros((32, PAIR), f32)
    for h in range(HORIZON):
        at = slice(h * PAIR, (h + 1) * PAIR)
        normed = (conv_ref[at, :] - mean) * inv * gain_ref[...]
        skip = jnp.dot(window_ref[at, :], res_ref[...], preferred_element_type=f32)
        act = (mish_by_exp(normed) + skip).astype(bf16)
        total += lax.dot_general(
            out_w_ref[h], act, (((1,), (1,)), ((), ())), preferred_element_type=f32
        )
    eps_ref[0] = total[:, :OWN]
    eps_ref[1] = total[:, OWN:]


def last_of(conv, own, other, gain, window, res, out_w):
    return pl.pallas_call(
        last_kernel,
        out_shape=jax.ShapeDtypeStruct((2, 32, OWN), f32),
        in_specs=[pl.BlockSpec(memory_space=pltpu.VMEM)] * 7,
        out_specs=pl.BlockSpec(memory_space=pltpu.VMEM),
        compiler_params=params(24),
        cost_estimate=pl.CostEstimate(
            flops=2 * ROWS * HALF * 80, bytes_accessed=2 * 2**20, transcendentals=ROWS * HALF
        ),
        name="last",
    )(conv, own, other, gain, window, res, out_w)


def body(
    noisy_sample,
    timestep,
    noise,
    obs_feat,
    step_w1,
    step_w2,
    film_weight,
    conv_in_w,
    residual_w,
    conv_mid_w,
    out_w,
    gain_one,
    gain_two,
):
    zq, zp, y, core, zl, x = (lax.axis_index(a) for a in AXES)
    zh = 2 * zq + zp

    stay = lax.dynamic_index_in_dim(film_weight, core, 1, keepdims=False)
    go = lax.dynamic_index_in_dim(film_weight, 1 - core, 1, keepdims=False)
    come = cores(go)

    keep = lax.dynamic_slice_in_dim(conv_mid_w, zp * HALF, HALF, 2)
    give = lax.dynamic_slice_in_dim(conv_mid_w, (1 - zp) * HALF, HALF, 2)
    w_own = lax.all_gather(keep, ("y", "core"), axis=0, tiled=False)

    chip = jnp.where(
        core == 0, jnp.concatenate([stay, come]), jnp.concatenate([come, stay])
    )
    chip, give = tie(chip, give)
    line = jnp.stack([chip, z_up(chip), z_down(chip), z_two(chip)])
    w_up, w_down = z_up(give), z_down(give)

    sample_b = noisy_sample.astype(bf16)
    sinus = sinusoid(timestep).astype(bf16)
    step_hidden = mish(jnp.dot(sinus, step_w1, preferred_element_type=f32)).astype(bf16)
    step_feat = jnp.dot(step_hidden, step_w2, preferred_element_type=f32)
    cond = mish(jnp.concatenate([step_feat, obs_feat.astype(f32)], axis=1)).astype(bf16)
    packed = jnp.concatenate([cond, jnp.pad(sample_b, ((0, 0), (0, 100)))], axis=1)
    partner = z_pair(packed)

    from_down, from_up = y_up(line), y_down(line)
    from_down, from_up, partner, w_up, w_down, keep = tie(
        from_down, from_up, partner, w_up, w_down, keep
    )
    far_a, far_b = y_up(from_down[:2]), y_down(from_up[2:])
    w_near = lax.all_gather(jnp.stack([w_up, w_down]), ("y", "core"), axis=0, tiled=False)
    w_far = z_two(keep)

    both = jnp.where(
        zp == 0, jnp.concatenate([packed, partner]), jnp.concatenate([partner, packed])
    )
    cond_blocks = both[:, :COND].reshape(PAIR, 16, 80).transpose(1, 0, 2)
    samples = jnp.pad(both[:, COND : COND + 28], ((0, 0), (14, 14)))
    window = jnp.concatenate([samples[:, 7 * p : 7 * p + 35] for p in range(HORIZON)])
    window = jnp.pad(window, ((0, 0), (0, WIN - 35)))
    coarse = lax.reduce_precision(gain_one, 8, 7)
    small = jnp.concatenate(
        [
            conv_in_w.reshape(TAPS * ACT, WIDE),
            coarse[None].astype(bf16),
            (gain_one - coarse)[None].astype(bf16),
            jnp.zeros((WIN - 37, WIDE), bf16),
        ]
    )

    mine = jnp.concatenate([line, from_down, from_up, far_a, far_b])
    mine, cond_blocks, window, small = tie(mine, cond_blocks, window, small)
    sibling = cores(mine)
    dz = (0, -1, 1, 2)
    order = [((zh + dz[r % 4]) % 4) * 4 + (y + dy) % 4 for dy in (0, -1, 1, 2) for r in range(4)]
    order = jnp.stack(order + [core]).astype(jnp.int32)
    film = film_of(order, cond_blocks, mine, sibling, small)

    film, w_far = tie(film, w_far)
    a_one, b_own, far_one = x_ring(film), zl_swap(film), y_ring(w_far)
    acts = first_of(0, window, film, None)
    a_one, acts = tie(a_one, acts)
    a_two = x_ring(a_one)
    b_own, acts = tie(b_own, acts)
    b_one = x_ring(b_own)
    acts = first_of(1, window, a_one, acts)
    far_one, acts = tie(far_one, acts)
    far_two = y_ring(far_one)
    acts = first_of(2, window, b_own, acts)
    a_two, acts = tie(a_two, acts)
    a_three = x_ring(a_two)
    acts = first_of(3, window, a_two, acts)
    b_one, acts = tie(b_one, acts)
    b_two = x_ring(b_one)
    far_two, acts = tie(far_two, acts)
    far_three = y_ring(far_two)
    acts = first_of(4, window, b_one, acts)
    acts = first_of(5, window, a_three, acts)
    b_two, acts = tie(b_two, acts)
    b_three = x_ring(b_two)
    far_three, acts = tie(far_three, acts)
    far_mine = jnp.stack([w_far, far_one, far_two, far_three])
    far_theirs = cores(far_mine)
    acts = first_of(6, window, b_two, acts)

    side = (0, 0, 1, 0, 1, 0, 1, 1)
    step = (0, 1, 0, 2, 1, 3, 2, 3)
    slots = [
        (zl if b == 0 else 1 - zl) * 4 + (x + s * (2 * core - 1)) % 4 for b, s in zip(side, step)
    ]
    where = [zh, y, core]
    early = jnp.stack(where + slots[:7]).astype(jnp.int32)
    late = jnp.stack(where + slots[7:]).astype(jnp.int32)
    weights = (w_own, w_near, far_mine, far_theirs)
    [conv] = mid_of(early, 0, 7, acts, weights, None, False)
    acts, conv = tie(acts, conv)
    acts = first_of(7, window, b_three, acts)
    conv, stats = mid_of(late, 7, 1, acts, weights, conv, True)
    other = z_pair(stats)

    out_h = lax.dynamic_slice_in_dim(out_w, zp * HALF, HALF, 0).T
    out_h = jnp.stack([jnp.pad(out_h, ((7 * h, 25 - 7 * h), (0, 0))) for h in range(HORIZON)])
    res_h = lax.dynamic_slice_in_dim(residual_w, zp * HALF, HALF, 1)
    res_h = jnp.pad(res_h, ((14, WIN - 21), (0, 0)))
    gain_h = lax.dynamic_slice_in_dim(gain_two, zp * HALF, HALF, 0)[None]
    part = last_of(conv, stats, other, gain_h, window, res_h, out_h)

    sent = jnp.broadcast_to(part[:, None], (2, 8, 32, OWN)).reshape(16, 32, OWN)
    got = lax.all_to_all(sent, ("zp", "zl", "x"), split_axis=0, concat_axis=0, tiled=True)
    eps = jnp.sum(got, axis=0).T[:, :28]

    root_b, root_a, of_start, of_sample, of_noise = denoise_coefficients(timestep)
    start = jnp.clip((noisy_sample - root_b * eps) / root_a, -1.0, 1.0)
    denoised = of_start * start + of_sample * noisy_sample + of_noise * noise
    return (eps, denoised)


def solution(mesh):
    fine = Mesh(mesh.devices.reshape(SIZES), AXES)
    return jax.shard_map(
        body,
        mesh=fine,
        in_specs=(
            P(DP, None),
            P(DP),
            P(DP, None),
            P(DP, None),
            P(),
            P(),
            P(DP, None, TENSOR),
            P(None, None, TENSOR),
            P(None, TENSOR),
            P(None, DP, TENSOR),
            P(TENSOR, None),
            P(TENSOR),
            P(TENSOR),
        ),
        out_specs=(P(DP, None), P(DP, None)),
        check_vma=False,
    )
```

```python
import math

import jax
import jax.numpy as jnp
import numpy as np
from jax import lax
from jax.experimental import pallas as pl
from jax.experimental.pallas import tpu as pltpu
from jax.sharding import Mesh, PartitionSpec as P

C = 4096
ACT = 7
HORIZON = 4
TAPS = 5
GROUPS = 8
STEP = 256
TRAIN_STEPS = 100
COND = 1280

AXES = ("zq", "zp", "y", "core", "zl", "x")
SIZES = (2, 2, 4, 2, 2, 4)
DP = ("zq", "zp", "y", "core")
TENSOR = ("zl", "x")

OWN = 128
PAIR = 256
ROWS = HORIZON * PAIR
WIDE = 512
HALF = 256
WIN = 64
FILM_ROWS = 2 * PAIR + WIN

f32, bf16 = jnp.float32, jnp.bfloat16


def moves(where):
    pairs = []
    for here in np.ndindex(*SIZES):
        zq, zp, y, core, zl, x = here
        zh, y, core, zl, x = where(2 * zq + zp, y, core, zl, x)
        there = ((zh % 4) // 2, zh % 2, y % 4, core % 2, zl % 2, x % 4)
        pairs.append(
            (int(np.ravel_multi_index(here, SIZES)), int(np.ravel_multi_index(there, SIZES)))
        )
    return pairs


def mover(where):
    pairs = moves(where)
    return lambda array: lax.ppermute(array, AXES, pairs)


z_up = mover(lambda zh, y, core, zl, x: (zh + 1, y, core, zl, x))
z_down = mover(lambda zh, y, core, zl, x: (zh - 1, y, core, zl, x))
z_two = mover(lambda zh, y, core, zl, x: (zh + 2, y, core, zl, x))
z_pair = mover(lambda zh, y, core, zl, x: (zh ^ 1, y, core, zl, x))
y_up = mover(lambda zh, y, core, zl, x: (zh, y + 1, core, zl, x))
y_down = mover(lambda zh, y, core, zl, x: (zh, y - 1, core, zl, x))
cores = mover(lambda zh, y, core, zl, x: (zh, y, 1 - core, zl, x))
zl_swap = mover(lambda zh, y, core, zl, x: (zh, y, core, 1 - zl, x))
y_ring = mover(lambda zh, y, core, zl, x: (zh, y + 1 - 2 * core, core, zl, x))
x_ring = mover(lambda zh, y, core, zl, x: (zh, y, core, zl, x + 1 - 2 * core))


def plan():
    pos = np.arange(TRAIN_STEPS + 1, dtype=np.float64) / TRAIN_STEPS
    curve = np.cos((pos + 0.008) / 1.008 * (math.pi / 2)) ** 2
    betas = np.minimum(1.0 - curve[1:] / curve[:-1], 0.999)
    return jnp.asarray(np.cumprod(1.0 - betas), f32)


def lookup(table, steps):
    onehot = (steps[:, None] == jnp.arange(table.shape[0], dtype=jnp.int32)[None, :]).astype(f32)
    return jnp.sum(onehot * table[None, :], axis=1)


def mish(value):
    return value * jnp.tanh(jax.nn.softplus(value))


def mish_by_exp(value):
    u = jnp.exp(jnp.minimum(value, 20.0))
    w = u * (u + 2.0)
    return value * (w * pltpu.reciprocal(w + 2.0, approx=True))


def tie(*arrays):
    return lax.optimization_barrier(arrays)


def sinusoid(steps):
    half = STEP // 2
    freqs = jnp.exp(jnp.arange(half, dtype=f32) * (-math.log(10000.0) / (half - 1)))
    angles = steps.astype(f32)[:, None] * freqs[None, :]
    return jnp.concatenate([jnp.sin(angles), jnp.cos(angles)], axis=1)


def denoise_coefficients(steps):
    alpha_bar = plan()
    now = lookup(alpha_bar, steps)[:, None]
    before = jnp.where(steps > 0, lookup(alpha_bar, jnp.maximum(steps - 1, 0)), 1.0)[:, None]
    beta_prod = 1.0 - now
    cur_alpha = now / before
    cur_beta = 1.0 - cur_alpha
    return (
        jnp.sqrt(beta_prod),
        jnp.sqrt(now),
        jnp.sqrt(before) * cur_beta / beta_prod,
        jnp.sqrt(cur_alpha) * (1.0 - before) / beta_prod,
        jnp.sqrt((1.0 - before) / beta_prod * cur_beta),
    )


def params(mib, **more):
    return pltpu.CompilerParams(vmem_limit_bytes=mib * 2**20, **more)


def film_kernel(order_ref, cond_ref, mine_ref, sibling_ref, small_ref, out_ref):
    core = order_ref[16]
    mine = jnp.zeros((PAIR, WIDE), f32)
    other = jnp.zeros((PAIR, WIDE), f32)
    for r in range(16):
        rows = cond_ref[order_ref[r]]
        mine += jnp.dot(rows, mine_ref[r], preferred_element_type=f32)
        other += jnp.dot(rows, sibling_ref[r], preferred_element_type=f32)
    out_ref[pl.ds(pl.multiple_of(core * PAIR, PAIR), PAIR), :] = mine.astype(bf16)
    out_ref[pl.ds(pl.multiple_of((1 - core) * PAIR, PAIR), PAIR), :] = other.astype(bf16)
    out_ref[2 * PAIR :, :] = small_ref[...]


def film_of(order, cond_blocks, mine, sibling, small):
    return pl.pallas_call(
        film_kernel,
        out_shape=jax.ShapeDtypeStruct((FILM_ROWS, WIDE), bf16),
        in_specs=[pl.BlockSpec(memory_space=pltpu.SMEM)]
        + [pl.BlockSpec(memory_space=pltpu.VMEM)] * 4,
        out_specs=pl.BlockSpec(memory_space=pltpu.VMEM),
        compiler_params=params(24),
        cost_estimate=pl.CostEstimate(
            flops=2 * PAIR * COND * 2 * WIDE, bytes_accessed=4 * 2**20, transcendentals=0
        ),
        name="film",
    )(order, cond_blocks, mine, sibling, small)


IN_VMEM = pl.BlockSpec(memory_space=pltpu.VMEM)


IN_HBM = pl.BlockSpec(memory_space=pltpu.HBM)


def split_kernel(place_ref, weight_ref, keep_ref, give_ref):
    for ref, which in ((keep_ref, place_ref[0]), (give_ref, 1 - place_ref[0])):
        at = pl.ds(pl.multiple_of(which * HALF, HALF), HALF)
        for k in range(TAPS):
            ref[:, k * HALF : (k + 1) * HALF] = weight_ref[k, :, at]


def split_of(place, weight):
    return pl.pallas_call(
        split_kernel,
        out_shape=[jax.ShapeDtypeStruct((OWN, TAPS * HALF), bf16)] * 2,
        in_specs=[pl.BlockSpec(memory_space=pltpu.SMEM), IN_VMEM],
        out_specs=[IN_VMEM] * 2,
        compiler_params=params(16),
        name="split",
    )(place, weight)


def first_kernel(window_ref, film_ref, out_ref, hidden_ref, act_ref, sem):
    hidden_ref[...] = jnp.dot(
        window_ref[...], film_ref[2 * PAIR :, :], preferred_element_type=f32
    )
    gain = (
        film_ref[2 * PAIR + 35 : 2 * PAIR + 36, :].astype(f32)
        + film_ref[2 * PAIR + 36 : 2 * PAIR + 37, :].astype(f32)
    )

    def lanes(value):
        return sum(value[:, c : c + 128] for c in range(0, WIDE, 128))

    parts = [slice(p * PAIR, (p + 1) * PAIR) for p in range(HORIZON)]
    total = sum(lanes(hidden_ref[a, :]) for a in parts)
    mean = jnp.sum(total, axis=1, keepdims=True) * (1.0 / (HORIZON * WIDE))
    total = sum(lanes((hidden_ref[a, :] - mean) ** 2) for a in parts)
    var = jnp.sum(total, axis=1, keepdims=True) * (1.0 / (HORIZON * WIDE))
    inv = lax.rsqrt(var + 1e-05)
    few, some = 16, 64
    for r in range(0, PAIR, few):
        at = slice(r, r + few)
        scale = film_ref[at, :].astype(f32)
        shift = film_ref[PAIR + r : PAIR + r + few, :].astype(f32)
        for p in range(HORIZON):
            a = slice(p * PAIR + r, p * PAIR + r + few)
            normed = (hidden_ref[a, :] - mean[at]) * (inv[at] * gain)
            act_ref[p, at, :] = (scale * mish_by_exp(normed) + shift).astype(bf16)
        if (r + few) % some == 0:
            done = slice(r + few - some, r + few)
            pltpu.make_async_copy(act_ref.at[:, done], out_ref.at[:, done], sem).start()
    pltpu.make_async_copy(act_ref, out_ref, sem).wait()


def first_of(window, film):
    return pl.pallas_call(
        first_kernel,
        out_shape=jax.ShapeDtypeStruct((HORIZON, PAIR, WIDE), bf16),
        in_specs=[IN_VMEM, IN_VMEM],
        out_specs=IN_HBM,
        scratch_shapes=[
            pltpu.VMEM((ROWS, WIDE), f32),
            pltpu.VMEM((HORIZON, PAIR, WIDE), bf16),
            pltpu.SemaphoreType.DMA,
        ],
        compiler_params=params(56),
        cost_estimate=pl.CostEstimate(
            flops=2 * ROWS * WIN * WIDE, bytes_accessed=2 * 2**20, transcendentals=ROWS * WIDE
        ),
        name="first",
    )(window, film)


def mid_kernel(count, more, stats, place_ref, *refs):
    refs = list(refs)
    sems, act_held, held = refs.pop(), refs.pop(), refs.pop()
    stats_ref = refs.pop() if stats else None
    out_ref = refs.pop()
    before_ref = refs.pop() if more else None
    own_ref, near_ref, mine_ref, theirs_ref = refs[-4:]
    acts = refs[:-4]
    zh, y, core = place_ref[0], place_ref[1], place_ref[2]

    def fetch(step):
        block = place_ref[3 + step]
        q, apart = block % 2, (block // 2 + 4 - zh) % 4
        into, sem = held.at[step % 3], sems.at[0, step % 3]
        pltpu.make_async_copy(acts[step], act_held.at[step % 3], sems.at[1, step % 3]).start()

        @pl.when(apart == 0)
        def _():
            pltpu.make_async_copy(own_ref.at[pl.ds(4 * q, 4)], into, sem).start()

        for way, side in ((3, 0), (1, 1)):

            @pl.when(apart == way)
            def _():
                pltpu.make_async_copy(near_ref.at[pl.ds(4 * q, 4), side], into, sem).start()

        @pl.when(apart == 2)
        def _():
            for odd in range(2):
                for ref, its in ((mine_ref, core), (theirs_ref, 1 - core)):
                    steps = (1 - 2 * its) * (y - 2 * q - odd)
                    source = ref.at[(steps + 8) % 4]
                    pltpu.make_async_copy(source, into.at[2 * odd + its], sem).start()

    for step in range(min(2, count)):
        fetch(step)
    for step in range(count):
        if step + 2 < count:
            fetch(step + 2)
        into, act = held.at[step % 3], act_held.at[step % 3]
        pltpu.make_async_copy(own_ref.at[pl.ds(0, 4)], into, sems.at[0, step % 3]).wait()
        pltpu.make_async_copy(acts[step], act, sems.at[1, step % 3]).wait()
        for h in range(HORIZON):
            at = slice(h * PAIR, (h + 1) * PAIR)
            total = out_ref[at, :] if step else before_ref[at, :] if more else None
            for p in range(HORIZON):
                k = p - h + 2
                if 0 <= k < TAPS:
                    term = jnp.dot(
                        act[p],
                        into[:, :, k * HALF : (k + 1) * HALF].reshape(WIDE, HALF),
                        preferred_element_type=f32,
                    )
                    total = term if total is None else total + term
            out_ref[at, :] = total

    if stats:
        parts = [out_ref[h * PAIR : (h + 1) * PAIR, :] for h in range(HORIZON)]
        mean = jnp.sum(sum(parts), axis=1, keepdims=True) * (1.0 / (HORIZON * HALF))
        spread = jnp.sum(sum((o - mean) ** 2 for o in parts), axis=1, keepdims=True)
        lane = lax.broadcasted_iota(jnp.int32, (PAIR, 128), 1)
        both = jnp.where(lane == 0, mean, jnp.where(lane == 1, spread, 0.0))
        stats_ref[...] = both.T[:8, :]


def mid_of(place, acts, weights, before, stats):
    count, more = len(acts), [] if before is None else [before]
    out_shape = [jax.ShapeDtypeStruct((ROWS, HALF), f32)]
    if stats:
        out_shape.append(jax.ShapeDtypeStruct((8, PAIR), f32))
    return pl.pallas_call(
        lambda *refs: mid_kernel(count, bool(more), stats, *refs),
        out_shape=out_shape,
        in_specs=[pl.BlockSpec(memory_space=pltpu.SMEM)]
        + [IN_HBM] * (count + 4)
        + [IN_VMEM] * len(more),
        out_specs=[IN_VMEM] * len(out_shape),
        scratch_shapes=[
            pltpu.VMEM((3, 4, OWN, TAPS * HALF), bf16),
            pltpu.VMEM((3, HORIZON, PAIR, WIDE), bf16),
            pltpu.SemaphoreType.DMA((2, 3)),
        ],
        compiler_params=params(56),
        cost_estimate=pl.CostEstimate(
            flops=2 * count * 14 * PAIR * WIDE * HALF,
            bytes_accessed=count * 5 * 2**19,
            transcendentals=0,
        ),
        name="mid",
    )(place, *acts, *weights, *more)


def last_kernel(conv_ref, own_ref, other_ref, gain_ref, window_ref, res_ref, out_w_ref, eps_ref):
    rows = jnp.concatenate([own_ref[...], other_ref[...], jnp.zeros((112, PAIR), f32)], axis=0).T
    mean_a, spread_a = rows[:, 0:1], rows[:, 1:2]
    mean_b, spread_b = rows[:, 8:9], rows[:, 9:10]
    each = HORIZON * HALF
    mean = 0.5 * (mean_a + mean_b)
    var = (spread_a + spread_b + (mean_a - mean_b) ** 2 * (0.5 * each)) * (0.5 / each)
    inv = lax.rsqrt(var + 1e-05)
    total = jnp.zeros((32, PAIR), f32)
    for h in range(HORIZON):
        at = slice(h * PAIR, (h + 1) * PAIR)
        normed = (conv_ref[at, :] - mean) * inv * gain_ref[...]
        skip = jnp.dot(window_ref[at, :], res_ref[...], preferred_element_type=f32)
        act = (mish_by_exp(normed) + skip).astype(bf16)
        total += lax.dot_general(
            out_w_ref[h], act, (((1,), (1,)), ((), ())), preferred_element_type=f32
        )
    for b in range(2):
        part = total[:, b * OWN : (b + 1) * OWN].astype(bf16)
        for copy in range(8):
            eps_ref[8 * b + copy] = part


def last_of(conv, own, other, gain, window, res, out_w):
    return pl.pallas_call(
        last_kernel,
        out_shape=jax.ShapeDtypeStruct((16, 32, OWN), bf16),
        in_specs=[pl.BlockSpec(memory_space=pltpu.VMEM)] * 7,
        out_specs=pl.BlockSpec(memory_space=pltpu.VMEM),
        compiler_params=params(24),
        cost_estimate=pl.CostEstimate(
            flops=2 * ROWS * HALF * 80, bytes_accessed=2 * 2**20, transcendentals=ROWS * HALF
        ),
        name="last",
    )(conv, own, other, gain, window, res, out_w)


def body(
    noisy_sample,
    timestep,
    noise,
    obs_feat,
    step_w1,
    step_w2,
    film_weight,
    conv_in_w,
    residual_w,
    conv_mid_w,
    out_w,
    gain_one,
    gain_two,
):
    zq, zp, y, core, zl, x = (lax.axis_index(a) for a in AXES)
    zh = 2 * zq + zp

    packed = jnp.concatenate(
        [
            obs_feat,
            noisy_sample.astype(bf16),
            timestep.astype(f32).astype(bf16)[:, None],
            jnp.zeros((OWN, 99), bf16),
        ],
        axis=1,
    )
    partner = z_pair(packed)

    stay = lax.dynamic_index_in_dim(film_weight, core, 1, keepdims=False)
    go = lax.dynamic_index_in_dim(film_weight, 1 - core, 1, keepdims=False)
    come = cores(go)

    keep, give = split_of(zp.reshape(1).astype(jnp.int32), conv_mid_w)
    w_own = lax.all_gather(keep, ("y", "core"), axis=0, tiled=False)

    chip = jnp.where(
        core == 0, jnp.concatenate([stay, come]), jnp.concatenate([come, stay])
    )
    line = jnp.stack([chip, z_up(chip), z_down(chip), z_two(chip)])
    line, give = tie(line, give)
    from_down, from_up = y_up(line), y_down(line)
    w_up, w_down = z_up(give), z_down(give)
    far_a, far_b = y_up(from_down[:2]), y_down(from_up[2:])

    both = jnp.where(
        zp == 0, jnp.concatenate([packed, partner]), jnp.concatenate([partner, packed])
    )
    feat, tail = both[:, :1024], both[:, 1024:]
    sinus = sinusoid(tail[:, 28]).astype(bf16)
    step_hidden = mish(jnp.dot(sinus, step_w1, preferred_element_type=f32)).astype(bf16)
    step_feat = jnp.dot(step_hidden, step_w2, preferred_element_type=f32)
    cond = mish(jnp.concatenate([step_feat, feat.astype(f32)], axis=1)).astype(bf16)
    cond_blocks = cond.reshape(PAIR, 16, 80).transpose(1, 0, 2)
    samples = jnp.pad(tail[:, :28], ((0, 0), (14, 14)))
    window = jnp.concatenate([samples[:, 7 * p : 7 * p + 35] for p in range(HORIZON)])
    window = jnp.pad(window, ((0, 0), (0, WIN - 35)))
    coarse = lax.reduce_precision(gain_one, 8, 7)
    small = jnp.concatenate(
        [
            conv_in_w.reshape(TAPS * ACT, WIDE),
            coarse[None].astype(bf16),
            (gain_one - coarse)[None].astype(bf16),
            jnp.zeros((WIN - 37, WIDE), bf16),
        ]
    )

    far_a, far_b, w_up, w_down, keep, cond_blocks, window, small = tie(
        far_a, far_b, w_up, w_down, keep, cond_blocks, window, small
    )
    mine = jnp.concatenate([line, from_down, from_up, far_a, far_b])
    sibling = cores(mine)
    w_near = lax.all_gather(jnp.stack([w_up, w_down]), ("y", "core"), axis=0, tiled=False)
    w_far = z_two(keep)
    dz = (0, -1, 1, 2)
    order = [((zh + dz[r % 4]) % 4) * 4 + (y + dy) % 4 for dy in (0, -1, 1, 2) for r in range(4)]
    order = jnp.stack(order + [core]).astype(jnp.int32)
    film = film_of(order, cond_blocks, mine, sibling, small)

    a_one, b_own = x_ring(film), zl_swap(film)
    act_a0 = first_of(window, film)
    a_one, act_a0 = tie(a_one, act_a0)
    a_two = x_ring(a_one)
    w_far, b_own, act_a0 = tie(w_far, b_own, act_a0)
    far_one, b_one = y_ring(w_far), x_ring(b_own)
    act_a1 = first_of(window, a_one)
    act_b0 = first_of(window, b_own)
    a_two, act_a1, act_b0 = tie(a_two, act_a1, act_b0)
    a_three = x_ring(a_two)
    far_one, act_a1, act_b0 = tie(far_one, act_a1, act_b0)
    far_two = y_ring(far_one)
    act_a2 = first_of(window, a_two)
    b_one, act_a2 = tie(b_one, act_a2)
    b_two = x_ring(b_one)
    act_b1 = first_of(window, b_one)
    far_two, act_b1 = tie(far_two, act_b1)
    far_three = y_ring(far_two)
    act_a3 = first_of(window, a_three)
    b_two, act_a3 = tie(b_two, act_a3)
    b_three = x_ring(b_two)
    act_b2 = first_of(window, b_two)
    far_three, act_b2 = tie(far_three, act_b2)
    far_mine = jnp.stack([w_far, far_one, far_two, far_three])
    far_theirs = cores(far_mine)

    acts = (act_a0, act_a1, act_b0, act_a2, act_b1, act_a3, act_b2)
    side = (0, 0, 1, 0, 1, 0, 1, 1)
    step = (0, 1, 0, 2, 1, 3, 2, 3)
    slots = [
        (zl if b == 0 else 1 - zl) * 4 + (x + s * (2 * core - 1)) % 4 for b, s in zip(side, step)
    ]
    where = [zh, y, core]
    early = jnp.stack(where + slots[:7]).astype(jnp.int32)
    late = jnp.stack(where + slots[7:]).astype(jnp.int32)
    early, late, act_a0 = tie(early, late, act_a0)
    weights = (w_own, w_near, far_mine, far_theirs)
    [conv] = mid_of(early, acts, weights, None, False)
    b_three, conv = tie(b_three, conv)
    act_b3 = first_of(window, b_three)
    conv, stats = mid_of(late, (act_b3,), weights, conv, True)
    other = z_pair(stats)

    out_h = lax.dynamic_slice_in_dim(out_w, zp * HALF, HALF, 0).T
    out_h = jnp.stack([jnp.pad(out_h, ((7 * h, 25 - 7 * h), (0, 0))) for h in range(HORIZON)])
    res_h = lax.dynamic_slice_in_dim(residual_w, zp * HALF, HALF, 1)
    res_h = jnp.pad(res_h, ((14, WIN - 21), (0, 0)))
    gain_h = lax.dynamic_slice_in_dim(gain_two, zp * HALF, HALF, 0)[None]
    part = last_of(conv, stats, other, gain_h, window, res_h, out_h)

    got = lax.all_to_all(part, ("zp", "zl", "x"), split_axis=0, concat_axis=0, tiled=True)
    eps = jnp.sum(got.astype(f32), axis=0).T[:, :28]

    root_b, root_a, of_start, of_sample, of_noise = denoise_coefficients(timestep)
    start = jnp.clip((noisy_sample - root_b * eps) / root_a, -1.0, 1.0)
    denoised = of_start * start + of_sample * noisy_sample + of_noise * noise
    return (eps, denoised)


def solution(mesh):
    fine = Mesh(mesh.devices.reshape(SIZES), AXES)
    return jax.shard_map(
        body,
        mesh=fine,
        in_specs=(
            P(DP, None),
            P(DP),
            P(DP, None),
            P(DP, None),
            P(),
            P(),
            P(DP, None, TENSOR),
            P(None, None, TENSOR),
            P(None, TENSOR),
            P(None, DP, TENSOR),
            P(TENSOR, None),
            P(TENSOR),
            P(TENSOR),
        ),
        out_specs=(P(DP, None), P(DP, None)),
        check_vma=False,
    )
```

```python
import math

import jax
import jax.numpy as jnp
import numpy as np
from jax import lax
from jax.experimental import pallas as pl
from jax.experimental.pallas import tpu as pltpu
from jax.sharding import Mesh, PartitionSpec as P

C = 4096
ACT = 7
HORIZON = 4
TAPS = 5
GROUPS = 8
STEP = 256
TRAIN_STEPS = 100
COND = 1280

AXES = ("zq", "zp", "y", "core", "zl", "x")
SIZES = (2, 2, 4, 2, 2, 4)
DP = ("zq", "zp", "y", "core")
TENSOR = ("zl", "x")

OWN = 128
PAIR = 256
ROWS = HORIZON * PAIR
WIDE = 512
HALF = 256
WIN = 64
FILM_ROWS = 2 * PAIR + WIN

f32, bf16 = jnp.float32, jnp.bfloat16


def moves(where):
    pairs = []
    for here in np.ndindex(*SIZES):
        zq, zp, y, core, zl, x = here
        zh, y, core, zl, x = where(2 * zq + zp, y, core, zl, x)
        there = ((zh % 4) // 2, zh % 2, y % 4, core % 2, zl % 2, x % 4)
        pairs.append(
            (int(np.ravel_multi_index(here, SIZES)), int(np.ravel_multi_index(there, SIZES)))
        )
    return pairs


def mover(where):
    pairs = moves(where)
    return lambda array: lax.ppermute(array, AXES, pairs)


z_up = mover(lambda zh, y, core, zl, x: (zh + 1, y, core, zl, x))
z_down = mover(lambda zh, y, core, zl, x: (zh - 1, y, core, zl, x))
z_two = mover(lambda zh, y, core, zl, x: (zh + 2, y, core, zl, x))
z_pair = mover(lambda zh, y, core, zl, x: (zh ^ 1, y, core, zl, x))
y_up = mover(lambda zh, y, core, zl, x: (zh, y + 1, core, zl, x))
y_down = mover(lambda zh, y, core, zl, x: (zh, y - 1, core, zl, x))
cores = mover(lambda zh, y, core, zl, x: (zh, y, 1 - core, zl, x))
zl_swap = mover(lambda zh, y, core, zl, x: (zh, y, core, 1 - zl, x))
y_ring = mover(lambda zh, y, core, zl, x: (zh, y + 1 - 2 * core, core, zl, x))
x_ring = mover(lambda zh, y, core, zl, x: (zh, y, core, zl, x + 1 - 2 * core))


def plan():
    pos = np.arange(TRAIN_STEPS + 1, dtype=np.float64) / TRAIN_STEPS
    curve = np.cos((pos + 0.008) / 1.008 * (math.pi / 2)) ** 2
    betas = np.minimum(1.0 - curve[1:] / curve[:-1], 0.999)
    return jnp.asarray(np.cumprod(1.0 - betas), f32)


def lookup(table, steps):
    onehot = (steps[:, None] == jnp.arange(table.shape[0], dtype=jnp.int32)[None, :]).astype(f32)
    return jnp.sum(onehot * table[None, :], axis=1)


def mish(value):
    return value * jnp.tanh(jax.nn.softplus(value))


def mish_by_exp(value):
    u = jnp.exp(jnp.minimum(value, 20.0))
    w = u * (u + 2.0)
    return value * (w * pltpu.reciprocal(w + 2.0, approx=True))


def tie(*arrays):
    return lax.optimization_barrier(arrays)


def sinusoid(steps):
    half = STEP // 2
    freqs = jnp.exp(jnp.arange(half, dtype=f32) * (-math.log(10000.0) / (half - 1)))
    angles = steps.astype(f32)[:, None] * freqs[None, :]
    return jnp.concatenate([jnp.sin(angles), jnp.cos(angles)], axis=1)


def denoise_coefficients(steps):
    alpha_bar = plan()
    now = lookup(alpha_bar, steps)[:, None]
    before = jnp.where(steps > 0, lookup(alpha_bar, jnp.maximum(steps - 1, 0)), 1.0)[:, None]
    beta_prod = 1.0 - now
    cur_alpha = now / before
    cur_beta = 1.0 - cur_alpha
    return (
        jnp.sqrt(beta_prod),
        jnp.sqrt(now),
        jnp.sqrt(before) * cur_beta / beta_prod,
        jnp.sqrt(cur_alpha) * (1.0 - before) / beta_prod,
        jnp.sqrt((1.0 - before) / beta_prod * cur_beta),
    )


IN_VMEM = pl.BlockSpec(memory_space=pltpu.VMEM)
IN_HBM = pl.BlockSpec(memory_space=pltpu.HBM)
SLOTS = 16


def params(mib, **more):
    return pltpu.CompilerParams(vmem_limit_bytes=mib * 2**20, **more)


def film_kernel(order_ref, cond_ref, *refs):
    core = order_ref[16]
    mine_refs, sibling_refs, small_ref, out_ref = refs[:8], refs[8:16], refs[16], refs[17]
    mine = jnp.zeros((PAIR, WIDE), f32)
    other = jnp.zeros((PAIR, WIDE), f32)
    for r in range(16):
        rows = cond_ref[order_ref[r]]
        mine += jnp.dot(rows, mine_refs[r // 2][r % 2], preferred_element_type=f32)
        other += jnp.dot(rows, sibling_refs[r // 2][r % 2], preferred_element_type=f32)
    out_ref[pl.ds(pl.multiple_of(core * PAIR, PAIR), PAIR), :] = mine.astype(bf16)
    out_ref[pl.ds(pl.multiple_of((1 - core) * PAIR, PAIR), PAIR), :] = other.astype(bf16)
    out_ref[2 * PAIR :, :] = small_ref[...]


def film_of(order, cond_blocks, mine, sibling, small):
    return pl.pallas_call(
        film_kernel,
        out_shape=jax.ShapeDtypeStruct((FILM_ROWS, WIDE), bf16),
        in_specs=[pl.BlockSpec(memory_space=pltpu.SMEM)] + [IN_VMEM] * 18,
        out_specs=IN_VMEM,
        compiler_params=params(24),
        cost_estimate=pl.CostEstimate(
            flops=2 * PAIR * COND * 2 * WIDE, bytes_accessed=4 * 2**20, transcendentals=0
        ),
        name="film",
    )(order, cond_blocks, *mine, *sibling, small)


def split_kernel(place_ref, weight_ref, keep_ref, give_ref):
    for ref, which in ((keep_ref, place_ref[0]), (give_ref, 1 - place_ref[0])):
        at = pl.ds(pl.multiple_of(which * HALF, HALF), HALF)
        for k in range(TAPS):
            ref[:, k * HALF : (k + 1) * HALF] = weight_ref[k, :, at]


def split_of(place, weight):
    return pl.pallas_call(
        split_kernel,
        out_shape=[jax.ShapeDtypeStruct((OWN, TAPS * HALF), bf16)] * 2,
        in_specs=[pl.BlockSpec(memory_space=pltpu.SMEM), IN_VMEM],
        out_specs=[IN_VMEM] * 2,
        compiler_params=params(16),
        name="split",
    )(place, weight)


def first_rows(window_ref, film_ref, hidden_ref, act_ref, after):
    hidden_ref[...] = jnp.dot(
        window_ref[...], film_ref[2 * PAIR :, :], preferred_element_type=f32
    )
    gain = (
        film_ref[2 * PAIR + 35 : 2 * PAIR + 36, :].astype(f32)
        + film_ref[2 * PAIR + 36 : 2 * PAIR + 37, :].astype(f32)
    )

    def lanes(value):
        return sum(value[:, c : c + 128] for c in range(0, WIDE, 128))

    parts = [slice(p * PAIR, (p + 1) * PAIR) for p in range(HORIZON)]
    total = sum(lanes(hidden_ref[a, :]) for a in parts)
    mean = jnp.sum(total, axis=1, keepdims=True) * (1.0 / (HORIZON * WIDE))
    total = sum(lanes((hidden_ref[a, :] - mean) ** 2) for a in parts)
    var = jnp.sum(total, axis=1, keepdims=True) * (1.0 / (HORIZON * WIDE))
    inv = lax.rsqrt(var + 1e-05)
    few = 16
    for r in range(0, PAIR, few):
        at = slice(r, r + few)
        scale = film_ref[at, :].astype(f32)
        shift = film_ref[PAIR + r : PAIR + r + few, :].astype(f32)
        for p in range(HORIZON):
            a = slice(p * PAIR + r, p * PAIR + r + few)
            normed = (hidden_ref[a, :] - mean[at]) * (inv[at] * gain)
            act_ref[p, at, :] = (scale * mish_by_exp(normed) + shift).astype(bf16)
        after(r + few)


def first_kernel(slot, window_ref, film_ref, *rest):
    out_ref, hidden_ref, act_ref, sem = rest[-4:]
    out_ref, some = out_ref.at[slot], 64

    def after(rows):
        if rows % some == 0:
            done = slice(rows - some, rows)
            pltpu.make_async_copy(act_ref.at[:, done], out_ref.at[:, done], sem).start()

    first_rows(window_ref, film_ref, hidden_ref, act_ref, after)
    pltpu.make_async_copy(act_ref, out_ref, sem).wait()


def first_of(slot, window, film, before):
    more = [] if before is None else [before]
    return pl.pallas_call(
        lambda *refs: first_kernel(slot, *refs),
        out_shape=jax.ShapeDtypeStruct((SLOTS, HORIZON, PAIR, WIDE), bf16),
        in_specs=[IN_VMEM, IN_VMEM] + [IN_HBM] * len(more),
        out_specs=IN_HBM,
        scratch_shapes=[
            pltpu.VMEM((ROWS, WIDE), f32),
            pltpu.VMEM((HORIZON, PAIR, WIDE), bf16),
            pltpu.SemaphoreType.DMA,
        ],
        input_output_aliases={2: 0} if more else {},
        compiler_params=params(46),
        cost_estimate=pl.CostEstimate(flops=1, bytes_accessed=1, transcendentals=0),
        name="first",
    )(window, film, *more)


def fetch_weights(place_ref, block, refs, into, sem):
    own_ref, near_ref, mine_ref, theirs_ref = refs
    zh, y, core = place_ref[0], place_ref[1], place_ref[2]
    q, apart = block % 2, (block // 2 + 4 - zh) % 4

    @pl.when(apart == 0)
    def _():
        pltpu.make_async_copy(own_ref.at[pl.ds(4 * q, 4)], into, sem).start()

    for way, side in ((3, 0), (1, 1)):

        @pl.when(apart == way)
        def _():
            pltpu.make_async_copy(near_ref.at[pl.ds(4 * q, 4), side], into, sem).start()

    @pl.when(apart == 2)
    def _():
        for odd in range(2):
            for ref, its in ((mine_ref, core), (theirs_ref, 1 - core)):
                steps = (1 - 2 * its) * (y - 2 * q - odd)
                source = ref.at[(steps + 8) % 4]
                pltpu.make_async_copy(source, into.at[2 * odd + its], sem).start()


def add_block(act, weight, before_ref, out_ref):
    for h in range(HORIZON):
        at = slice(h * PAIR, (h + 1) * PAIR)
        total = None if before_ref is None else before_ref[at, :]
        for p in range(HORIZON):
            k = p - h + 2
            if 0 <= k < TAPS:
                term = jnp.dot(
                    act[p],
                    weight[:, :, k * HALF : (k + 1) * HALF].reshape(WIDE, HALF),
                    preferred_element_type=f32,
                )
                total = term if total is None else total + term
        out_ref[at, :] = total


def mid_kernel(count, place_ref, acts_ref, *refs):
    out_ref, held, act_held, sems = refs[-4:]
    weights = refs[:4]

    def fetch(step):
        at = step % 3
        pltpu.make_async_copy(acts_ref.at[step], act_held.at[at], sems.at[1, at]).start()
        fetch_weights(place_ref, place_ref[3 + step], weights, held.at[at], sems.at[0, at])

    for step in range(2):
        fetch(step)
    for step in range(count):
        if step + 2 < count:
            fetch(step + 2)
        at = step % 3
        pltpu.make_async_copy(weights[0].at[pl.ds(0, 4)], held.at[at], sems.at[0, at]).wait()
        pltpu.make_async_copy(acts_ref.at[step], act_held.at[at], sems.at[1, at]).wait()
        add_block(act_held.at[at], held.at[at], out_ref if step else None, out_ref)


def mid_of(place, count, acts, weights):
    return pl.pallas_call(
        lambda *refs: mid_kernel(count, *refs),
        out_shape=jax.ShapeDtypeStruct((ROWS, HALF), f32),
        in_specs=[pl.BlockSpec(memory_space=pltpu.SMEM)] + [IN_HBM] * 5,
        out_specs=IN_VMEM,
        scratch_shapes=[
            pltpu.VMEM((3, 4, OWN, TAPS * HALF), bf16),
            pltpu.VMEM((3, HORIZON, PAIR, WIDE), bf16),
            pltpu.SemaphoreType.DMA((2, 3)),
        ],
        compiler_params=params(56),
        cost_estimate=pl.CostEstimate(flops=1, bytes_accessed=1, transcendentals=0),
        name="mid",
    )(place, acts, *weights)


def end_kernel(place_ref, window_ref, film_ref, before_ref, *refs):
    out_ref, stats_ref, hidden_ref, act_ref, held, sem = refs[-6:]
    weights = refs[:4]
    fetch_weights(place_ref, place_ref[3], weights, held, sem)
    first_rows(window_ref, film_ref, hidden_ref, act_ref, lambda rows: None)
    pltpu.make_async_copy(weights[0].at[pl.ds(0, 4)], held, sem).wait()
    add_block(act_ref, held, before_ref, out_ref)
    parts = [out_ref[h * PAIR : (h + 1) * PAIR, :] for h in range(HORIZON)]
    mean = jnp.sum(sum(parts), axis=1, keepdims=True) * (1.0 / (HORIZON * HALF))
    spread = jnp.sum(sum((o - mean) ** 2 for o in parts), axis=1, keepdims=True)
    lane = lax.broadcasted_iota(jnp.int32, (PAIR, 128), 1)
    both = jnp.where(lane == 0, mean, jnp.where(lane == 1, spread, 0.0))
    stats_ref[...] = both.T[:8, :]


def end_of(place, window, film, before, weights):
    return pl.pallas_call(
        end_kernel,
        out_shape=[
            jax.ShapeDtypeStruct((ROWS, HALF), f32),
            jax.ShapeDtypeStruct((8, PAIR), f32),
        ],
        in_specs=[pl.BlockSpec(memory_space=pltpu.SMEM)] + [IN_VMEM] * 3 + [IN_HBM] * 4,
        out_specs=[IN_VMEM] * 2,
        scratch_shapes=[
            pltpu.VMEM((ROWS, WIDE), f32),
            pltpu.VMEM((HORIZON, PAIR, WIDE), bf16),
            pltpu.VMEM((4, OWN, TAPS * HALF), bf16),
            pltpu.SemaphoreType.DMA,
        ],
        compiler_params=params(57),
        cost_estimate=pl.CostEstimate(flops=1, bytes_accessed=1, transcendentals=0),
        name="end",
    )(place, window, film, before, *weights)


def last_kernel(conv_ref, own_ref, other_ref, gain_ref, window_ref, res_ref, out_w_ref, eps_ref):
    rows = jnp.concatenate([own_ref[...], other_ref[...], jnp.zeros((112, PAIR), f32)], axis=0).T
    mean_a, spread_a = rows[:, 0:1], rows[:, 1:2]
    mean_b, spread_b = rows[:, 8:9], rows[:, 9:10]
    each = HORIZON * HALF
    mean = 0.5 * (mean_a + mean_b)
    var = (spread_a + spread_b + (mean_a - mean_b) ** 2 * (0.5 * each)) * (0.5 / each)
    inv = lax.rsqrt(var + 1e-05)
    total = jnp.zeros((32, PAIR), f32)
    for h in range(HORIZON):
        at = slice(h * PAIR, (h + 1) * PAIR)
        normed = (conv_ref[at, :] - mean) * inv * gain_ref[...]
        skip = jnp.dot(window_ref[at, :], res_ref[...], preferred_element_type=f32)
        act = (mish_by_exp(normed) + skip).astype(bf16)
        total += lax.dot_general(
            out_w_ref[h], act, (((1,), (1,)), ((), ())), preferred_element_type=f32
        )
    for b in range(2):
        part = total[:, b * OWN : (b + 1) * OWN].astype(bf16)
        for copy in range(8):
            eps_ref[8 * b + copy] = part


def last_of(conv, own, other, gain, window, res, out_w):
    return pl.pallas_call(
        last_kernel,
        out_shape=jax.ShapeDtypeStruct((16, 32, OWN), bf16),
        in_specs=[pl.BlockSpec(memory_space=pltpu.VMEM)] * 7,
        out_specs=pl.BlockSpec(memory_space=pltpu.VMEM),
        compiler_params=params(24),
        cost_estimate=pl.CostEstimate(
            flops=2 * ROWS * HALF * 80, bytes_accessed=2 * 2**20, transcendentals=ROWS * HALF
        ),
        name="last",
    )(conv, own, other, gain, window, res, out_w)


def body(
    noisy_sample,
    timestep,
    noise,
    obs_feat,
    step_w1,
    step_w2,
    film_weight,
    conv_in_w,
    residual_w,
    conv_mid_w,
    out_w,
    gain_one,
    gain_two,
):
    zq, zp, y, core, zl, x = (lax.axis_index(a) for a in AXES)
    zh = 2 * zq + zp

    packed = jnp.concatenate(
        [
            obs_feat,
            noisy_sample.astype(bf16),
            timestep.astype(f32).astype(bf16)[:, None],
            jnp.zeros((OWN, 99), bf16),
        ],
        axis=1,
    )

    stay = lax.dynamic_index_in_dim(film_weight, core, 1, keepdims=False)
    go = lax.dynamic_index_in_dim(film_weight, 1 - core, 1, keepdims=False)
    come = cores(go)

    keep, give = split_of(zp.reshape(1).astype(jnp.int32), conv_mid_w)
    w_own = lax.all_gather(keep, ("y", "core"), axis=0, tiled=False)

    chip = jnp.where(
        core == 0, jnp.concatenate([stay, come]), jnp.concatenate([come, stay])
    )
    z_a, z_b, z_c = z_up(chip), z_down(chip), z_two(chip)
    line_a, line_b = jnp.stack([chip, z_a]), jnp.stack([z_b, z_c])
    line_a, packed = tie(line_a, packed)
    down_a, up_a, down_b, up_b = y_up(line_a), y_down(line_a), y_up(line_b), y_down(line_b)
    partner = z_pair(packed)
    partner, give = tie(partner, give)
    w_up, w_down = z_up(give), z_down(give)
    sibling = [cores(line_a), cores(line_b)]
    down_a, *sibling = tie(down_a, *sibling)
    far_a = y_up(down_a)
    up_b, *sibling = tie(up_b, *sibling)
    far_b = y_down(up_b)
    sibling += [cores(piece) for piece in (down_a, down_b, up_a, up_b)]

    both = jnp.where(
        zp == 0, jnp.concatenate([packed, partner]), jnp.concatenate([partner, packed])
    )
    feat, tail = both[:, :1024], both[:, 1024:]
    sinus = sinusoid(tail[:, 28]).astype(bf16)
    step_hidden = mish(jnp.dot(sinus, step_w1, preferred_element_type=f32)).astype(bf16)
    step_feat = jnp.dot(step_hidden, step_w2, preferred_element_type=f32)
    cond = mish(jnp.concatenate([step_feat, feat.astype(f32)], axis=1)).astype(bf16)
    cond_blocks = cond.reshape(PAIR, 16, 80).transpose(1, 0, 2)
    samples = jnp.pad(tail[:, :28], ((0, 0), (14, 14)))
    window = jnp.concatenate([samples[:, 7 * p : 7 * p + 35] for p in range(HORIZON)])
    window = jnp.pad(window, ((0, 0), (0, WIN - 35)))
    coarse = lax.reduce_precision(gain_one, 8, 7)
    small = jnp.concatenate(
        [
            conv_in_w.reshape(TAPS * ACT, WIDE),
            coarse[None].astype(bf16),
            (gain_one - coarse)[None].astype(bf16),
            jnp.zeros((WIN - 37, WIDE), bf16),
        ]
    )

    far_a, far_b, keep, cond_blocks, window, small, *sibling = tie(
        far_a, far_b, keep, cond_blocks, window, small, *sibling
    )
    mine = (line_a, line_b, down_a, down_b, up_a, up_b, far_a, far_b)
    sibling += [cores(far_a), cores(far_b)]
    w_far = z_two(keep)
    dz = (0, -1, 1, 2)
    order = [((zh + dz[r % 4]) % 4) * 4 + (y + dy) % 4 for dy in (0, -1, 1, 2) for r in range(4)]
    order = jnp.stack(order + [core]).astype(jnp.int32)
    side, step = (0, 0, 1, 0, 1, 0, 1, 1), (0, 1, 0, 2, 1, 3, 2, 3)
    slots = [
        (zl if b == 0 else 1 - zl) * 4 + (x + s * (2 * core - 1)) % 4 for b, s in zip(side, step)
    ]
    early = jnp.stack([zh, y, core] + slots[:7]).astype(jnp.int32)
    late = jnp.stack([zh, y, core] + slots[7:]).astype(jnp.int32)
    order, early, late = tie(order, early, late)
    film = film_of(order, cond_blocks, mine, sibling, small)

    a_one, b_own = x_ring(film), zl_swap(film)
    acts = first_of(0, window, film, None)
    w_up, w_down, acts = tie(w_up, w_down, acts)
    w_near = lax.all_gather(jnp.stack([w_up, w_down]), ("y", "core"), axis=0, tiled=False)
    a_one, acts = tie(a_one, acts)
    a_two = x_ring(a_one)
    b_own, acts = tie(b_own, acts)
    b_one = x_ring(b_own)
    acts = first_of(1, window, a_one, acts)
    w_far, acts = tie(w_far, acts)
    far_one = y_ring(w_far)
    acts = first_of(2, window, b_own, acts)
    a_two, acts = tie(a_two, acts)
    a_three = x_ring(a_two)
    b_one, acts = tie(b_one, acts)
    b_two = x_ring(b_one)
    acts = first_of(3, window, a_two, acts)
    far_one, acts = tie(far_one, acts)
    far_two = y_ring(far_one)
    acts = first_of(4, window, b_one, acts)
    b_two, acts = tie(b_two, acts)
    b_three = x_ring(b_two)
    acts = first_of(5, window, a_three, acts)
    far_two, acts = tie(far_two, acts)
    far_three = y_ring(far_two)
    acts = first_of(6, window, b_two, acts)
    far_three, acts = tie(far_three, acts)
    far_mine = jnp.stack([w_far, far_one, far_two, far_three])
    far_theirs = cores(far_mine)

    weights = (w_own, w_near, far_mine, far_theirs)
    conv = mid_of(early, 7, acts, weights)
    conv, stats = end_of(late, window, b_three, conv, weights)
    other = z_pair(stats)

    out_h = lax.dynamic_slice_in_dim(out_w, zp * HALF, HALF, 0).T
    out_h = jnp.stack([jnp.pad(out_h, ((7 * h, 25 - 7 * h), (0, 0))) for h in range(HORIZON)])
    res_h = lax.dynamic_slice_in_dim(residual_w, zp * HALF, HALF, 1)
    res_h = jnp.pad(res_h, ((14, WIN - 21), (0, 0)))
    gain_h = lax.dynamic_slice_in_dim(gain_two, zp * HALF, HALF, 0)[None]
    part = last_of(conv, stats, other, gain_h, window, res_h, out_h)

    got = lax.all_to_all(part, ("zp", "zl", "x"), split_axis=0, concat_axis=0, tiled=True)
    eps = jnp.sum(got.astype(f32), axis=0).T[:, :28]

    root_b, root_a, of_start, of_sample, of_noise = denoise_coefficients(timestep)
    start = jnp.clip((noisy_sample - root_b * eps) / root_a, -1.0, 1.0)
    denoised = of_start * start + of_sample * noisy_sample + of_noise * noise
    return (eps, denoised)


def solution(mesh):
    fine = Mesh(mesh.devices.reshape(SIZES), AXES)
    return jax.shard_map(
        body,
        mesh=fine,
        in_specs=(
            P(DP, None),
            P(DP),
            P(DP, None),
            P(DP, None),
            P(),
            P(),
            P(DP, None, TENSOR),
            P(None, None, TENSOR),
            P(None, TENSOR),
            P(None, DP, TENSOR),
            P(TENSOR, None),
            P(TENSOR),
            P(TENSOR),
        ),
        out_specs=(P(DP, None), P(DP, None)),
        check_vma=False,
    )
```

```python
import math

import jax
import jax.numpy as jnp
import numpy as np
from jax import lax
from jax.experimental import pallas as pl
from jax.experimental.pallas import tpu as pltpu
from jax.sharding import Mesh, PartitionSpec as P

C = 4096
ACT = 7
HORIZON = 4
TAPS = 5
GROUPS = 8
STEP = 256
TRAIN_STEPS = 100
COND = 1280

AXES = ("zq", "zp", "y", "core", "zl", "x")
SIZES = (2, 2, 4, 2, 2, 4)
DP = ("zq", "zp", "y", "core")
TENSOR = ("zl", "x")

OWN = 128
PAIR = 256
ROWS = HORIZON * PAIR
WIDE = 512
HALF = 256
WIN = 64
FILM_ROWS = 2 * PAIR + WIN

f32, bf16 = jnp.float32, jnp.bfloat16


def moves(where):
    pairs = []
    for here in np.ndindex(*SIZES):
        zq, zp, y, core, zl, x = here
        zh, y, core, zl, x = where(2 * zq + zp, y, core, zl, x)
        there = ((zh % 4) // 2, zh % 2, y % 4, core % 2, zl % 2, x % 4)
        pairs.append(
            (int(np.ravel_multi_index(here, SIZES)), int(np.ravel_multi_index(there, SIZES)))
        )
    return pairs


def mover(where):
    pairs = moves(where)
    return lambda array: lax.ppermute(array, AXES, pairs)


z_up = mover(lambda zh, y, core, zl, x: (zh + 1, y, core, zl, x))
z_down = mover(lambda zh, y, core, zl, x: (zh - 1, y, core, zl, x))
z_two = mover(lambda zh, y, core, zl, x: (zh + 2, y, core, zl, x))
z_pair = mover(lambda zh, y, core, zl, x: (zh ^ 1, y, core, zl, x))
y_up = mover(lambda zh, y, core, zl, x: (zh, y + 1, core, zl, x))
y_down = mover(lambda zh, y, core, zl, x: (zh, y - 1, core, zl, x))
cores = mover(lambda zh, y, core, zl, x: (zh, y, 1 - core, zl, x))
zl_swap = mover(lambda zh, y, core, zl, x: (zh, y, core, 1 - zl, x))
y_ring = mover(lambda zh, y, core, zl, x: (zh, y + 1 - 2 * core, core, zl, x))
x_ring = mover(lambda zh, y, core, zl, x: (zh, y, core, zl, x + 1 - 2 * core))


def plan():
    pos = np.arange(TRAIN_STEPS + 1, dtype=np.float64) / TRAIN_STEPS
    curve = np.cos((pos + 0.008) / 1.008 * (math.pi / 2)) ** 2
    betas = np.minimum(1.0 - curve[1:] / curve[:-1], 0.999)
    return jnp.asarray(np.cumprod(1.0 - betas), f32)


def lookup(table, steps):
    onehot = (steps[:, None] == jnp.arange(table.shape[0], dtype=jnp.int32)[None, :]).astype(f32)
    return jnp.sum(onehot * table[None, :], axis=1)


def mish_by_exp(value):
    u = jnp.exp(jnp.minimum(value, 20.0))
    w = u * (u + 2.0)
    return value * (w * pltpu.reciprocal(w + 2.0, approx=True))


def tie(*arrays):
    return lax.optimization_barrier(arrays)


def denoise_coefficients(steps):
    alpha_bar = plan()
    now = lookup(alpha_bar, steps)[:, None]
    before = jnp.where(steps > 0, lookup(alpha_bar, jnp.maximum(steps - 1, 0)), 1.0)[:, None]
    beta_prod = 1.0 - now
    cur_alpha = now / before
    cur_beta = 1.0 - cur_alpha
    return (
        jnp.sqrt(beta_prod),
        jnp.sqrt(now),
        jnp.sqrt(before) * cur_beta / beta_prod,
        jnp.sqrt(cur_alpha) * (1.0 - before) / beta_prod,
        jnp.sqrt((1.0 - before) / beta_prod * cur_beta),
    )


IN_VMEM = pl.BlockSpec(memory_space=pltpu.VMEM)
IN_HBM = pl.BlockSpec(memory_space=pltpu.HBM)
LIMIT = 48
SLOTS = 16


def params(mib, **more):
    return pltpu.CompilerParams(vmem_limit_bytes=mib * 2**20, **more)


def cond_kernel(place_ref, own_ref, partner_ref, w1_ref, w2_ref, cond_ref, window_ref, held_ref):
    lane = lax.broadcasted_iota(jnp.int32, (OWN, 128), 1)
    half_step = STEP // 2
    freqs = jnp.exp(lane.astype(f32) * (-math.log(10000.0) / (half_step - 1)))
    for ref, half in ((own_ref, place_ref[0]), (partner_ref, 1 - place_ref[0])):
        tail = ref[:, 1024:].astype(f32)
        angles = tail[:, 28:29] * freqs
        sinus = jnp.concatenate([jnp.sin(angles), jnp.cos(angles)], axis=1).astype(bf16)
        hidden = mish_by_exp(jnp.dot(sinus, w1_ref[...], preferred_element_type=f32)).astype(bf16)
        feat = jnp.dot(hidden, w2_ref[...], preferred_element_type=f32)
        held_ref[:, :STEP] = mish_by_exp(feat)
        held_ref[:, STEP:] = mish_by_exp(ref[:, :1024].astype(f32))
        rows = pl.ds(pl.multiple_of(half * OWN, OWN), OWN)
        for d in range(16):
            cond_ref[d, rows, :] = held_ref[:, 80 * d : 80 * d + 80].astype(bf16)
        samples = jnp.where(lane < 28, tail, 0.0)
        for p in range(HORIZON):
            seen = pltpu.roll(samples, (14 - 7 * p) % 128, 1)
            seen = jnp.where(lane < 35, seen, 0.0).astype(bf16)
            rows = pl.ds(pl.multiple_of(p * PAIR + half * OWN, OWN), OWN)
            window_ref[rows, :] = seen[:, :WIN]


def cond_of(place, own, partner, w1, w2):
    return pl.pallas_call(
        cond_kernel,
        out_shape=[
            jax.ShapeDtypeStruct((16, PAIR, 80), bf16),
            jax.ShapeDtypeStruct((ROWS, WIN), bf16),
        ],
        in_specs=[pl.BlockSpec(memory_space=pltpu.SMEM)] + [IN_VMEM] * 4,
        out_specs=[IN_VMEM] * 2,
        scratch_shapes=[pltpu.VMEM((OWN, COND), f32)],
        compiler_params=params(16),
        name="cond",
    )(place, own, partner, w1, w2)


def film_kernel(blocks, order_ref, cond_ref, *refs):
    pieces, refs = refs[: len(blocks)], refs[len(blocks) :]
    half = len(blocks) // 2
    more = len(refs) == 3
    for side in range(2):
        total = refs[0][side] if more else jnp.zeros((PAIR, WIDE), f32)
        for at, block in enumerate(blocks):
            total += jnp.dot(
                cond_ref[order_ref[block]],
                pieces[side * half + at // 2][at % 2],
                preferred_element_type=f32,
            )
        if more:
            place = order_ref[16] if side == 0 else 1 - order_ref[16]
            rows = pl.ds(pl.multiple_of(place * PAIR, PAIR), PAIR)
            refs[2][rows, :] = total.astype(bf16)
        else:
            refs[0][side] = total
    if more:
        refs[2][2 * PAIR :, :] = refs[1][...]


def film_of(order, cond_blocks, blocks, mine, sibling, *more):
    out = ((FILM_ROWS, WIDE), bf16) if more else ((2, PAIR, WIDE), f32)
    return pl.pallas_call(
        lambda *refs: film_kernel(blocks, *refs),
        out_shape=jax.ShapeDtypeStruct(*out),
        in_specs=[pl.BlockSpec(memory_space=pltpu.SMEM)]
        + [IN_VMEM] * (1 + len(blocks) + len(more)),
        out_specs=IN_VMEM,
        compiler_params=params(16),
        cost_estimate=pl.CostEstimate(flops=1, bytes_accessed=1, transcendentals=0),
        name="film",
    )(order, cond_blocks, *mine, *sibling, *more)


def split_kernel(place_ref, weight_ref, keep_ref, give_ref):
    for ref, which in ((keep_ref, place_ref[0]), (give_ref, 1 - place_ref[0])):
        at = pl.ds(pl.multiple_of(which * HALF, HALF), HALF)
        for k in range(TAPS):
            ref[:, k * HALF : (k + 1) * HALF] = weight_ref[k, :, at]


def split_of(place, weight):
    return pl.pallas_call(
        split_kernel,
        out_shape=[jax.ShapeDtypeStruct((OWN, TAPS * HALF), bf16)] * 2,
        in_specs=[pl.BlockSpec(memory_space=pltpu.SMEM), IN_VMEM],
        out_specs=[IN_VMEM] * 2,
        compiler_params=params(16),
        name="split",
    )(place, weight)


def first_rows(window_ref, film_ref, hidden_ref, act_ref, after):
    hidden_ref[...] = jnp.dot(
        window_ref[...], film_ref[2 * PAIR :, :], preferred_element_type=f32
    )
    gain = (
        film_ref[2 * PAIR + 35 : 2 * PAIR + 36, :].astype(f32)
        + film_ref[2 * PAIR + 36 : 2 * PAIR + 37, :].astype(f32)
    )

    def lanes(value):
        return sum(value[:, c : c + 128] for c in range(0, WIDE, 128))

    parts = [slice(p * PAIR, (p + 1) * PAIR) for p in range(HORIZON)]
    total = sum(lanes(hidden_ref[a, :]) for a in parts)
    mean = jnp.sum(total, axis=1, keepdims=True) * (1.0 / (HORIZON * WIDE))
    total = sum(lanes((hidden_ref[a, :] - mean) ** 2) for a in parts)
    var = jnp.sum(total, axis=1, keepdims=True) * (1.0 / (HORIZON * WIDE))
    inv = lax.rsqrt(var + 1e-05)
    few = 16
    for r in range(0, PAIR, few):
        at = slice(r, r + few)
        scale = film_ref[at, :].astype(f32)
        shift = film_ref[PAIR + r : PAIR + r + few, :].astype(f32)
        for p in range(HORIZON):
            a = slice(p * PAIR + r, p * PAIR + r + few)
            normed = (hidden_ref[a, :] - mean[at]) * (inv[at] * gain)
            act_ref[p, at, :] = (scale * mish_by_exp(normed) + shift).astype(bf16)
        after(r + few)


def first_kernel(slot, window_ref, film_ref, *rest):
    out_ref, hidden_ref, act_ref, sem = rest[-4:]
    out_ref, some = out_ref.at[slot], 64

    def after(rows):
        if rows % some == 0:
            done = slice(rows - some, rows)
            pltpu.make_async_copy(act_ref.at[:, done], out_ref.at[:, done], sem).start()

    first_rows(window_ref, film_ref, hidden_ref, act_ref, after)
    pltpu.make_async_copy(act_ref, out_ref, sem).wait()


def first_of(slot, window, film, before):
    more = [] if before is None else [before]
    return pl.pallas_call(
        lambda *refs: first_kernel(slot, *refs),
        out_shape=jax.ShapeDtypeStruct((SLOTS, HORIZON, PAIR, WIDE), bf16),
        in_specs=[IN_VMEM, IN_VMEM] + [IN_HBM] * len(more),
        out_specs=IN_HBM,
        scratch_shapes=[
            pltpu.VMEM((ROWS, WIDE), f32),
            pltpu.VMEM((HORIZON, PAIR, WIDE), bf16),
            pltpu.SemaphoreType.DMA,
        ],
        input_output_aliases={2: 0} if more else {},
        compiler_params=params(LIMIT),
        cost_estimate=pl.CostEstimate(flops=1, bytes_accessed=1, transcendentals=0),
        name="first",
    )(window, film, *more)


def fetch_weights(place_ref, block, refs, into, sem):
    own_ref, near_ref, mine_refs, theirs_refs = refs[0], refs[1], refs[2:6], refs[6:10]
    zh, y, core = place_ref[0], place_ref[1], place_ref[2]
    q, apart = block % 2, (block // 2 + 4 - zh) % 4

    @pl.when(apart == 0)
    def _():
        pltpu.make_async_copy(own_ref.at[pl.ds(4 * q, 4)], into, sem).start()

    for way, side in ((3, 0), (1, 1)):

        @pl.when(apart == way)
        def _():
            pltpu.make_async_copy(near_ref.at[pl.ds(4 * q, 4), side], into, sem).start()

    for odd in range(2):
        for far_refs, its in ((mine_refs, core), (theirs_refs, 1 - core)):
            steps = ((1 - 2 * its) * (y - 2 * q - odd) + 8) % 4
            for j in range(4):

                @pl.when(jnp.logical_and(apart == 2, steps == j))
                def _():
                    pltpu.make_async_copy(far_refs[j], into.at[2 * odd + its], sem).start()


def add_block(act, weight, before_ref, out_ref):
    for h in range(HORIZON):
        at = slice(h * PAIR, (h + 1) * PAIR)
        total = None if before_ref is None else before_ref[at, :]
        for p in range(HORIZON):
            k = p - h + 2
            if 0 <= k < TAPS:
                term = jnp.dot(
                    act[p],
                    weight[:, :, k * HALF : (k + 1) * HALF].reshape(WIDE, HALF),
                    preferred_element_type=f32,
                )
                total = term if total is None else total + term
        out_ref[at, :] = total


def mid_kernel(count, place_ref, acts_ref, *refs):
    out_ref, held, act_held, sems = refs[-4:]
    weights = refs[:10]

    def fetch(step):
        at = step % 3
        pltpu.make_async_copy(acts_ref.at[step], act_held.at[at], sems.at[1, at]).start()
        fetch_weights(place_ref, place_ref[3 + step], weights, held.at[at], sems.at[0, at])

    for step in range(2):
        fetch(step)
    for step in range(count):
        if step + 2 < count:
            fetch(step + 2)
        at = step % 3
        pltpu.make_async_copy(weights[0].at[pl.ds(0, 4)], held.at[at], sems.at[0, at]).wait()
        pltpu.make_async_copy(acts_ref.at[step], act_held.at[at], sems.at[1, at]).wait()
        add_block(act_held.at[at], held.at[at], out_ref if step else None, out_ref)


def mid_of(place, count, acts, weights):
    return pl.pallas_call(
        lambda *refs: mid_kernel(count, *refs),
        out_shape=jax.ShapeDtypeStruct((ROWS, HALF), f32),
        in_specs=[pl.BlockSpec(memory_space=pltpu.SMEM)] + [IN_HBM] * 11,
        out_specs=IN_VMEM,
        scratch_shapes=[
            pltpu.VMEM((3, 4, OWN, TAPS * HALF), bf16),
            pltpu.VMEM((3, HORIZON, PAIR, WIDE), bf16),
            pltpu.SemaphoreType.DMA((2, 3)),
        ],
        compiler_params=params(LIMIT),
        cost_estimate=pl.CostEstimate(flops=1, bytes_accessed=1, transcendentals=0),
        name="mid",
    )(place, acts, *weights)


def end_kernel(place_ref, window_ref, film_ref, before_ref, *refs):
    out_ref, stats_ref, hidden_ref, act_ref, held, sem = refs[-6:]
    weights = refs[:10]
    fetch_weights(place_ref, place_ref[3], weights, held, sem)
    first_rows(window_ref, film_ref, hidden_ref, act_ref, lambda rows: None)
    pltpu.make_async_copy(weights[0].at[pl.ds(0, 4)], held, sem).wait()
    add_block(act_ref, held, before_ref, out_ref)
    parts = [out_ref[h * PAIR : (h + 1) * PAIR, :] for h in range(HORIZON)]
    mean = jnp.sum(sum(parts), axis=1, keepdims=True) * (1.0 / (HORIZON * HALF))
    spread = jnp.sum(sum((o - mean) ** 2 for o in parts), axis=1, keepdims=True)
    lane = lax.broadcasted_iota(jnp.int32, (PAIR, 128), 1)
    both = jnp.where(lane == 0, mean, jnp.where(lane == 1, spread, 0.0))
    stats_ref[...] = both.T[:8, :]


def end_of(place, window, film, before, weights):
    return pl.pallas_call(
        end_kernel,
        out_shape=[
            jax.ShapeDtypeStruct((ROWS, HALF), f32),
            jax.ShapeDtypeStruct((8, PAIR), f32),
        ],
        in_specs=[pl.BlockSpec(memory_space=pltpu.SMEM)] + [IN_VMEM] * 3 + [IN_HBM] * 10,
        out_specs=[IN_VMEM] * 2,
        scratch_shapes=[
            pltpu.VMEM((ROWS, WIDE), f32),
            pltpu.VMEM((HORIZON, PAIR, WIDE), bf16),
            pltpu.VMEM((4, OWN, TAPS * HALF), bf16),
            pltpu.SemaphoreType.DMA,
        ],
        compiler_params=params(LIMIT),
        cost_estimate=pl.CostEstimate(flops=1, bytes_accessed=1, transcendentals=0),
        name="end",
    )(place, window, film, before, *weights)


def last_kernel(conv_ref, own_ref, other_ref, gain_ref, window_ref, res_ref, out_w_ref, eps_ref):
    rows = jnp.concatenate([own_ref[...], other_ref[...], jnp.zeros((112, PAIR), f32)], axis=0).T
    mean_a, spread_a = rows[:, 0:1], rows[:, 1:2]
    mean_b, spread_b = rows[:, 8:9], rows[:, 9:10]
    each = HORIZON * HALF
    mean = 0.5 * (mean_a + mean_b)
    var = (spread_a + spread_b + (mean_a - mean_b) ** 2 * (0.5 * each)) * (0.5 / each)
    inv = lax.rsqrt(var + 1e-05)
    total = jnp.zeros((32, PAIR), f32)
    for h in range(HORIZON):
        at = slice(h * PAIR, (h + 1) * PAIR)
        normed = (conv_ref[at, :] - mean) * inv * gain_ref[...]
        skip = jnp.dot(window_ref[at, :], res_ref[...], preferred_element_type=f32)
        act = (mish_by_exp(normed) + skip).astype(bf16)
        total += lax.dot_general(
            out_w_ref[h], act, (((1,), (1,)), ((), ())), preferred_element_type=f32
        )
    for b in range(2):
        part = total[:, b * OWN : (b + 1) * OWN].astype(bf16)
        for copy in range(8):
            eps_ref[8 * b + copy] = part


def last_of(conv, own, other, gain, window, res, out_w):
    return pl.pallas_call(
        last_kernel,
        out_shape=jax.ShapeDtypeStruct((16, 32, OWN), bf16),
        in_specs=[pl.BlockSpec(memory_space=pltpu.VMEM)] * 7,
        out_specs=pl.BlockSpec(memory_space=pltpu.VMEM),
        compiler_params=params(24),
        cost_estimate=pl.CostEstimate(
            flops=2 * ROWS * HALF * 80, bytes_accessed=2 * 2**20, transcendentals=ROWS * HALF
        ),
        name="last",
    )(conv, own, other, gain, window, res, out_w)


def body(
    noisy_sample,
    timestep,
    noise,
    obs_feat,
    step_w1,
    step_w2,
    film_weight,
    conv_in_w,
    residual_w,
    conv_mid_w,
    out_w,
    gain_one,
    gain_two,
):
    zq, zp, y, core, zl, x = (lax.axis_index(a) for a in AXES)
    zh = 2 * zq + zp

    packed = jnp.concatenate(
        [
            obs_feat,
            noisy_sample.astype(bf16),
            timestep.astype(f32).astype(bf16)[:, None],
            jnp.zeros((OWN, 99), bf16),
        ],
        axis=1,
    )

    stay = lax.dynamic_index_in_dim(film_weight, core, 1, keepdims=False)
    go = lax.dynamic_index_in_dim(film_weight, 1 - core, 1, keepdims=False)
    come = cores(go)

    pair_place = zp.reshape(1).astype(jnp.int32)
    keep, give = split_of(pair_place, conv_mid_w)
    w_own = lax.all_gather(keep, ("y", "core"), axis=0, tiled=False)
    w_up, w_down = z_up(give), z_down(give)

    chip = jnp.where(
        core == 0, jnp.concatenate([stay, come]), jnp.concatenate([come, stay])
    )
    z_a, z_b, z_c = z_up(chip), z_down(chip), z_two(chip)
    line_a, line_b = jnp.stack([chip, z_a]), jnp.stack([z_b, z_c])
    line_a, line_b, packed, w_up, w_down = tie(line_a, line_b, packed, w_up, w_down)
    down_a, up_a, down_b, up_b = y_up(line_a), y_down(line_a), y_up(line_b), y_down(line_b)
    partner = z_pair(packed)
    sibling = [cores(line_a), cores(line_b)]
    down_a, *sibling = tie(down_a, *sibling)
    far_a = y_up(down_a)
    up_b, *sibling = tie(up_b, *sibling)
    far_b = y_down(up_b)
    sibling += [cores(piece) for piece in (down_a, down_b, up_a, up_b)]
    partner, keep = tie(partner, keep)
    w_far = z_two(keep)
    w_near = lax.all_gather(jnp.stack([w_up, w_down]), ("y", "core"), axis=0, tiled=False)

    cond_blocks, window = cond_of(pair_place, packed, partner, step_w1, step_w2)
    coarse = lax.reduce_precision(gain_one, 8, 7)
    small = jnp.concatenate(
        [
            conv_in_w.reshape(TAPS * ACT, WIDE),
            coarse[None].astype(bf16),
            (gain_one - coarse)[None].astype(bf16),
            jnp.zeros((WIN - 37, WIDE), bf16),
        ]
    )

    dz = (0, -1, 1, 2)
    order = [((zh + dz[r % 4]) % 4) * 4 + (y + dy) % 4 for dy in (0, -1, 1, 2) for r in range(4)]
    order = jnp.stack(order + [core]).astype(jnp.int32)
    side, step = (0, 0, 1, 0, 1, 0, 1, 1), (0, 1, 0, 2, 1, 3, 2, 3)
    slots = [
        (zl if b == 0 else 1 - zl) * 4 + (x + s * (2 * core - 1)) % 4 for b, s in zip(side, step)
    ]
    early = jnp.stack([zh, y, core] + slots[:7]).astype(jnp.int32)
    late = jnp.stack([zh, y, core] + slots[7:]).astype(jnp.int32)
    order, early, late = tie(order, early, late)
    near_pieces = (line_a, line_b, down_a, down_b, up_a, up_b)
    part = film_of(order, cond_blocks, range(12), near_pieces, sibling)
    far_a, far_b, part, small, window = tie(far_a, far_b, part, small, window)
    far_sibling = (cores(far_a), cores(far_b))
    film = film_of(order, cond_blocks, range(12, 16), (far_a, far_b), far_sibling, part, small)

    a_one, b_own = x_ring(film), zl_swap(film)
    acts = first_of(0, window, film, None)
    w_far, acts = tie(w_far, acts)
    far_one, other_far = y_ring(w_far), cores(w_far)
    a_one, acts = tie(a_one, acts)
    a_two = x_ring(a_one)
    acts = first_of(1, window, a_one, acts)
    b_own, acts = tie(b_own, acts)
    b_one = x_ring(b_own)
    acts = first_of(2, window, b_own, acts)
    a_two, acts = tie(a_two, acts)
    a_three = x_ring(a_two)
    acts = first_of(3, window, a_two, acts)
    b_one, acts = tie(b_one, acts)
    b_two = x_ring(b_one)
    far_one, acts = tie(far_one, acts)
    far_two, other_one = y_ring(far_one), cores(far_one)
    acts = first_of(4, window, b_one, acts)
    acts = first_of(5, window, a_three, acts)
    b_two, acts = tie(b_two, acts)
    b_three = x_ring(b_two)
    far_two, acts = tie(far_two, acts)
    far_three, other_two = y_ring(far_two), cores(far_two)
    acts = first_of(6, window, b_two, acts)
    other_three = cores(far_three)

    weights = (w_own, w_near, w_far, far_one, far_two, far_three)
    weights += (other_far, other_one, other_two, other_three)
    conv = mid_of(early, 7, acts, weights)
    conv, stats = end_of(late, window, b_three, conv, weights)
    other = z_pair(stats)

    out_h = lax.dynamic_slice_in_dim(out_w, zp * HALF, HALF, 0).T
    out_h = jnp.stack([jnp.pad(out_h, ((7 * h, 25 - 7 * h), (0, 0))) for h in range(HORIZON)])
    res_h = lax.dynamic_slice_in_dim(residual_w, zp * HALF, HALF, 1)
    res_h = jnp.pad(res_h, ((14, WIN - 21), (0, 0)))
    gain_h = lax.dynamic_slice_in_dim(gain_two, zp * HALF, HALF, 0)[None]
    part = last_of(conv, stats, other, gain_h, window, res_h, out_h)

    got = lax.all_to_all(part, ("zp", "zl", "x"), split_axis=0, concat_axis=0, tiled=True)
    eps = jnp.sum(got.astype(f32), axis=0).T[:, :28]

    root_b, root_a, of_start, of_sample, of_noise = denoise_coefficients(timestep)
    start = jnp.clip((noisy_sample - root_b * eps) / root_a, -1.0, 1.0)
    denoised = of_start * start + of_sample * noisy_sample + of_noise * noise
    return (eps, denoised)


def solution(mesh):
    fine = Mesh(mesh.devices.reshape(SIZES), AXES)
    return jax.shard_map(
        body,
        mesh=fine,
        in_specs=(
            P(DP, None),
            P(DP),
            P(DP, None),
            P(DP, None),
            P(),
            P(),
            P(DP, None, TENSOR),
            P(None, None, TENSOR),
            P(None, TENSOR),
            P(None, DP, TENSOR),
            P(TENSOR, None),
            P(TENSOR),
            P(TENSOR),
        ),
        out_specs=(P(DP, None), P(DP, None)),
        check_vma=False,
    )
```

```python
import math

import jax
import jax.numpy as jnp
import numpy as np
from jax import lax
from jax.experimental import pallas as pl
from jax.experimental.pallas import tpu as pltpu
from jax.sharding import Mesh, PartitionSpec as P

C = 4096
ACT = 7
HORIZON = 4
TAPS = 5
GROUPS = 8
STEP = 256
TRAIN_STEPS = 100
COND = 1280

AXES = ("zq", "zp", "y", "core", "zl", "x")
SIZES = (2, 2, 4, 2, 2, 4)
DP = ("zq", "zp", "y", "core")
TENSOR = ("zl", "x")

OWN = 128
PAIR = 256
ROWS = HORIZON * PAIR
WIDE = 512
HALF = 256
WIN = 64
FILM_ROWS = 2 * PAIR + WIN

f32, bf16 = jnp.float32, jnp.bfloat16


def moves(where):
    pairs = []
    for here in np.ndindex(*SIZES):
        zq, zp, y, core, zl, x = here
        zh, y, core, zl, x = where(2 * zq + zp, y, core, zl, x)
        there = ((zh % 4) // 2, zh % 2, y % 4, core % 2, zl % 2, x % 4)
        pairs.append(
            (int(np.ravel_multi_index(here, SIZES)), int(np.ravel_multi_index(there, SIZES)))
        )
    return pairs


def mover(where):
    pairs = moves(where)
    return lambda array: lax.ppermute(array, AXES, pairs)


z_up = mover(lambda zh, y, core, zl, x: (zh + 1, y, core, zl, x))
z_down = mover(lambda zh, y, core, zl, x: (zh - 1, y, core, zl, x))
z_two = mover(lambda zh, y, core, zl, x: (zh + 2, y, core, zl, x))
z_pair = mover(lambda zh, y, core, zl, x: (zh ^ 1, y, core, zl, x))
y_up = mover(lambda zh, y, core, zl, x: (zh, y + 1, core, zl, x))
y_down = mover(lambda zh, y, core, zl, x: (zh, y - 1, core, zl, x))
cores = mover(lambda zh, y, core, zl, x: (zh, y, 1 - core, zl, x))
zl_swap = mover(lambda zh, y, core, zl, x: (zh, y, core, 1 - zl, x))
y_ring = mover(lambda zh, y, core, zl, x: (zh, y + 1 - 2 * core, core, zl, x))
x_ring = mover(lambda zh, y, core, zl, x: (zh, y, core, zl, x + 1 - 2 * core))


def plan():
    pos = np.arange(TRAIN_STEPS + 1, dtype=np.float64) / TRAIN_STEPS
    curve = np.cos((pos + 0.008) / 1.008 * (math.pi / 2)) ** 2
    betas = np.minimum(1.0 - curve[1:] / curve[:-1], 0.999)
    return jnp.asarray(np.cumprod(1.0 - betas), f32)


def lookup(table, steps):
    onehot = (steps[:, None] == jnp.arange(table.shape[0], dtype=jnp.int32)[None, :]).astype(f32)
    return jnp.sum(onehot * table[None, :], axis=1)


def mish_by_exp(value):
    u = jnp.exp(jnp.minimum(value, 20.0))
    w = u * (u + 2.0)
    return value * (w * pltpu.reciprocal(w + 2.0, approx=True))


def tie(*arrays):
    return lax.optimization_barrier(arrays)


def denoise_coefficients(steps):
    alpha_bar = plan()
    now = lookup(alpha_bar, steps)[:, None]
    before = jnp.where(steps > 0, lookup(alpha_bar, jnp.maximum(steps - 1, 0)), 1.0)[:, None]
    beta_prod = 1.0 - now
    cur_alpha = now / before
    cur_beta = 1.0 - cur_alpha
    return (
        jnp.sqrt(beta_prod),
        jnp.sqrt(now),
        jnp.sqrt(before) * cur_beta / beta_prod,
        jnp.sqrt(cur_alpha) * (1.0 - before) / beta_prod,
        jnp.sqrt((1.0 - before) / beta_prod * cur_beta),
    )


IN_VMEM = pl.BlockSpec(memory_space=pltpu.VMEM)
IN_HBM = pl.BlockSpec(memory_space=pltpu.HBM)
LIMIT = 48
SLOTS = 16


def params(mib, **more):
    return pltpu.CompilerParams(vmem_limit_bytes=mib * 2**20, **more)


def cond_kernel(place_ref, own_ref, partner_ref, w1_ref, w2_ref, cond_ref, window_ref, held_ref):
    lane = lax.broadcasted_iota(jnp.int32, (OWN, 128), 1)
    half_step = STEP // 2
    freqs = jnp.exp(lane.astype(f32) * (-math.log(10000.0) / (half_step - 1)))
    for ref, half in ((own_ref, place_ref[0]), (partner_ref, 1 - place_ref[0])):
        tail = ref[:, 1024:].astype(f32)
        angles = tail[:, 28:29] * freqs
        sinus = jnp.concatenate([jnp.sin(angles), jnp.cos(angles)], axis=1).astype(bf16)
        hidden = mish_by_exp(jnp.dot(sinus, w1_ref[...], preferred_element_type=f32)).astype(bf16)
        feat = jnp.dot(hidden, w2_ref[...], preferred_element_type=f32)
        held_ref[:, :STEP] = mish_by_exp(feat)
        held_ref[:, STEP:] = mish_by_exp(ref[:, :1024].astype(f32))
        rows = pl.ds(pl.multiple_of(half * OWN, OWN), OWN)
        for d in range(16):
            cond_ref[d, rows, :] = held_ref[:, 80 * d : 80 * d + 80].astype(bf16)
        samples = jnp.where(lane < 28, tail, 0.0)
        for p in range(HORIZON):
            seen = pltpu.roll(samples, (14 - 7 * p) % 128, 1)
            seen = jnp.where(lane < 35, seen, 0.0).astype(bf16)
            rows = pl.ds(pl.multiple_of(p * PAIR + half * OWN, OWN), OWN)
            window_ref[rows, :] = seen[:, :WIN]


def cond_of(place, own, partner, w1, w2):
    return pl.pallas_call(
        cond_kernel,
        out_shape=[
            jax.ShapeDtypeStruct((16, PAIR, 80), bf16),
            jax.ShapeDtypeStruct((ROWS, WIN), bf16),
        ],
        in_specs=[pl.BlockSpec(memory_space=pltpu.SMEM)] + [IN_VMEM] * 4,
        out_specs=[IN_VMEM] * 2,
        scratch_shapes=[pltpu.VMEM((OWN, COND), f32)],
        compiler_params=params(16),
        name="cond",
    )(place, own, partner, w1, w2)


def film_kernel(blocks, order_ref, cond_ref, *refs):
    pieces, refs = refs[: len(blocks)], refs[len(blocks) :]
    half = len(blocks) // 2
    more = len(refs) == 3
    for side in range(2):
        total = refs[0][side] if more else jnp.zeros((PAIR, WIDE), f32)
        for at, block in enumerate(blocks):
            total += jnp.dot(
                cond_ref[order_ref[block]],
                pieces[side * half + at // 2][at % 2],
                preferred_element_type=f32,
            )
        if more:
            place = order_ref[16] if side == 0 else 1 - order_ref[16]
            rows = pl.ds(pl.multiple_of(place * PAIR, PAIR), PAIR)
            refs[2][rows, :] = total.astype(bf16)
        else:
            refs[0][side] = total
    if more:
        refs[2][2 * PAIR :, :] = refs[1][...]


def film_of(order, cond_blocks, blocks, mine, sibling, *more):
    out = ((FILM_ROWS, WIDE), bf16) if more else ((2, PAIR, WIDE), f32)
    return pl.pallas_call(
        lambda *refs: film_kernel(blocks, *refs),
        out_shape=jax.ShapeDtypeStruct(*out),
        in_specs=[pl.BlockSpec(memory_space=pltpu.SMEM)]
        + [IN_VMEM] * (1 + len(blocks) + len(more)),
        out_specs=IN_VMEM,
        compiler_params=params(16),
        cost_estimate=pl.CostEstimate(flops=1, bytes_accessed=1, transcendentals=0),
        name="film",
    )(order, cond_blocks, *mine, *sibling, *more)


def split_kernel(place_ref, weight_ref, keep_ref, give_ref):
    for ref, which in ((keep_ref, place_ref[0]), (give_ref, 1 - place_ref[0])):
        at = pl.ds(pl.multiple_of(which * HALF, HALF), HALF)
        for k in range(TAPS):
            ref[:, k * HALF : (k + 1) * HALF] = weight_ref[k, :, at]


def split_of(place, weight):
    return pl.pallas_call(
        split_kernel,
        out_shape=[jax.ShapeDtypeStruct((OWN, TAPS * HALF), bf16)] * 2,
        in_specs=[pl.BlockSpec(memory_space=pltpu.SMEM), IN_VMEM],
        out_specs=[IN_VMEM] * 2,
        compiler_params=params(16),
        name="split",
    )(place, weight)


def first_rows(window_ref, film_ref, hidden_ref, act_ref, after):
    hidden_ref[...] = jnp.dot(
        window_ref[...], film_ref[2 * PAIR :, :], preferred_element_type=f32
    )
    gain = (
        film_ref[2 * PAIR + 35 : 2 * PAIR + 36, :].astype(f32)
        + film_ref[2 * PAIR + 36 : 2 * PAIR + 37, :].astype(f32)
    )

    def lanes(value):
        return sum(value[:, c : c + 128] for c in range(0, WIDE, 128))

    parts = [slice(p * PAIR, (p + 1) * PAIR) for p in range(HORIZON)]
    total = sum(lanes(hidden_ref[a, :]) for a in parts)
    mean = jnp.sum(total, axis=1, keepdims=True) * (1.0 / (HORIZON * WIDE))
    total = sum(lanes((hidden_ref[a, :] - mean) ** 2) for a in parts)
    var = jnp.sum(total, axis=1, keepdims=True) * (1.0 / (HORIZON * WIDE))
    inv = lax.rsqrt(var + 1e-05)
    few = 16
    for r in range(0, PAIR, few):
        at = slice(r, r + few)
        scale = film_ref[at, :].astype(f32)
        shift = film_ref[PAIR + r : PAIR + r + few, :].astype(f32)
        for p in range(HORIZON):
            a = slice(p * PAIR + r, p * PAIR + r + few)
            normed = (hidden_ref[a, :] - mean[at]) * (inv[at] * gain)
            act_ref[p, at, :] = (scale * mish_by_exp(normed) + shift).astype(bf16)
        after(r + few)


def first_kernel(slot, window_ref, film_ref, *rest):
    out_ref, hidden_ref, act_ref, sem = rest[-4:]
    out_ref, some = out_ref.at[slot], 64

    def after(rows):
        if rows % some == 0:
            done = slice(rows - some, rows)
            pltpu.make_async_copy(act_ref.at[:, done], out_ref.at[:, done], sem).start()

    first_rows(window_ref, film_ref, hidden_ref, act_ref, after)
    pltpu.make_async_copy(act_ref, out_ref, sem).wait()


def first_of(slot, window, film, before):
    more = [] if before is None else [before]
    return pl.pallas_call(
        lambda *refs: first_kernel(slot, *refs),
        out_shape=jax.ShapeDtypeStruct((SLOTS, HORIZON, PAIR, WIDE), bf16),
        in_specs=[IN_VMEM, IN_VMEM] + [IN_HBM] * len(more),
        out_specs=IN_HBM,
        scratch_shapes=[
            pltpu.VMEM((ROWS, WIDE), f32),
            pltpu.VMEM((HORIZON, PAIR, WIDE), bf16),
            pltpu.SemaphoreType.DMA,
        ],
        input_output_aliases={2: 0} if more else {},
        compiler_params=params(LIMIT),
        cost_estimate=pl.CostEstimate(flops=1, bytes_accessed=1, transcendentals=0),
        name="first",
    )(window, film, *more)


def fetch_weights(place_ref, block, refs, into, sem):
    own_ref, near_ref, mine_refs, theirs_refs = refs[0], refs[1], refs[2:6], refs[6:10]
    zh, y, core = place_ref[0], place_ref[1], place_ref[2]
    q, apart = block % 2, (block // 2 + 4 - zh) % 4

    @pl.when(apart == 0)
    def _():
        pltpu.make_async_copy(own_ref.at[pl.ds(4 * q, 4)], into, sem).start()

    for way, side in ((3, 0), (1, 1)):

        @pl.when(apart == way)
        def _():
            pltpu.make_async_copy(near_ref.at[pl.ds(4 * q, 4), side], into, sem).start()

    for odd in range(2):
        for far_refs, its in ((mine_refs, core), (theirs_refs, 1 - core)):
            steps = ((1 - 2 * its) * (y - 2 * q - odd) + 8) % 4
            for j in range(4):

                @pl.when(jnp.logical_and(apart == 2, steps == j))
                def _():
                    pltpu.make_async_copy(far_refs[j], into.at[2 * odd + its], sem).start()


def add_block(act, weight, before_ref, out_ref):
    for h in range(HORIZON):
        at = slice(h * PAIR, (h + 1) * PAIR)
        total = None if before_ref is None else before_ref[at, :]
        for p in range(HORIZON):
            k = p - h + 2
            if 0 <= k < TAPS:
                term = jnp.dot(
                    act[p],
                    weight[:, :, k * HALF : (k + 1) * HALF].reshape(WIDE, HALF),
                    preferred_element_type=f32,
                )
                total = term if total is None else total + term
        out_ref[at, :] = total


def mid_kernel(count, place_ref, acts_ref, *refs):
    out_ref, held, act_held, sems = refs[-4:]
    weights = refs[:10]

    def fetch(step):
        at = step % 3
        pltpu.make_async_copy(acts_ref.at[step], act_held.at[at], sems.at[1, at]).start()
        fetch_weights(place_ref, place_ref[3 + step], weights, held.at[at], sems.at[0, at])

    for step in range(2):
        fetch(step)
    for step in range(count):
        if step + 2 < count:
            fetch(step + 2)
        at = step % 3
        pltpu.make_async_copy(weights[0].at[pl.ds(0, 4)], held.at[at], sems.at[0, at]).wait()
        pltpu.make_async_copy(acts_ref.at[step], act_held.at[at], sems.at[1, at]).wait()
        add_block(act_held.at[at], held.at[at], out_ref if step else None, out_ref)


def mid_of(place, count, acts, weights):
    return pl.pallas_call(
        lambda *refs: mid_kernel(count, *refs),
        out_shape=jax.ShapeDtypeStruct((ROWS, HALF), f32),
        in_specs=[pl.BlockSpec(memory_space=pltpu.SMEM)] + [IN_HBM] * 11,
        out_specs=IN_VMEM,
        scratch_shapes=[
            pltpu.VMEM((3, 4, OWN, TAPS * HALF), bf16),
            pltpu.VMEM((3, HORIZON, PAIR, WIDE), bf16),
            pltpu.SemaphoreType.DMA((2, 3)),
        ],
        compiler_params=params(LIMIT),
        cost_estimate=pl.CostEstimate(flops=1, bytes_accessed=1, transcendentals=0),
        name="mid",
    )(place, acts, *weights)


def end_kernel(place_ref, window_ref, film_ref, before_ref, *refs):
    out_ref, stats_ref, hidden_ref, act_ref, held, sem = refs[-6:]
    weights = refs[:10]
    fetch_weights(place_ref, place_ref[3], weights, held, sem)
    first_rows(window_ref, film_ref, hidden_ref, act_ref, lambda rows: None)
    pltpu.make_async_copy(weights[0].at[pl.ds(0, 4)], held, sem).wait()
    add_block(act_ref, held, before_ref, out_ref)
    parts = [out_ref[h * PAIR : (h + 1) * PAIR, :] for h in range(HORIZON)]
    mean = jnp.sum(sum(parts), axis=1, keepdims=True) * (1.0 / (HORIZON * HALF))
    spread = jnp.sum(sum((o - mean) ** 2 for o in parts), axis=1, keepdims=True)
    lane = lax.broadcasted_iota(jnp.int32, (PAIR, 128), 1)
    both = jnp.where(lane == 0, mean, jnp.where(lane == 1, spread, 0.0))
    stats_ref[...] = both.T[:8, :]


def end_of(place, window, film, before, weights):
    return pl.pallas_call(
        end_kernel,
        out_shape=[
            jax.ShapeDtypeStruct((ROWS, HALF), f32),
            jax.ShapeDtypeStruct((8, PAIR), f32),
        ],
        in_specs=[pl.BlockSpec(memory_space=pltpu.SMEM)] + [IN_VMEM] * 3 + [IN_HBM] * 10,
        out_specs=[IN_VMEM] * 2,
        scratch_shapes=[
            pltpu.VMEM((ROWS, WIDE), f32),
            pltpu.VMEM((HORIZON, PAIR, WIDE), bf16),
            pltpu.VMEM((4, OWN, TAPS * HALF), bf16),
            pltpu.SemaphoreType.DMA,
        ],
        compiler_params=params(LIMIT),
        cost_estimate=pl.CostEstimate(flops=1, bytes_accessed=1, transcendentals=0),
        name="end",
    )(place, window, film, before, *weights)


def last_kernel(conv_ref, own_ref, other_ref, gain_ref, window_ref, res_ref, out_w_ref, eps_ref):
    rows = jnp.concatenate([own_ref[...], other_ref[...], jnp.zeros((112, PAIR), f32)], axis=0).T
    mean_a, spread_a = rows[:, 0:1], rows[:, 1:2]
    mean_b, spread_b = rows[:, 8:9], rows[:, 9:10]
    each = HORIZON * HALF
    mean = 0.5 * (mean_a + mean_b)
    var = (spread_a + spread_b + (mean_a - mean_b) ** 2 * (0.5 * each)) * (0.5 / each)
    inv = lax.rsqrt(var + 1e-05)
    total = jnp.zeros((32, PAIR), f32)
    for h in range(HORIZON):
        at = slice(h * PAIR, (h + 1) * PAIR)
        normed = (conv_ref[at, :] - mean) * inv * gain_ref[...]
        skip = jnp.dot(window_ref[at, :], res_ref[...], preferred_element_type=f32)
        act = (mish_by_exp(normed) + skip).astype(bf16)
        total += lax.dot_general(
            out_w_ref[h], act, (((1,), (1,)), ((), ())), preferred_element_type=f32
        )
    for b in range(2):
        part = total[:, b * OWN : (b + 1) * OWN].astype(bf16)
        for copy in range(8):
            eps_ref[8 * b + copy] = part


def last_of(conv, own, other, gain, window, res, out_w):
    return pl.pallas_call(
        last_kernel,
        out_shape=jax.ShapeDtypeStruct((16, 32, OWN), bf16),
        in_specs=[pl.BlockSpec(memory_space=pltpu.VMEM)] * 7,
        out_specs=pl.BlockSpec(memory_space=pltpu.VMEM),
        compiler_params=params(24),
        cost_estimate=pl.CostEstimate(
            flops=2 * ROWS * HALF * 80, bytes_accessed=2 * 2**20, transcendentals=ROWS * HALF
        ),
        name="last",
    )(conv, own, other, gain, window, res, out_w)


def body(
    noisy_sample,
    timestep,
    noise,
    obs_feat,
    step_w1,
    step_w2,
    film_weight,
    conv_in_w,
    residual_w,
    conv_mid_w,
    out_w,
    gain_one,
    gain_two,
):
    zq, zp, y, core, zl, x = (lax.axis_index(a) for a in AXES)
    zh = 2 * zq + zp

    packed = jnp.concatenate(
        [
            obs_feat,
            noisy_sample.astype(bf16),
            timestep.astype(f32).astype(bf16)[:, None],
            jnp.zeros((OWN, 99), bf16),
        ],
        axis=1,
    )

    stay = lax.dynamic_index_in_dim(film_weight, core, 1, keepdims=False)
    go = lax.dynamic_index_in_dim(film_weight, 1 - core, 1, keepdims=False)
    come = cores(go)

    pair_place = zp.reshape(1).astype(jnp.int32)
    keep, give = split_of(pair_place, conv_mid_w)
    w_own = lax.all_gather(keep, ("y", "core"), axis=0, tiled=False)
    w_up, w_down = z_up(give), z_down(give)

    chip = jnp.where(
        core == 0, jnp.concatenate([stay, come]), jnp.concatenate([come, stay])
    )
    z_a, z_b, z_c = z_up(chip), z_down(chip), z_two(chip)
    line_a, line_b = jnp.stack([chip, z_a]), jnp.stack([z_b, z_c])
    line_a, line_b, packed, w_up, w_down = tie(line_a, line_b, packed, w_up, w_down)
    down_a, up_a, down_b, up_b = y_up(line_a), y_down(line_a), y_up(line_b), y_down(line_b)
    partner = z_pair(packed)
    sibling = [cores(line_a), cores(line_b)]
    down_a, *sibling = tie(down_a, *sibling)
    far_a = y_up(down_a)
    up_b, *sibling = tie(up_b, *sibling)
    far_b = y_down(up_b)
    sibling += [cores(piece) for piece in (down_a, down_b, up_a, up_b)]
    partner, keep = tie(partner, keep)
    w_far = z_two(keep)
    w_near = lax.all_gather(jnp.stack([w_up, w_down]), ("y", "core"), axis=0, tiled=False)

    cond_blocks, window = cond_of(pair_place, packed, partner, step_w1, step_w2)
    coarse = lax.reduce_precision(gain_one, 8, 7)
    small = jnp.concatenate(
        [
            conv_in_w.reshape(TAPS * ACT, WIDE),
            coarse[None].astype(bf16),
            (gain_one - coarse)[None].astype(bf16),
            jnp.zeros((WIN - 37, WIDE), bf16),
        ]
    )

    dz = (0, -1, 1, 2)
    order = [((zh + dz[r % 4]) % 4) * 4 + (y + dy) % 4 for dy in (0, -1, 1, 2) for r in range(4)]
    order = jnp.stack(order + [core]).astype(jnp.int32)
    side, step = (0, 0, 1, 0, 1, 0, 1, 1), (0, 1, 0, 2, 1, 3, 2, 3)
    slots = [
        (zl if b == 0 else 1 - zl) * 4 + (x + s * (2 * core - 1)) % 4 for b, s in zip(side, step)
    ]
    early = jnp.stack([zh, y, core] + slots[:7]).astype(jnp.int32)
    late = jnp.stack([zh, y, core] + slots[7:]).astype(jnp.int32)
    order, early, late = tie(order, early, late)
    near_pieces = (line_a, line_b, down_a, down_b, up_a, up_b)
    part = film_of(order, cond_blocks, range(12), near_pieces, sibling)
    far_a, far_b, part, small, window, w_far = tie(far_a, far_b, part, small, window, w_far)
    far_sibling = (cores(far_a), cores(far_b))
    film = film_of(order, cond_blocks, range(12, 16), (far_a, far_b), far_sibling, part, small)

    a_one, b_own = x_ring(film), zl_swap(film)
    far_one, other_far = y_ring(w_far), cores(w_far)
    acts = first_of(0, window, film, None)
    a_one, far_one, acts = tie(a_one, far_one, acts)
    a_two, far_two, other_one = x_ring(a_one), y_ring(far_one), cores(far_one)
    acts = first_of(1, window, a_one, acts)
    b_own, acts = tie(b_own, acts)
    b_one = x_ring(b_own)
    acts = first_of(2, window, b_own, acts)
    a_two, far_two, acts = tie(a_two, far_two, acts)
    a_three, far_three, other_two = x_ring(a_two), y_ring(far_two), cores(far_two)
    acts = first_of(3, window, a_two, acts)
    b_one, acts = tie(b_one, acts)
    b_two = x_ring(b_one)
    acts = first_of(4, window, b_one, acts)
    acts = first_of(5, window, a_three, acts)
    b_two, far_three, acts = tie(b_two, far_three, acts)
    b_three, other_three = x_ring(b_two), cores(far_three)
    acts = first_of(6, window, b_two, acts)

    weights = (w_own, w_near, w_far, far_one, far_two, far_three)
    weights += (other_far, other_one, other_two, other_three)
    conv = mid_of(early, 7, acts, weights)
    conv, stats = end_of(late, window, b_three, conv, weights)
    other = z_pair(stats)

    out_h = lax.dynamic_slice_in_dim(out_w, zp * HALF, HALF, 0).T
    out_h = jnp.stack([jnp.pad(out_h, ((7 * h, 25 - 7 * h), (0, 0))) for h in range(HORIZON)])
    res_h = lax.dynamic_slice_in_dim(residual_w, zp * HALF, HALF, 1)
    res_h = jnp.pad(res_h, ((14, WIN - 21), (0, 0)))
    gain_h = lax.dynamic_slice_in_dim(gain_two, zp * HALF, HALF, 0)[None]
    part = last_of(conv, stats, other, gain_h, window, res_h, out_h)

    got = lax.all_to_all(part, ("zp", "zl", "x"), split_axis=0, concat_axis=0, tiled=True)
    eps = jnp.sum(got.astype(f32), axis=0).T[:, :28]

    root_b, root_a, of_start, of_sample, of_noise = denoise_coefficients(timestep)
    start = jnp.clip((noisy_sample - root_b * eps) / root_a, -1.0, 1.0)
    denoised = of_start * start + of_sample * noisy_sample + of_noise * noise
    return (eps, denoised)


def solution(mesh):
    fine = Mesh(mesh.devices.reshape(SIZES), AXES)
    return jax.shard_map(
        body,
        mesh=fine,
        in_specs=(
            P(DP, None),
            P(DP),
            P(DP, None),
            P(DP, None),
            P(),
            P(),
            P(DP, None, TENSOR),
            P(None, None, TENSOR),
            P(None, TENSOR),
            P(None, DP, TENSOR),
            P(TENSOR, None),
            P(TENSOR),
            P(TENSOR),
        ),
        out_specs=(P(DP, None), P(DP, None)),
        check_vma=False,
    )
```

```python
import math

import jax
import jax.numpy as jnp
import numpy as np
from jax import lax
from jax.experimental import pallas as pl
from jax.experimental.pallas import tpu as pltpu
from jax.sharding import Mesh, PartitionSpec as P

C = 4096
ACT = 7
HORIZON = 4
TAPS = 5
GROUPS = 8
STEP = 256
TRAIN_STEPS = 100
COND = 1280

AXES = ("zq", "zp", "y", "core", "zl", "x")
SIZES = (2, 2, 4, 2, 2, 4)
DP = ("zq", "zp", "y", "core")
TENSOR = ("zl", "x")

OWN = 128
PAIR = 256
ROWS = HORIZON * PAIR
WIDE = 512
HALF = 256
WIN = 64
FILM_ROWS = 2 * PAIR + WIN

f32, bf16 = jnp.float32, jnp.bfloat16


def moves(where):
    pairs = []
    for here in np.ndindex(*SIZES):
        zq, zp, y, core, zl, x = here
        zh, y, core, zl, x = where(2 * zq + zp, y, core, zl, x)
        there = ((zh % 4) // 2, zh % 2, y % 4, core % 2, zl % 2, x % 4)
        pairs.append(
            (int(np.ravel_multi_index(here, SIZES)), int(np.ravel_multi_index(there, SIZES)))
        )
    return pairs


def mover(where):
    pairs = moves(where)
    return lambda array: lax.ppermute(array, AXES, pairs)


z_up = mover(lambda zh, y, core, zl, x: (zh + 1, y, core, zl, x))
z_down = mover(lambda zh, y, core, zl, x: (zh - 1, y, core, zl, x))
z_two = mover(lambda zh, y, core, zl, x: (zh + 2, y, core, zl, x))
z_pair = mover(lambda zh, y, core, zl, x: (zh ^ 1, y, core, zl, x))
y_up = mover(lambda zh, y, core, zl, x: (zh, y + 1, core, zl, x))
y_down = mover(lambda zh, y, core, zl, x: (zh, y - 1, core, zl, x))
cores = mover(lambda zh, y, core, zl, x: (zh, y, 1 - core, zl, x))
zl_swap = mover(lambda zh, y, core, zl, x: (zh, y, core, 1 - zl, x))
y_ring = mover(lambda zh, y, core, zl, x: (zh, y + 1 - 2 * core, core, zl, x))
x_ring = mover(lambda zh, y, core, zl, x: (zh, y, core, zl, x + 1 - 2 * core))


def plan():
    pos = np.arange(TRAIN_STEPS + 1, dtype=np.float64) / TRAIN_STEPS
    curve = np.cos((pos + 0.008) / 1.008 * (math.pi / 2)) ** 2
    betas = np.minimum(1.0 - curve[1:] / curve[:-1], 0.999)
    return jnp.asarray(np.cumprod(1.0 - betas), f32)


def lookup(table, steps):
    onehot = (steps[:, None] == jnp.arange(table.shape[0], dtype=jnp.int32)[None, :]).astype(f32)
    return jnp.sum(onehot * table[None, :], axis=1)


def mish_by_exp(value):
    u = jnp.exp(jnp.minimum(value, 20.0))
    w = u * (u + 2.0)
    return value * (w * pltpu.reciprocal(w + 2.0, approx=True))


def tie(*arrays):
    return lax.optimization_barrier(arrays)


def denoise_coefficients(steps):
    alpha_bar = plan()
    now = lookup(alpha_bar, steps)[:, None]
    before = jnp.where(steps > 0, lookup(alpha_bar, jnp.maximum(steps - 1, 0)), 1.0)[:, None]
    beta_prod = 1.0 - now
    cur_alpha = now / before
    cur_beta = 1.0 - cur_alpha
    return (
        jnp.sqrt(beta_prod),
        jnp.sqrt(now),
        jnp.sqrt(before) * cur_beta / beta_prod,
        jnp.sqrt(cur_alpha) * (1.0 - before) / beta_prod,
        jnp.sqrt((1.0 - before) / beta_prod * cur_beta),
    )


IN_VMEM = pl.BlockSpec(memory_space=pltpu.VMEM)
IN_HBM = pl.BlockSpec(memory_space=pltpu.HBM)
LIMIT = 48
SLOTS = 16


def params(mib, **more):
    return pltpu.CompilerParams(vmem_limit_bytes=mib * 2**20, **more)


def cond_kernel(place_ref, own_ref, partner_ref, w1_ref, w2_ref, cond_ref, window_ref, held_ref):
    lane = lax.broadcasted_iota(jnp.int32, (OWN, 128), 1)
    half_step = STEP // 2
    freqs = jnp.exp(lane.astype(f32) * (-math.log(10000.0) / (half_step - 1)))
    for ref, half in ((own_ref, place_ref[0]), (partner_ref, 1 - place_ref[0])):
        tail = ref[:, 1024:].astype(f32)
        angles = tail[:, 28:29] * freqs
        sinus = jnp.concatenate([jnp.sin(angles), jnp.cos(angles)], axis=1).astype(bf16)
        hidden = mish_by_exp(jnp.dot(sinus, w1_ref[...], preferred_element_type=f32)).astype(bf16)
        feat = jnp.dot(hidden, w2_ref[...], preferred_element_type=f32)
        held_ref[:, :STEP] = mish_by_exp(feat)
        held_ref[:, STEP:] = mish_by_exp(ref[:, :1024].astype(f32))
        rows = pl.ds(pl.multiple_of(half * OWN, OWN), OWN)
        for d in range(16):
            cond_ref[d, rows, :] = held_ref[:, 80 * d : 80 * d + 80].astype(bf16)
        samples = jnp.where(lane < 28, tail, 0.0)
        for p in range(HORIZON):
            seen = pltpu.roll(samples, (14 - 7 * p) % 128, 1)
            seen = jnp.where(lane < 35, seen, 0.0).astype(bf16)
            rows = pl.ds(pl.multiple_of(p * PAIR + half * OWN, OWN), OWN)
            window_ref[rows, :] = seen[:, :WIN]


def cond_of(place, own, partner, w1, w2):
    return pl.pallas_call(
        cond_kernel,
        out_shape=[
            jax.ShapeDtypeStruct((16, PAIR, 80), bf16),
            jax.ShapeDtypeStruct((ROWS, WIN), bf16),
        ],
        in_specs=[pl.BlockSpec(memory_space=pltpu.SMEM)] + [IN_VMEM] * 4,
        out_specs=[IN_VMEM] * 2,
        scratch_shapes=[pltpu.VMEM((OWN, COND), f32)],
        compiler_params=params(16),
        name="cond",
    )(place, own, partner, w1, w2)


def film_kernel(blocks, order_ref, cond_ref, *refs):
    pieces, refs = refs[: len(blocks)], refs[len(blocks) :]
    half = len(blocks) // 2
    more = len(refs) == 3
    for side in range(2):
        total = refs[0][side] if more else jnp.zeros((PAIR, WIDE), f32)
        for at, block in enumerate(blocks):
            total += jnp.dot(
                cond_ref[order_ref[block]],
                pieces[side * half + at // 2][at % 2],
                preferred_element_type=f32,
            )
        if more:
            place = order_ref[16] if side == 0 else 1 - order_ref[16]
            rows = pl.ds(pl.multiple_of(place * PAIR, PAIR), PAIR)
            refs[2][rows, :] = total.astype(bf16)
        else:
            refs[0][side] = total
    if more:
        refs[2][2 * PAIR :, :] = refs[1][...]


def film_of(order, cond_blocks, blocks, mine, sibling, *more):
    out = ((FILM_ROWS, WIDE), bf16) if more else ((2, PAIR, WIDE), f32)
    return pl.pallas_call(
        lambda *refs: film_kernel(blocks, *refs),
        out_shape=jax.ShapeDtypeStruct(*out),
        in_specs=[pl.BlockSpec(memory_space=pltpu.SMEM)]
        + [IN_VMEM] * (1 + len(blocks) + len(more)),
        out_specs=IN_VMEM,
        compiler_params=params(16),
        cost_estimate=pl.CostEstimate(flops=1, bytes_accessed=1, transcendentals=0),
        name="film",
    )(order, cond_blocks, *mine, *sibling, *more)


def split_kernel(place_ref, weight_ref, keep_ref, give_ref):
    for ref, which in ((keep_ref, place_ref[0]), (give_ref, 1 - place_ref[0])):
        at = pl.ds(pl.multiple_of(which * HALF, HALF), HALF)
        for k in range(TAPS):
            ref[:, k * HALF : (k + 1) * HALF] = weight_ref[k, :, at]


def split_of(place, weight):
    return pl.pallas_call(
        split_kernel,
        out_shape=[jax.ShapeDtypeStruct((OWN, TAPS * HALF), bf16)] * 2,
        in_specs=[pl.BlockSpec(memory_space=pltpu.SMEM), IN_VMEM],
        out_specs=[IN_VMEM] * 2,
        compiler_params=params(16),
        name="split",
    )(place, weight)


def join_kernel(count, *refs):
    for at in range(count):
        refs[-1][at] = refs[at][...]


def join_of(arrays, after):
    return pl.pallas_call(
        lambda *refs: join_kernel(len(arrays), *refs),
        out_shape=jax.ShapeDtypeStruct((len(arrays), *arrays[0].shape), bf16),
        in_specs=[IN_VMEM] * len(arrays) + [pl.BlockSpec(memory_space=pl.ANY)] * len(after),
        out_specs=IN_VMEM,
        compiler_params=params(16),
        cost_estimate=pl.CostEstimate(flops=1, bytes_accessed=1, transcendentals=0),
        name="join",
    )(*arrays, *after)


def first_rows(window_ref, film_ref, hidden_ref, act_ref, after):
    hidden_ref[...] = jnp.dot(
        window_ref[...], film_ref[2 * PAIR :, :], preferred_element_type=f32
    )
    gain = (
        film_ref[2 * PAIR + 35 : 2 * PAIR + 36, :].astype(f32)
        + film_ref[2 * PAIR + 36 : 2 * PAIR + 37, :].astype(f32)
    )

    def lanes(value):
        return sum(value[:, c : c + 128] for c in range(0, WIDE, 128))

    parts = [slice(p * PAIR, (p + 1) * PAIR) for p in range(HORIZON)]
    total = sum(lanes(hidden_ref[a, :]) for a in parts)
    mean = jnp.sum(total, axis=1, keepdims=True) * (1.0 / (HORIZON * WIDE))
    total = sum(lanes((hidden_ref[a, :] - mean) ** 2) for a in parts)
    var = jnp.sum(total, axis=1, keepdims=True) * (1.0 / (HORIZON * WIDE))
    inv = lax.rsqrt(var + 1e-05)
    few = 16
    for r in range(0, PAIR, few):
        at = slice(r, r + few)
        scale = film_ref[at, :].astype(f32)
        shift = film_ref[PAIR + r : PAIR + r + few, :].astype(f32)
        for p in range(HORIZON):
            a = slice(p * PAIR + r, p * PAIR + r + few)
            normed = (hidden_ref[a, :] - mean[at]) * (inv[at] * gain)
            act_ref[p, at, :] = (scale * mish_by_exp(normed) + shift).astype(bf16)
        after(r + few)


def first_kernel(slot, window_ref, film_ref, *rest):
    out_ref, hidden_ref, act_ref, sem = rest[-4:]
    out_ref, some = out_ref.at[slot], 64

    def after(rows):
        if rows % some == 0:
            done = slice(rows - some, rows)
            pltpu.make_async_copy(act_ref.at[:, done], out_ref.at[:, done], sem).start()

    first_rows(window_ref, film_ref, hidden_ref, act_ref, after)
    pltpu.make_async_copy(act_ref, out_ref, sem).wait()


def first_of(slot, window, film, before):
    more = [] if before is None else [before]
    return pl.pallas_call(
        lambda *refs: first_kernel(slot, *refs),
        out_shape=jax.ShapeDtypeStruct((SLOTS, HORIZON, PAIR, WIDE), bf16),
        in_specs=[IN_VMEM, IN_VMEM] + [IN_HBM] * len(more),
        out_specs=IN_HBM,
        scratch_shapes=[
            pltpu.VMEM((ROWS, WIDE), f32),
            pltpu.VMEM((HORIZON, PAIR, WIDE), bf16),
            pltpu.SemaphoreType.DMA,
        ],
        input_output_aliases={2: 0} if more else {},
        compiler_params=params(LIMIT),
        cost_estimate=pl.CostEstimate(flops=1, bytes_accessed=1, transcendentals=0),
        name="first",
    )(window, film, *more)


def fetch_weights(place_ref, block, refs, into, sem):
    own_ref, near_ref, mine_refs, theirs_refs = refs[0], refs[1], refs[2:6], refs[6:10]
    zh, y, core = place_ref[0], place_ref[1], place_ref[2]
    q, apart = block % 2, (block // 2 + 4 - zh) % 4

    @pl.when(apart == 0)
    def _():
        pltpu.make_async_copy(own_ref.at[pl.ds(4 * q, 4)], into, sem).start()

    for way, side in ((3, 0), (1, 1)):

        @pl.when(apart == way)
        def _():
            pltpu.make_async_copy(near_ref.at[pl.ds(4 * q, 4), side], into, sem).start()

    for odd in range(2):
        for far_refs, its in ((mine_refs, core), (theirs_refs, 1 - core)):
            steps = ((1 - 2 * its) * (y - 2 * q - odd) + 8) % 4
            for j in range(4):

                @pl.when(jnp.logical_and(apart == 2, steps == j))
                def _():
                    pltpu.make_async_copy(far_refs[j], into.at[2 * odd + its], sem).start()


def add_block(act, weight, before_ref, out_ref):
    for h in range(HORIZON):
        at = slice(h * PAIR, (h + 1) * PAIR)
        total = None if before_ref is None else before_ref[at, :]
        for p in range(HORIZON):
            k = p - h + 2
            if 0 <= k < TAPS:
                term = jnp.dot(
                    act[p],
                    weight[:, :, k * HALF : (k + 1) * HALF].reshape(WIDE, HALF),
                    preferred_element_type=f32,
                )
                total = term if total is None else total + term
        out_ref[at, :] = total


def mid_kernel(count, place_ref, acts_ref, *refs):
    out_ref, held, act_held, sems = refs[-4:]
    weights = refs[:10]

    def fetch(step):
        at = step % 3
        pltpu.make_async_copy(acts_ref.at[step], act_held.at[at], sems.at[1, at]).start()
        fetch_weights(place_ref, place_ref[3 + step], weights, held.at[at], sems.at[0, at])

    for step in range(2):
        fetch(step)
    for step in range(count):
        if step + 2 < count:
            fetch(step + 2)
        at = step % 3
        pltpu.make_async_copy(weights[0].at[pl.ds(0, 4)], held.at[at], sems.at[0, at]).wait()
        pltpu.make_async_copy(acts_ref.at[step], act_held.at[at], sems.at[1, at]).wait()
        add_block(act_held.at[at], held.at[at], out_ref if step else None, out_ref)


def mid_of(place, count, acts, weights):
    return pl.pallas_call(
        lambda *refs: mid_kernel(count, *refs),
        out_shape=jax.ShapeDtypeStruct((ROWS, HALF), f32),
        in_specs=[pl.BlockSpec(memory_space=pltpu.SMEM)] + [IN_HBM] * 11,
        out_specs=IN_VMEM,
        scratch_shapes=[
            pltpu.VMEM((3, 4, OWN, TAPS * HALF), bf16),
            pltpu.VMEM((3, HORIZON, PAIR, WIDE), bf16),
            pltpu.SemaphoreType.DMA((2, 3)),
        ],
        compiler_params=params(LIMIT),
        cost_estimate=pl.CostEstimate(flops=1, bytes_accessed=1, transcendentals=0),
        name="mid",
    )(place, acts, *weights)


def end_kernel(place_ref, window_ref, film_ref, before_ref, *refs):
    out_ref, stats_ref, hidden_ref, act_ref, held, sem = refs[-6:]
    weights = refs[:10]
    fetch_weights(place_ref, place_ref[3], weights, held, sem)
    first_rows(window_ref, film_ref, hidden_ref, act_ref, lambda rows: None)
    pltpu.make_async_copy(weights[0].at[pl.ds(0, 4)], held, sem).wait()
    add_block(act_ref, held, before_ref, out_ref)
    parts = [out_ref[h * PAIR : (h + 1) * PAIR, :] for h in range(HORIZON)]
    mean = jnp.sum(sum(parts), axis=1, keepdims=True) * (1.0 / (HORIZON * HALF))
    spread = jnp.sum(sum((o - mean) ** 2 for o in parts), axis=1, keepdims=True)
    lane = lax.broadcasted_iota(jnp.int32, (PAIR, 128), 1)
    both = jnp.where(lane == 0, mean, jnp.where(lane == 1, spread, 0.0))
    stats_ref[...] = both.T[:8, :]


def end_of(place, window, film, before, weights):
    return pl.pallas_call(
        end_kernel,
        out_shape=[
            jax.ShapeDtypeStruct((ROWS, HALF), f32),
            jax.ShapeDtypeStruct((8, PAIR), f32),
        ],
        in_specs=[pl.BlockSpec(memory_space=pltpu.SMEM)] + [IN_VMEM] * 3 + [IN_HBM] * 10,
        out_specs=[IN_VMEM] * 2,
        scratch_shapes=[
            pltpu.VMEM((ROWS, WIDE), f32),
            pltpu.VMEM((HORIZON, PAIR, WIDE), bf16),
            pltpu.VMEM((4, OWN, TAPS * HALF), bf16),
            pltpu.SemaphoreType.DMA,
        ],
        compiler_params=params(LIMIT),
        cost_estimate=pl.CostEstimate(flops=1, bytes_accessed=1, transcendentals=0),
        name="end",
    )(place, window, film, before, *weights)


def last_kernel(conv_ref, own_ref, other_ref, gain_ref, window_ref, res_ref, out_w_ref, eps_ref):
    rows = jnp.concatenate([own_ref[...], other_ref[...], jnp.zeros((112, PAIR), f32)], axis=0).T
    mean_a, spread_a = rows[:, 0:1], rows[:, 1:2]
    mean_b, spread_b = rows[:, 8:9], rows[:, 9:10]
    each = HORIZON * HALF
    mean = 0.5 * (mean_a + mean_b)
    var = (spread_a + spread_b + (mean_a - mean_b) ** 2 * (0.5 * each)) * (0.5 / each)
    inv = lax.rsqrt(var + 1e-05)
    total = jnp.zeros((32, PAIR), f32)
    for h in range(HORIZON):
        at = slice(h * PAIR, (h + 1) * PAIR)
        normed = (conv_ref[at, :] - mean) * inv * gain_ref[...]
        skip = jnp.dot(window_ref[at, :], res_ref[...], preferred_element_type=f32)
        act = (mish_by_exp(normed) + skip).astype(bf16)
        total += lax.dot_general(
            out_w_ref[h], act, (((1,), (1,)), ((), ())), preferred_element_type=f32
        )
    for b in range(2):
        part = total[:, b * OWN : (b + 1) * OWN].astype(bf16)
        for copy in range(8):
            eps_ref[8 * b + copy] = part


def last_of(conv, own, other, gain, window, res, out_w):
    return pl.pallas_call(
        last_kernel,
        out_shape=jax.ShapeDtypeStruct((16, 32, OWN), bf16),
        in_specs=[pl.BlockSpec(memory_space=pltpu.VMEM)] * 7,
        out_specs=pl.BlockSpec(memory_space=pltpu.VMEM),
        compiler_params=params(24),
        cost_estimate=pl.CostEstimate(
            flops=2 * ROWS * HALF * 80, bytes_accessed=2 * 2**20, transcendentals=ROWS * HALF
        ),
        name="last",
    )(conv, own, other, gain, window, res, out_w)


def body(
    noisy_sample,
    timestep,
    noise,
    obs_feat,
    step_w1,
    step_w2,
    film_weight,
    conv_in_w,
    residual_w,
    conv_mid_w,
    out_w,
    gain_one,
    gain_two,
):
    zq, zp, y, core, zl, x = (lax.axis_index(a) for a in AXES)
    zh = 2 * zq + zp

    packed = jnp.concatenate(
        [
            obs_feat,
            noisy_sample.astype(bf16),
            timestep.astype(f32).astype(bf16)[:, None],
            jnp.zeros((OWN, 99), bf16),
        ],
        axis=1,
    )

    stay = lax.dynamic_index_in_dim(film_weight, core, 1, keepdims=False)
    go = lax.dynamic_index_in_dim(film_weight, 1 - core, 1, keepdims=False)
    come = cores(go)

    pair_place = zp.reshape(1).astype(jnp.int32)
    keep, give = split_of(pair_place, conv_mid_w)
    w_own = lax.all_gather(keep, ("y", "core"), axis=0, tiled=False)

    chip = jnp.where(
        core == 0, jnp.concatenate([stay, come]), jnp.concatenate([come, stay])
    )
    z_a, z_b, z_c = z_up(chip), z_down(chip), z_two(chip)
    line_a, line_b = jnp.stack([chip, z_a]), jnp.stack([z_b, z_c])
    partner = z_pair(packed)
    line_a, line_b, partner, give = tie(line_a, line_b, partner, give)
    down_a, up_a, down_b, up_b = y_up(line_a), y_down(line_a), y_up(line_b), y_down(line_b)
    w_up, w_down = z_up(give), z_down(give)
    sibling = [cores(line_a), cores(line_b)]
    far_a, far_b = y_up(down_a), y_down(up_b)
    early_pieces = (far_a, far_b, down_b, up_a, *sibling, w_own[0, :16, :128])
    w_near = join_of((w_up, w_down), early_pieces)
    w_near = lax.all_gather(w_near, ("y", "core"), axis=0, tiled=False)
    w_far = z_two(keep)
    sibling += [cores(piece) for piece in (down_a, down_b, up_a, up_b)]

    cond_blocks, window = cond_of(pair_place, packed, partner, step_w1, step_w2)
    coarse = lax.reduce_precision(gain_one, 8, 7)
    small = jnp.concatenate(
        [
            conv_in_w.reshape(TAPS * ACT, WIDE),
            coarse[None].astype(bf16),
            (gain_one - coarse)[None].astype(bf16),
            jnp.zeros((WIN - 37, WIDE), bf16),
        ]
    )

    dz = (0, -1, 1, 2)
    order = [((zh + dz[r % 4]) % 4) * 4 + (y + dy) % 4 for dy in (0, -1, 1, 2) for r in range(4)]
    order = jnp.stack(order + [core]).astype(jnp.int32)
    side, step = (0, 0, 1, 0, 1, 0, 1, 1), (0, 1, 0, 2, 1, 3, 2, 3)
    slots = [
        (zl if b == 0 else 1 - zl) * 4 + (x + s * (2 * core - 1)) % 4 for b, s in zip(side, step)
    ]
    early = jnp.stack([zh, y, core] + slots[:7]).astype(jnp.int32)
    late = jnp.stack([zh, y, core] + slots[7:]).astype(jnp.int32)
    order, early, late = tie(order, early, late)
    near_pieces = (line_a, line_b, down_a, down_b, up_a, up_b)
    part = film_of(order, cond_blocks, range(12), near_pieces, sibling)
    far_a, far_b, part, small, window, w_far = tie(far_a, far_b, part, small, window, w_far)
    far_sibling = (cores(far_a), cores(far_b))
    film = film_of(order, cond_blocks, range(12, 16), (far_a, far_b), far_sibling, part, small)

    a_one, b_own = x_ring(film), zl_swap(film)
    far_one, other_far = y_ring(w_far), cores(w_far)
    acts = first_of(0, window, film, None)
    a_one, far_one, acts = tie(a_one, far_one, acts)
    a_two, far_two, other_one = x_ring(a_one), y_ring(far_one), cores(far_one)
    acts = first_of(1, window, a_one, acts)
    b_own, acts = tie(b_own, acts)
    b_one = x_ring(b_own)
    acts = first_of(2, window, b_own, acts)
    a_two, far_two, acts = tie(a_two, far_two, acts)
    a_three, far_three, other_two = x_ring(a_two), y_ring(far_two), cores(far_two)
    acts = first_of(3, window, a_two, acts)
    b_one, acts = tie(b_one, acts)
    b_two = x_ring(b_one)
    acts = first_of(4, window, b_one, acts)
    acts = first_of(5, window, a_three, acts)
    b_two, far_three, acts = tie(b_two, far_three, acts)
    b_three, other_three = x_ring(b_two), cores(far_three)
    acts = first_of(6, window, b_two, acts)

    weights = (w_own, w_near, w_far, far_one, far_two, far_three)
    weights += (other_far, other_one, other_two, other_three)
    conv = mid_of(early, 7, acts, weights)
    conv, stats = end_of(late, window, b_three, conv, weights)
    other = z_pair(stats)

    out_h = lax.dynamic_slice_in_dim(out_w, zp * HALF, HALF, 0).T
    out_h = jnp.stack([jnp.pad(out_h, ((7 * h, 25 - 7 * h), (0, 0))) for h in range(HORIZON)])
    res_h = lax.dynamic_slice_in_dim(residual_w, zp * HALF, HALF, 1)
    res_h = jnp.pad(res_h, ((14, WIN - 21), (0, 0)))
    gain_h = lax.dynamic_slice_in_dim(gain_two, zp * HALF, HALF, 0)[None]
    part = last_of(conv, stats, other, gain_h, window, res_h, out_h)

    got = lax.all_to_all(part, ("zp", "zl", "x"), split_axis=0, concat_axis=0, tiled=True)
    eps = jnp.sum(got.astype(f32), axis=0).T[:, :28]

    root_b, root_a, of_start, of_sample, of_noise = denoise_coefficients(timestep)
    start = jnp.clip((noisy_sample - root_b * eps) / root_a, -1.0, 1.0)
    denoised = of_start * start + of_sample * noisy_sample + of_noise * noise
    return (eps, denoised)


def solution(mesh):
    fine = Mesh(mesh.devices.reshape(SIZES), AXES)
    return jax.shard_map(
        body,
        mesh=fine,
        in_specs=(
            P(DP, None),
            P(DP),
            P(DP, None),
            P(DP, None),
            P(),
            P(),
            P(DP, None, TENSOR),
            P(None, None, TENSOR),
            P(None, TENSOR),
            P(None, DP, TENSOR),
            P(TENSOR, None),
            P(TENSOR),
            P(TENSOR),
        ),
        out_specs=(P(DP, None), P(DP, None)),
        check_vma=False,
    )
```

```python
import math

import jax
import jax.numpy as jnp
import numpy as np
from jax import lax
from jax.experimental import pallas as pl
from jax.experimental.pallas import tpu as pltpu
from jax.sharding import Mesh, PartitionSpec as P

C = 4096
ACT = 7
HORIZON = 4
TAPS = 5
GROUPS = 8
STEP = 256
TRAIN_STEPS = 100
COND = 1280

AXES = ("zq", "zp", "y", "core", "zl", "x")
SIZES = (2, 2, 4, 2, 2, 4)
DP = ("zq", "zp", "y", "core")
TENSOR = ("zl", "x")

OWN = 128
PAIR = 256
ROWS = HORIZON * PAIR
WIDE = 512
HALF = 256
WIN = 64
FILM_ROWS = 2 * PAIR + WIN

f32, bf16 = jnp.float32, jnp.bfloat16


def moves(where):
    pairs = []
    for here in np.ndindex(*SIZES):
        zq, zp, y, core, zl, x = here
        zh, y, core, zl, x = where(2 * zq + zp, y, core, zl, x)
        there = ((zh % 4) // 2, zh % 2, y % 4, core % 2, zl % 2, x % 4)
        pairs.append(
            (int(np.ravel_multi_index(here, SIZES)), int(np.ravel_multi_index(there, SIZES)))
        )
    return pairs


def mover(where):
    pairs = moves(where)
    return lambda array: lax.ppermute(array, AXES, pairs)


z_up = mover(lambda zh, y, core, zl, x: (zh + 1, y, core, zl, x))
z_down = mover(lambda zh, y, core, zl, x: (zh - 1, y, core, zl, x))
z_two = mover(lambda zh, y, core, zl, x: (zh + 2, y, core, zl, x))
z_pair = mover(lambda zh, y, core, zl, x: (zh ^ 1, y, core, zl, x))
y_up = mover(lambda zh, y, core, zl, x: (zh, y + 1, core, zl, x))
y_down = mover(lambda zh, y, core, zl, x: (zh, y - 1, core, zl, x))
cores = mover(lambda zh, y, core, zl, x: (zh, y, 1 - core, zl, x))
zl_swap = mover(lambda zh, y, core, zl, x: (zh, y, core, 1 - zl, x))
y_ring = mover(lambda zh, y, core, zl, x: (zh, y + 1 - 2 * core, core, zl, x))
x_ring = mover(lambda zh, y, core, zl, x: (zh, y, core, zl, x + 1 - 2 * core))


def plan():
    pos = np.arange(TRAIN_STEPS + 1, dtype=np.float64) / TRAIN_STEPS
    curve = np.cos((pos + 0.008) / 1.008 * (math.pi / 2)) ** 2
    betas = np.minimum(1.0 - curve[1:] / curve[:-1], 0.999)
    return jnp.asarray(np.cumprod(1.0 - betas), f32)


def lookup(table, steps):
    onehot = (steps[:, None] == jnp.arange(table.shape[0], dtype=jnp.int32)[None, :]).astype(f32)
    return jnp.sum(onehot * table[None, :], axis=1)


def mish_by_exp(value):
    u = jnp.exp(jnp.minimum(value, 20.0))
    w = u * (u + 2.0)
    return value * (w * pltpu.reciprocal(w + 2.0, approx=True))


def tie(*arrays):
    return lax.optimization_barrier(arrays)


def denoise_coefficients(steps):
    alpha_bar = plan()
    now = lookup(alpha_bar, steps)[:, None]
    before = jnp.where(steps > 0, lookup(alpha_bar, jnp.maximum(steps - 1, 0)), 1.0)[:, None]
    beta_prod = 1.0 - now
    cur_alpha = now / before
    cur_beta = 1.0 - cur_alpha
    return (
        jnp.sqrt(beta_prod),
        jnp.sqrt(now),
        jnp.sqrt(before) * cur_beta / beta_prod,
        jnp.sqrt(cur_alpha) * (1.0 - before) / beta_prod,
        jnp.sqrt((1.0 - before) / beta_prod * cur_beta),
    )


IN_VMEM = pl.BlockSpec(memory_space=pltpu.VMEM)
IN_HBM = pl.BlockSpec(memory_space=pltpu.HBM)
LIMIT = 48
SLOTS = 16


def params(mib, **more):
    return pltpu.CompilerParams(vmem_limit_bytes=mib * 2**20, **more)


def cond_kernel(place_ref, own_ref, partner_ref, w1_ref, w2_ref, cond_ref, window_ref, held_ref):
    lane = lax.broadcasted_iota(jnp.int32, (OWN, 128), 1)
    half_step = STEP // 2
    freqs = jnp.exp(lane.astype(f32) * (-math.log(10000.0) / (half_step - 1)))
    for ref, half in ((own_ref, place_ref[0]), (partner_ref, 1 - place_ref[0])):
        tail = ref[:, 1024:].astype(f32)
        angles = tail[:, 28:29] * freqs
        sinus = jnp.concatenate([jnp.sin(angles), jnp.cos(angles)], axis=1).astype(bf16)
        hidden = mish_by_exp(jnp.dot(sinus, w1_ref[...], preferred_element_type=f32)).astype(bf16)
        feat = jnp.dot(hidden, w2_ref[...], preferred_element_type=f32)
        held_ref[:, :STEP] = mish_by_exp(feat)
        held_ref[:, STEP:] = mish_by_exp(ref[:, :1024].astype(f32))
        rows = pl.ds(pl.multiple_of(half * OWN, OWN), OWN)
        for d in range(16):
            cond_ref[d, rows, :] = held_ref[:, 80 * d : 80 * d + 80].astype(bf16)
        samples = jnp.where(lane < 28, tail, 0.0)
        for p in range(HORIZON):
            seen = pltpu.roll(samples, (14 - 7 * p) % 128, 1)
            seen = jnp.where(lane < 35, seen, 0.0).astype(bf16)
            rows = pl.ds(pl.multiple_of(p * PAIR + half * OWN, OWN), OWN)
            window_ref[rows, :] = seen[:, :WIN]


def cond_of(place, own, partner, w1, w2):
    return pl.pallas_call(
        cond_kernel,
        out_shape=[
            jax.ShapeDtypeStruct((16, PAIR, 80), bf16),
            jax.ShapeDtypeStruct((ROWS, WIN), bf16),
        ],
        in_specs=[pl.BlockSpec(memory_space=pltpu.SMEM)] + [IN_VMEM] * 4,
        out_specs=[IN_VMEM] * 2,
        scratch_shapes=[pltpu.VMEM((OWN, COND), f32)],
        compiler_params=params(16),
        name="cond",
    )(place, own, partner, w1, w2)


def film_kernel(blocks, order_ref, cond_ref, *refs):
    pieces, refs = refs[: len(blocks)], refs[len(blocks) :]
    half = len(blocks) // 2
    more = len(refs) == 3
    for side in range(2):
        total = refs[0][side] if more else jnp.zeros((PAIR, WIDE), f32)
        for at, block in enumerate(blocks):
            total += jnp.dot(
                cond_ref[order_ref[block]],
                pieces[side * half + at // 2][at % 2],
                preferred_element_type=f32,
            )
        if more:
            place = order_ref[16] if side == 0 else 1 - order_ref[16]
            rows = pl.ds(pl.multiple_of(place * PAIR, PAIR), PAIR)
            refs[2][rows, :] = total.astype(bf16)
        else:
            refs[0][side] = total
    if more:
        refs[2][2 * PAIR :, :] = refs[1][...]


def film_of(order, cond_blocks, blocks, mine, sibling, *more):
    out = ((FILM_ROWS, WIDE), bf16) if more else ((2, PAIR, WIDE), f32)
    return pl.pallas_call(
        lambda *refs: film_kernel(blocks, *refs),
        out_shape=jax.ShapeDtypeStruct(*out),
        in_specs=[pl.BlockSpec(memory_space=pltpu.SMEM)]
        + [IN_VMEM] * (1 + len(blocks) + len(more)),
        out_specs=IN_VMEM,
        compiler_params=params(16),
        cost_estimate=pl.CostEstimate(flops=1, bytes_accessed=1, transcendentals=0),
        name="film",
    )(order, cond_blocks, *mine, *sibling, *more)


def split_kernel(place_ref, weight_ref, keep_ref, give_ref):
    for ref, which in ((keep_ref, place_ref[0]), (give_ref, 1 - place_ref[0])):
        at = pl.ds(pl.multiple_of(which * HALF, HALF), HALF)
        for k in range(TAPS):
            ref[:, k * HALF : (k + 1) * HALF] = weight_ref[k, :, at]


def split_of(place, weight):
    return pl.pallas_call(
        split_kernel,
        out_shape=[jax.ShapeDtypeStruct((OWN, TAPS * HALF), bf16)] * 2,
        in_specs=[pl.BlockSpec(memory_space=pltpu.SMEM), IN_VMEM],
        out_specs=[IN_VMEM] * 2,
        compiler_params=params(16),
        name="split",
    )(place, weight)


def join_kernel(count, *refs):
    for at in range(count):
        refs[-1][at] = refs[at][...]


def join_of(arrays, after):
    return pl.pallas_call(
        lambda *refs: join_kernel(len(arrays), *refs),
        out_shape=jax.ShapeDtypeStruct((len(arrays), *arrays[0].shape), bf16),
        in_specs=[IN_VMEM] * len(arrays) + [pl.BlockSpec(memory_space=pl.ANY)] * len(after),
        out_specs=IN_VMEM,
        compiler_params=params(16),
        cost_estimate=pl.CostEstimate(flops=1, bytes_accessed=1, transcendentals=0),
        name="join",
    )(*arrays, *after)


def first_rows(window_ref, film_ref, hidden_ref, act_ref, after):
    hidden_ref[...] = jnp.dot(
        window_ref[...], film_ref[2 * PAIR :, :], preferred_element_type=f32
    )
    gain = (
        film_ref[2 * PAIR + 35 : 2 * PAIR + 36, :].astype(f32)
        + film_ref[2 * PAIR + 36 : 2 * PAIR + 37, :].astype(f32)
    )

    def lanes(value):
        return sum(value[:, c : c + 128] for c in range(0, WIDE, 128))

    parts = [slice(p * PAIR, (p + 1) * PAIR) for p in range(HORIZON)]
    total = sum(lanes(hidden_ref[a, :]) for a in parts)
    mean = jnp.sum(total, axis=1, keepdims=True) * (1.0 / (HORIZON * WIDE))
    total = sum(lanes((hidden_ref[a, :] - mean) ** 2) for a in parts)
    var = jnp.sum(total, axis=1, keepdims=True) * (1.0 / (HORIZON * WIDE))
    inv = lax.rsqrt(var + 1e-05)
    few = 16
    for r in range(0, PAIR, few):
        at = slice(r, r + few)
        scale = film_ref[at, :].astype(f32)
        shift = film_ref[PAIR + r : PAIR + r + few, :].astype(f32)
        for p in range(HORIZON):
            a = slice(p * PAIR + r, p * PAIR + r + few)
            normed = (hidden_ref[a, :] - mean[at]) * (inv[at] * gain)
            act_ref[p, at, :] = (scale * mish_by_exp(normed) + shift).astype(bf16)
        after(r + few)


def first_kernel(slot, window_ref, film_ref, *rest):
    out_ref, hidden_ref, act_ref, sem = rest[-4:]
    out_ref, some = out_ref.at[slot], 64

    def after(rows):
        if rows % some == 0:
            done = slice(rows - some, rows)
            pltpu.make_async_copy(act_ref.at[:, done], out_ref.at[:, done], sem).start()

    first_rows(window_ref, film_ref, hidden_ref, act_ref, after)
    pltpu.make_async_copy(act_ref, out_ref, sem).wait()


def first_of(slot, window, film, before):
    more = [] if before is None else [before]
    return pl.pallas_call(
        lambda *refs: first_kernel(slot, *refs),
        out_shape=jax.ShapeDtypeStruct((SLOTS, HORIZON, PAIR, WIDE), bf16),
        in_specs=[IN_VMEM, IN_VMEM] + [IN_HBM] * len(more),
        out_specs=IN_HBM,
        scratch_shapes=[
            pltpu.VMEM((ROWS, WIDE), f32),
            pltpu.VMEM((HORIZON, PAIR, WIDE), bf16),
            pltpu.SemaphoreType.DMA,
        ],
        input_output_aliases={2: 0} if more else {},
        compiler_params=params(LIMIT),
        cost_estimate=pl.CostEstimate(flops=1, bytes_accessed=1, transcendentals=0),
        name="first",
    )(window, film, *more)


def fetch_weights(place_ref, block, refs, into, sem):
    own_ref, near_ref, mine_refs, theirs_refs = refs[0], refs[1], refs[2:6], refs[6:10]
    zh, y, core = place_ref[0], place_ref[1], place_ref[2]
    q, apart = block % 2, (block // 2 + 4 - zh) % 4

    @pl.when(apart == 0)
    def _():
        pltpu.make_async_copy(own_ref.at[pl.ds(4 * q, 4)], into, sem).start()

    for way, side in ((3, 0), (1, 1)):

        @pl.when(apart == way)
        def _():
            pltpu.make_async_copy(near_ref.at[pl.ds(4 * q, 4), side], into, sem).start()

    for odd in range(2):
        for far_refs, its in ((mine_refs, core), (theirs_refs, 1 - core)):
            steps = ((1 - 2 * its) * (y - 2 * q - odd) + 8) % 4
            for j in range(4):

                @pl.when(jnp.logical_and(apart == 2, steps == j))
                def _():
                    pltpu.make_async_copy(far_refs[j], into.at[2 * odd + its], sem).start()


def add_block(act, weight, before_ref, out_ref):
    for h in range(HORIZON):
        at = slice(h * PAIR, (h + 1) * PAIR)
        total = None if before_ref is None else before_ref[at, :]
        for p in range(HORIZON):
            k = p - h + 2
            if 0 <= k < TAPS:
                term = jnp.dot(
                    act[p],
                    weight[:, :, k * HALF : (k + 1) * HALF].reshape(WIDE, HALF),
                    preferred_element_type=f32,
                )
                total = term if total is None else total + term
        out_ref[at, :] = total


def mid_kernel(count, place_ref, acts_ref, *refs):
    out_ref, held, act_held, sems = refs[-4:]
    weights = refs[:10]

    def fetch(step):
        at = step % 3
        pltpu.make_async_copy(acts_ref.at[step], act_held.at[at], sems.at[1, at]).start()
        fetch_weights(place_ref, place_ref[3 + step], weights, held.at[at], sems.at[0, at])

    for step in range(2):
        fetch(step)
    for step in range(count):
        if step + 2 < count:
            fetch(step + 2)
        at = step % 3
        pltpu.make_async_copy(weights[0].at[pl.ds(0, 4)], held.at[at], sems.at[0, at]).wait()
        pltpu.make_async_copy(acts_ref.at[step], act_held.at[at], sems.at[1, at]).wait()
        add_block(act_held.at[at], held.at[at], out_ref if step else None, out_ref)


def mid_of(place, count, acts, weights):
    return pl.pallas_call(
        lambda *refs: mid_kernel(count, *refs),
        out_shape=jax.ShapeDtypeStruct((ROWS, HALF), f32),
        in_specs=[pl.BlockSpec(memory_space=pltpu.SMEM)] + [IN_HBM] * 11,
        out_specs=IN_VMEM,
        scratch_shapes=[
            pltpu.VMEM((3, 4, OWN, TAPS * HALF), bf16),
            pltpu.VMEM((3, HORIZON, PAIR, WIDE), bf16),
            pltpu.SemaphoreType.DMA((2, 3)),
        ],
        compiler_params=params(LIMIT),
        cost_estimate=pl.CostEstimate(flops=1, bytes_accessed=1, transcendentals=0),
        name="mid",
    )(place, acts, *weights)


def end_kernel(place_ref, window_ref, film_ref, before_ref, *refs):
    out_ref, stats_ref, hidden_ref, act_ref, held, sem = refs[-6:]
    weights = refs[:10]
    fetch_weights(place_ref, place_ref[3], weights, held, sem)
    first_rows(window_ref, film_ref, hidden_ref, act_ref, lambda rows: None)
    pltpu.make_async_copy(weights[0].at[pl.ds(0, 4)], held, sem).wait()
    add_block(act_ref, held, before_ref, out_ref)
    parts = [out_ref[h * PAIR : (h + 1) * PAIR, :] for h in range(HORIZON)]
    mean = jnp.sum(sum(parts), axis=1, keepdims=True) * (1.0 / (HORIZON * HALF))
    spread = jnp.sum(sum((o - mean) ** 2 for o in parts), axis=1, keepdims=True)
    lane = lax.broadcasted_iota(jnp.int32, (PAIR, 128), 1)
    both = jnp.where(lane == 0, mean, jnp.where(lane == 1, spread, 0.0))
    stats_ref[...] = both.T[:8, :]


def end_of(place, window, film, before, weights):
    return pl.pallas_call(
        end_kernel,
        out_shape=[
            jax.ShapeDtypeStruct((ROWS, HALF), f32),
            jax.ShapeDtypeStruct((8, PAIR), f32),
        ],
        in_specs=[pl.BlockSpec(memory_space=pltpu.SMEM)] + [IN_VMEM] * 3 + [IN_HBM] * 10,
        out_specs=[IN_VMEM] * 2,
        scratch_shapes=[
            pltpu.VMEM((ROWS, WIDE), f32),
            pltpu.VMEM((HORIZON, PAIR, WIDE), bf16),
            pltpu.VMEM((4, OWN, TAPS * HALF), bf16),
            pltpu.SemaphoreType.DMA,
        ],
        compiler_params=params(LIMIT),
        cost_estimate=pl.CostEstimate(flops=1, bytes_accessed=1, transcendentals=0),
        name="end",
    )(place, window, film, before, *weights)


def last_kernel(conv_ref, own_ref, other_ref, gain_ref, window_ref, res_ref, out_w_ref, eps_ref):
    rows = jnp.concatenate([own_ref[...], other_ref[...], jnp.zeros((112, PAIR), f32)], axis=0).T
    mean_a, spread_a = rows[:, 0:1], rows[:, 1:2]
    mean_b, spread_b = rows[:, 8:9], rows[:, 9:10]
    each = HORIZON * HALF
    mean = 0.5 * (mean_a + mean_b)
    var = (spread_a + spread_b + (mean_a - mean_b) ** 2 * (0.5 * each)) * (0.5 / each)
    inv = lax.rsqrt(var + 1e-05)
    total = jnp.zeros((32, PAIR), f32)
    for h in range(HORIZON):
        at = slice(h * PAIR, (h + 1) * PAIR)
        normed = (conv_ref[at, :] - mean) * inv * gain_ref[...]
        skip = jnp.dot(window_ref[at, :], res_ref[...], preferred_element_type=f32)
        act = (mish_by_exp(normed) + skip).astype(bf16)
        total += lax.dot_general(
            out_w_ref[h], act, (((1,), (1,)), ((), ())), preferred_element_type=f32
        )
    for b in range(2):
        part = total[:, b * OWN : (b + 1) * OWN].astype(bf16)
        for copy in range(8):
            eps_ref[8 * b + copy] = part


def last_of(conv, own, other, gain, window, res, out_w):
    return pl.pallas_call(
        last_kernel,
        out_shape=jax.ShapeDtypeStruct((16, 32, OWN), bf16),
        in_specs=[pl.BlockSpec(memory_space=pltpu.VMEM)] * 7,
        out_specs=pl.BlockSpec(memory_space=pltpu.VMEM),
        compiler_params=params(24),
        cost_estimate=pl.CostEstimate(
            flops=2 * ROWS * HALF * 80, bytes_accessed=2 * 2**20, transcendentals=ROWS * HALF
        ),
        name="last",
    )(conv, own, other, gain, window, res, out_w)


def body(
    noisy_sample,
    timestep,
    noise,
    obs_feat,
    step_w1,
    step_w2,
    film_weight,
    conv_in_w,
    residual_w,
    conv_mid_w,
    out_w,
    gain_one,
    gain_two,
):
    zq, zp, y, core, zl, x = (lax.axis_index(a) for a in AXES)
    zh = 2 * zq + zp

    packed = jnp.concatenate(
        [
            obs_feat,
            noisy_sample.astype(bf16),
            timestep.astype(f32).astype(bf16)[:, None],
            jnp.zeros((OWN, 99), bf16),
        ],
        axis=1,
    )

    stay = lax.dynamic_index_in_dim(film_weight, core, 1, keepdims=False)
    go = lax.dynamic_index_in_dim(film_weight, 1 - core, 1, keepdims=False)
    come = cores(go)

    pair_place = zp.reshape(1).astype(jnp.int32)
    keep, give = split_of(pair_place, conv_mid_w)
    w_own = lax.all_gather(keep, ("y", "core"), axis=0, tiled=False)
    w_up, w_down = z_up(give), z_down(give)

    chip = jnp.where(
        core == 0, jnp.concatenate([stay, come]), jnp.concatenate([come, stay])
    )
    z_a, z_b, z_c = z_up(chip), z_down(chip), z_two(chip)
    line_a, line_b = jnp.stack([chip, z_a]), jnp.stack([z_b, z_c])
    line_a, line_b, packed, w_up, w_down = tie(line_a, line_b, packed, w_up, w_down)
    down_a, up_a, down_b, up_b = y_up(line_a), y_down(line_a), y_up(line_b), y_down(line_b)
    partner = z_pair(packed)
    w_far = z_two(keep)
    sibling = [cores(line_a), cores(line_b)]
    far_a, far_b = y_up(down_a), y_down(up_b)
    sibling += [cores(piece) for piece in (down_a, down_b, up_a, up_b)]
    w_near = join_of((w_up, w_down), (far_a, far_b, *sibling[:2], down_b, up_a, partner, w_far))
    w_near = lax.all_gather(w_near, ("y", "core"), axis=0, tiled=False)

    cond_blocks, window = cond_of(pair_place, packed, partner, step_w1, step_w2)
    coarse = lax.reduce_precision(gain_one, 8, 7)
    small = jnp.concatenate(
        [
            conv_in_w.reshape(TAPS * ACT, WIDE),
            coarse[None].astype(bf16),
            (gain_one - coarse)[None].astype(bf16),
            jnp.zeros((WIN - 37, WIDE), bf16),
        ]
    )

    dz = (0, -1, 1, 2)
    order = [((zh + dz[r % 4]) % 4) * 4 + (y + dy) % 4 for dy in (0, -1, 1, 2) for r in range(4)]
    order = jnp.stack(order + [core]).astype(jnp.int32)
    side, step = (0, 0, 1, 0, 1, 0, 1, 1), (0, 1, 0, 2, 1, 3, 2, 3)
    slots = [
        (zl if b == 0 else 1 - zl) * 4 + (x + s * (2 * core - 1)) % 4 for b, s in zip(side, step)
    ]
    early = jnp.stack([zh, y, core] + slots[:7]).astype(jnp.int32)
    late = jnp.stack([zh, y, core] + slots[7:]).astype(jnp.int32)
    order, early, late = tie(order, early, late)
    near_pieces = (line_a, line_b, down_a, down_b, up_a, up_b)
    part = film_of(order, cond_blocks, range(12), near_pieces, sibling)
    far_a, far_b, part, small, window, w_far = tie(far_a, far_b, part, small, window, w_far)
    far_sibling = (cores(far_a), cores(far_b))
    film = film_of(order, cond_blocks, range(12, 16), (far_a, far_b), far_sibling, part, small)

    a_one, b_own = x_ring(film), zl_swap(film)
    far_one, other_far = y_ring(w_far), cores(w_far)
    acts = first_of(0, window, film, None)
    a_one, far_one, acts = tie(a_one, far_one, acts)
    a_two, far_two, other_one = x_ring(a_one), y_ring(far_one), cores(far_one)
    acts = first_of(1, window, a_one, acts)
    b_own, acts = tie(b_own, acts)
    b_one = x_ring(b_own)
    acts = first_of(2, window, b_own, acts)
    a_two, far_two, acts = tie(a_two, far_two, acts)
    a_three, far_three, other_two = x_ring(a_two), y_ring(far_two), cores(far_two)
    acts = first_of(3, window, a_two, acts)
    b_one, acts = tie(b_one, acts)
    b_two = x_ring(b_one)
    acts = first_of(4, window, b_one, acts)
    acts = first_of(5, window, a_three, acts)
    b_two, far_three, acts = tie(b_two, far_three, acts)
    b_three, other_three = x_ring(b_two), cores(far_three)
    acts = first_of(6, window, b_two, acts)

    weights = (w_own, w_near, w_far, far_one, far_two, far_three)
    weights += (other_far, other_one, other_two, other_three)
    conv = mid_of(early, 7, acts, weights)
    conv, stats = end_of(late, window, b_three, conv, weights)
    other = z_pair(stats)

    out_h = lax.dynamic_slice_in_dim(out_w, zp * HALF, HALF, 0).T
    out_h = jnp.stack([jnp.pad(out_h, ((7 * h, 25 - 7 * h), (0, 0))) for h in range(HORIZON)])
    res_h = lax.dynamic_slice_in_dim(residual_w, zp * HALF, HALF, 1)
    res_h = jnp.pad(res_h, ((14, WIN - 21), (0, 0)))
    gain_h = lax.dynamic_slice_in_dim(gain_two, zp * HALF, HALF, 0)[None]
    part = last_of(conv, stats, other, gain_h, window, res_h, out_h)

    got = lax.all_to_all(part, ("zp", "zl", "x"), split_axis=0, concat_axis=0, tiled=True)
    eps = jnp.sum(got.astype(f32), axis=0).T[:, :28]

    root_b, root_a, of_start, of_sample, of_noise = denoise_coefficients(timestep)
    start = jnp.clip((noisy_sample - root_b * eps) / root_a, -1.0, 1.0)
    denoised = of_start * start + of_sample * noisy_sample + of_noise * noise
    return (eps, denoised)


def solution(mesh):
    fine = Mesh(mesh.devices.reshape(SIZES), AXES)
    return jax.shard_map(
        body,
        mesh=fine,
        in_specs=(
            P(DP, None),
            P(DP),
            P(DP, None),
            P(DP, None),
            P(),
            P(),
            P(DP, None, TENSOR),
            P(None, None, TENSOR),
            P(None, TENSOR),
            P(None, DP, TENSOR),
            P(TENSOR, None),
            P(TENSOR),
            P(TENSOR),
        ),
        out_specs=(P(DP, None), P(DP, None)),
        check_vma=False,
    )
```

```python
import math

import jax
import jax.numpy as jnp
import numpy as np
from jax import lax
from jax.experimental import pallas as pl
from jax.experimental.pallas import tpu as pltpu
from jax.sharding import Mesh, PartitionSpec as P

C = 4096
ACT = 7
HORIZON = 4
TAPS = 5
GROUPS = 8
STEP = 256
TRAIN_STEPS = 100
COND = 1280

AXES = ("zq", "zp", "y", "core", "zl", "x")
SIZES = (2, 2, 4, 2, 2, 4)
DP = ("zq", "zp", "y", "core")
TENSOR = ("zl", "x")

OWN = 128
PAIR = 256
ROWS = HORIZON * PAIR
WIDE = 512
HALF = 256
WIN = 64
FILM_ROWS = 2 * PAIR + WIN

f32, bf16 = jnp.float32, jnp.bfloat16


def moves(where):
    pairs = []
    for here in np.ndindex(*SIZES):
        zq, zp, y, core, zl, x = here
        zh, y, core, zl, x = where(2 * zq + zp, y, core, zl, x)
        there = ((zh % 4) // 2, zh % 2, y % 4, core % 2, zl % 2, x % 4)
        pairs.append(
            (int(np.ravel_multi_index(here, SIZES)), int(np.ravel_multi_index(there, SIZES)))
        )
    return pairs


def mover(where):
    pairs = moves(where)
    return lambda array: lax.ppermute(array, AXES, pairs)


z_up = mover(lambda zh, y, core, zl, x: (zh + 1, y, core, zl, x))
z_down = mover(lambda zh, y, core, zl, x: (zh - 1, y, core, zl, x))
z_two = mover(lambda zh, y, core, zl, x: (zh + 2, y, core, zl, x))
z_pair = mover(lambda zh, y, core, zl, x: (zh ^ 1, y, core, zl, x))
y_up = mover(lambda zh, y, core, zl, x: (zh, y + 1, core, zl, x))
y_down = mover(lambda zh, y, core, zl, x: (zh, y - 1, core, zl, x))
cores = mover(lambda zh, y, core, zl, x: (zh, y, 1 - core, zl, x))
zl_swap = mover(lambda zh, y, core, zl, x: (zh, y, core, 1 - zl, x))
y_ring = mover(lambda zh, y, core, zl, x: (zh, y + 1 - 2 * core, core, zl, x))
x_ring = mover(lambda zh, y, core, zl, x: (zh, y, core, zl, x + 1 - 2 * core))


def plan():
    pos = np.arange(TRAIN_STEPS + 1, dtype=np.float64) / TRAIN_STEPS
    curve = np.cos((pos + 0.008) / 1.008 * (math.pi / 2)) ** 2
    betas = np.minimum(1.0 - curve[1:] / curve[:-1], 0.999)
    return jnp.asarray(np.cumprod(1.0 - betas), f32)


def lookup(table, steps):
    onehot = (steps[:, None] == jnp.arange(table.shape[0], dtype=jnp.int32)[None, :]).astype(f32)
    return jnp.sum(onehot * table[None, :], axis=1)


def mish_by_exp(value):
    u = jnp.exp(jnp.minimum(value, 20.0))
    w = u * (u + 2.0)
    return value * (w * pltpu.reciprocal(w + 2.0, approx=True))


def tie(*arrays):
    return lax.optimization_barrier(arrays)


def denoise_coefficients(steps):
    alpha_bar = plan()
    now = lookup(alpha_bar, steps)[:, None]
    before = jnp.where(steps > 0, lookup(alpha_bar, jnp.maximum(steps - 1, 0)), 1.0)[:, None]
    beta_prod = 1.0 - now
    cur_alpha = now / before
    cur_beta = 1.0 - cur_alpha
    return (
        jnp.sqrt(beta_prod),
        jnp.sqrt(now),
        jnp.sqrt(before) * cur_beta / beta_prod,
        jnp.sqrt(cur_alpha) * (1.0 - before) / beta_prod,
        jnp.sqrt((1.0 - before) / beta_prod * cur_beta),
    )


IN_VMEM = pl.BlockSpec(memory_space=pltpu.VMEM)
IN_HBM = pl.BlockSpec(memory_space=pltpu.HBM)
LIMIT = 48
EARLY = 5
SLOTS = 16


def params(mib, **more):
    return pltpu.CompilerParams(vmem_limit_bytes=mib * 2**20, **more)


def cond_kernel(place_ref, own_ref, partner_ref, w1_ref, w2_ref, *refs):
    cond_ref, window_ref, held_ref = refs[-3:]
    lane = lax.broadcasted_iota(jnp.int32, (OWN, 128), 1)
    half_step = STEP // 2
    freqs = jnp.exp(lane.astype(f32) * (-math.log(10000.0) / (half_step - 1)))
    for ref, half in ((own_ref, place_ref[0]), (partner_ref, 1 - place_ref[0])):
        tail = ref[:, 1024:].astype(f32)
        angles = tail[:, 28:29] * freqs
        sinus = jnp.concatenate([jnp.sin(angles), jnp.cos(angles)], axis=1).astype(bf16)
        hidden = mish_by_exp(jnp.dot(sinus, w1_ref[...], preferred_element_type=f32)).astype(bf16)
        feat = jnp.dot(hidden, w2_ref[...], preferred_element_type=f32)
        held_ref[:, :STEP] = mish_by_exp(feat)
        held_ref[:, STEP:] = mish_by_exp(ref[:, :1024].astype(f32))
        rows = pl.ds(pl.multiple_of(half * OWN, OWN), OWN)
        for d in range(16):
            cond_ref[d, rows, :] = held_ref[:, 80 * d : 80 * d + 80].astype(bf16)
        samples = jnp.where(lane < 28, tail, 0.0)
        for p in range(HORIZON):
            seen = pltpu.roll(samples, (14 - 7 * p) % 128, 1)
            seen = jnp.where(lane < 35, seen, 0.0).astype(bf16)
            rows = pl.ds(pl.multiple_of(p * PAIR + half * OWN, OWN), OWN)
            window_ref[rows, :] = seen[:, :WIN]


def cond_of(place, own, partner, w1, w2, *after):
    return pl.pallas_call(
        cond_kernel,
        out_shape=[
            jax.ShapeDtypeStruct((16, PAIR, 80), bf16),
            jax.ShapeDtypeStruct((ROWS, WIN), bf16),
        ],
        in_specs=[pl.BlockSpec(memory_space=pltpu.SMEM)] + [IN_VMEM] * 4
        + [pl.BlockSpec(memory_space=pl.ANY)] * len(after),
        out_specs=[IN_VMEM] * 2,
        scratch_shapes=[pltpu.VMEM((OWN, COND), f32)],
        compiler_params=params(16),
        name="cond",
    )(place, own, partner, w1, w2, *after)


def film_kernel(blocks, order_ref, cond_ref, *refs):
    pieces, refs = refs[: len(blocks)], refs[len(blocks) :]
    half = len(blocks) // 2
    more = len(refs) == 3
    for side in range(2):
        total = refs[0][side] if more else jnp.zeros((PAIR, WIDE), f32)
        for at, block in enumerate(blocks):
            total += jnp.dot(
                cond_ref[order_ref[block]],
                pieces[side * half + at // 2][at % 2],
                preferred_element_type=f32,
            )
        if more:
            place = order_ref[16] if side == 0 else 1 - order_ref[16]
            rows = pl.ds(pl.multiple_of(place * PAIR, PAIR), PAIR)
            refs[2][rows, :] = total.astype(bf16)
        else:
            refs[0][side] = total
    if more:
        refs[2][2 * PAIR :, :] = refs[1][...]


def film_of(order, cond_blocks, blocks, mine, sibling, *more):
    out = ((FILM_ROWS, WIDE), bf16) if more else ((2, PAIR, WIDE), f32)
    return pl.pallas_call(
        lambda *refs: film_kernel(blocks, *refs),
        out_shape=jax.ShapeDtypeStruct(*out),
        in_specs=[pl.BlockSpec(memory_space=pltpu.SMEM)]
        + [IN_VMEM] * (1 + len(blocks) + len(more)),
        out_specs=IN_VMEM,
        compiler_params=params(16),
        cost_estimate=pl.CostEstimate(flops=1, bytes_accessed=1, transcendentals=0),
        name="film",
    )(order, cond_blocks, *mine, *sibling, *more)


def split_kernel(place_ref, weight_ref, keep_ref, give_ref):
    for ref, which in ((keep_ref, place_ref[0]), (give_ref, 1 - place_ref[0])):
        at = pl.ds(pl.multiple_of(which * HALF, HALF), HALF)
        for k in range(TAPS):
            ref[:, k * HALF : (k + 1) * HALF] = weight_ref[k, :, at]


def split_of(place, weight):
    return pl.pallas_call(
        split_kernel,
        out_shape=[jax.ShapeDtypeStruct((OWN, TAPS * HALF), bf16)] * 2,
        in_specs=[pl.BlockSpec(memory_space=pltpu.SMEM), IN_VMEM],
        out_specs=[IN_VMEM] * 2,
        compiler_params=params(16),
        name="split",
    )(place, weight)


def first_rows(window_ref, film_ref, hidden_ref, act_ref, after):
    hidden_ref[...] = jnp.dot(
        window_ref[...], film_ref[2 * PAIR :, :], preferred_element_type=f32
    )
    gain = (
        film_ref[2 * PAIR + 35 : 2 * PAIR + 36, :].astype(f32)
        + film_ref[2 * PAIR + 36 : 2 * PAIR + 37, :].astype(f32)
    )

    def lanes(value):
        return sum(value[:, c : c + 128] for c in range(0, WIDE, 128))

    parts = [slice(p * PAIR, (p + 1) * PAIR) for p in range(HORIZON)]
    total = sum(lanes(hidden_ref[a, :]) for a in parts)
    mean = jnp.sum(total, axis=1, keepdims=True) * (1.0 / (HORIZON * WIDE))
    total = sum(lanes((hidden_ref[a, :] - mean) ** 2) for a in parts)
    var = jnp.sum(total, axis=1, keepdims=True) * (1.0 / (HORIZON * WIDE))
    inv = lax.rsqrt(var + 1e-05)
    few = 16
    for r in range(0, PAIR, few):
        at = slice(r, r + few)
        scale = film_ref[at, :].astype(f32)
        shift = film_ref[PAIR + r : PAIR + r + few, :].astype(f32)
        for p in range(HORIZON):
            a = slice(p * PAIR + r, p * PAIR + r + few)
            normed = (hidden_ref[a, :] - mean[at]) * (inv[at] * gain)
            act_ref[p, at, :] = (scale * mish_by_exp(normed) + shift).astype(bf16)
        after(r + few)


def first_kernel(slot, window_ref, film_ref, *rest):
    out_ref, hidden_ref, act_ref, sem = rest[-4:]
    out_ref, some = out_ref.at[slot], 64

    def after(rows):
        if rows % some == 0:
            done = slice(rows - some, rows)
            pltpu.make_async_copy(act_ref.at[:, done], out_ref.at[:, done], sem).start()

    first_rows(window_ref, film_ref, hidden_ref, act_ref, after)
    pltpu.make_async_copy(act_ref, out_ref, sem).wait()


def first_of(slot, window, film, before, *after):
    more = [] if before is None else [before, *after]
    return pl.pallas_call(
        lambda *refs: first_kernel(slot, *refs),
        out_shape=jax.ShapeDtypeStruct((SLOTS, HORIZON, PAIR, WIDE), bf16),
        in_specs=[IN_VMEM, IN_VMEM] + [IN_HBM] * len(more),
        out_specs=IN_HBM,
        scratch_shapes=[
            pltpu.VMEM((ROWS, WIDE), f32),
            pltpu.VMEM((HORIZON, PAIR, WIDE), bf16),
            pltpu.SemaphoreType.DMA,
        ],
        input_output_aliases={2: 0} if more else {},
        compiler_params=params(LIMIT),
        cost_estimate=pl.CostEstimate(flops=1, bytes_accessed=1, transcendentals=0),
        name="first",
    )(window, film, *more)


def fetch_weights(place_ref, block, refs, into, sem):
    own_ref, near_ref, mine_refs, theirs_refs = refs[0], refs[1], refs[2:6], refs[6:10]
    zh, y, core = place_ref[0], place_ref[1], place_ref[2]
    q, apart = block % 2, (block // 2 + 4 - zh) % 4

    @pl.when(apart == 0)
    def _():
        pltpu.make_async_copy(own_ref.at[pl.ds(4 * q, 4)], into, sem).start()

    for way, side in ((3, 0), (1, 1)):

        @pl.when(apart == way)
        def _():
            pltpu.make_async_copy(near_ref.at[pl.ds(4 * q, 4), side], into, sem).start()

    for odd in range(2):
        for far_refs, its in ((mine_refs, core), (theirs_refs, 1 - core)):
            steps = ((1 - 2 * its) * (y - 2 * q - odd) + 8) % 4
            for j in range(4):

                @pl.when(jnp.logical_and(apart == 2, steps == j))
                def _():
                    pltpu.make_async_copy(far_refs[j], into.at[2 * odd + its], sem).start()


def add_block(act, weight, before_ref, out_ref):
    for h in range(HORIZON):
        at = slice(h * PAIR, (h + 1) * PAIR)
        total = None if before_ref is None else before_ref[at, :]
        for p in range(HORIZON):
            k = p - h + 2
            if 0 <= k < TAPS:
                term = jnp.dot(
                    act[p],
                    weight[:, :, k * HALF : (k + 1) * HALF].reshape(WIDE, HALF),
                    preferred_element_type=f32,
                )
                total = term if total is None else total + term
        out_ref[at, :] = total


def mid_kernel(count, early, place_ref, acts_ref, *refs):
    out_ref, held, act_held, sems = refs[-4:]
    if early:
        weights = (*refs[:2], *[refs[0].at[0]] * 8)
        out_ref[...] = jnp.zeros_like(out_ref)
    else:
        weights = refs[:10]
        out_ref[...] = refs[10][...]

    def mine(step):
        far = (place_ref[3 + step] // 2 + 4 - place_ref[0]) % 4 == 2
        return jnp.logical_not(far) if early else jnp.logical_or(far, step >= EARLY)

    def fetch(step):
        at = step % 3

        @pl.when(mine(step))
        def _():
            pltpu.make_async_copy(acts_ref.at[step], act_held.at[at], sems.at[1, at]).start()
            fetch_weights(place_ref, place_ref[3 + step], weights, held.at[at], sems.at[0, at])

    for step in range(2):
        fetch(step)
    for step in range(count):
        if step + 2 < count:
            fetch(step + 2)
        at = step % 3

        @pl.when(mine(step))
        def _():
            pltpu.make_async_copy(weights[0].at[pl.ds(0, 4)], held.at[at], sems.at[0, at]).wait()
            pltpu.make_async_copy(acts_ref.at[step], act_held.at[at], sems.at[1, at]).wait()
            add_block(act_held.at[at], held.at[at], out_ref, out_ref)


def mid_of(place, count, acts, weights, *before):
    return pl.pallas_call(
        lambda *refs: mid_kernel(count, not before, *refs),
        out_shape=jax.ShapeDtypeStruct((ROWS, HALF), f32),
        in_specs=[pl.BlockSpec(memory_space=pltpu.SMEM)]
        + [IN_HBM] * (1 + len(weights))
        + [IN_VMEM] * len(before),
        out_specs=IN_VMEM,
        scratch_shapes=[
            pltpu.VMEM((3, 4, OWN, TAPS * HALF), bf16),
            pltpu.VMEM((3, HORIZON, PAIR, WIDE), bf16),
            pltpu.SemaphoreType.DMA((2, 3)),
        ],
        compiler_params=params(LIMIT),
        cost_estimate=pl.CostEstimate(flops=1, bytes_accessed=1, transcendentals=0),
        name="mid",
    )(place, acts, *weights, *before)


def end_kernel(place_ref, window_ref, film_ref, before_ref, *refs):
    out_ref, stats_ref, hidden_ref, act_ref, held, sem = refs[-6:]
    weights = refs[:10]
    fetch_weights(place_ref, place_ref[3], weights, held, sem)
    first_rows(window_ref, film_ref, hidden_ref, act_ref, lambda rows: None)
    pltpu.make_async_copy(weights[0].at[pl.ds(0, 4)], held, sem).wait()
    add_block(act_ref, held, before_ref, out_ref)
    parts = [out_ref[h * PAIR : (h + 1) * PAIR, :] for h in range(HORIZON)]
    mean = jnp.sum(sum(parts), axis=1, keepdims=True) * (1.0 / (HORIZON * HALF))
    spread = jnp.sum(sum((o - mean) ** 2 for o in parts), axis=1, keepdims=True)
    lane = lax.broadcasted_iota(jnp.int32, (PAIR, 128), 1)
    both = jnp.where(lane == 0, mean, jnp.where(lane == 1, spread, 0.0))
    stats_ref[...] = both.T[:8, :]


def end_of(place, window, film, before, weights):
    return pl.pallas_call(
        end_kernel,
        out_shape=[
            jax.ShapeDtypeStruct((ROWS, HALF), f32),
            jax.ShapeDtypeStruct((8, PAIR), f32),
        ],
        in_specs=[pl.BlockSpec(memory_space=pltpu.SMEM)] + [IN_VMEM] * 3 + [IN_HBM] * 10,
        out_specs=[IN_VMEM] * 2,
        scratch_shapes=[
            pltpu.VMEM((ROWS, WIDE), f32),
            pltpu.VMEM((HORIZON, PAIR, WIDE), bf16),
            pltpu.VMEM((4, OWN, TAPS * HALF), bf16),
            pltpu.SemaphoreType.DMA,
        ],
        compiler_params=params(LIMIT),
        cost_estimate=pl.CostEstimate(flops=1, bytes_accessed=1, transcendentals=0),
        name="end",
    )(place, window, film, before, *weights)


def last_kernel(conv_ref, own_ref, other_ref, gain_ref, window_ref, res_ref, out_w_ref, eps_ref):
    rows = jnp.concatenate([own_ref[...], other_ref[...], jnp.zeros((112, PAIR), f32)], axis=0).T
    mean_a, spread_a = rows[:, 0:1], rows[:, 1:2]
    mean_b, spread_b = rows[:, 8:9], rows[:, 9:10]
    each = HORIZON * HALF
    mean = 0.5 * (mean_a + mean_b)
    var = (spread_a + spread_b + (mean_a - mean_b) ** 2 * (0.5 * each)) * (0.5 / each)
    inv = lax.rsqrt(var + 1e-05)
    total = jnp.zeros((32, PAIR), f32)
    for h in range(HORIZON):
        at = slice(h * PAIR, (h + 1) * PAIR)
        normed = (conv_ref[at, :] - mean) * inv * gain_ref[...]
        skip = jnp.dot(window_ref[at, :], res_ref[...], preferred_element_type=f32)
        act = (mish_by_exp(normed) + skip).astype(bf16)
        total += lax.dot_general(
            out_w_ref[h], act, (((1,), (1,)), ((), ())), preferred_element_type=f32
        )
    for b in range(2):
        part = total[:, b * OWN : (b + 1) * OWN].astype(bf16)
        for copy in range(8):
            eps_ref[8 * b + copy] = part


def last_of(conv, own, other, gain, window, res, out_w):
    return pl.pallas_call(
        last_kernel,
        out_shape=jax.ShapeDtypeStruct((16, 32, OWN), bf16),
        in_specs=[pl.BlockSpec(memory_space=pltpu.VMEM)] * 7,
        out_specs=pl.BlockSpec(memory_space=pltpu.VMEM),
        compiler_params=params(24),
        cost_estimate=pl.CostEstimate(
            flops=2 * ROWS * HALF * 80, bytes_accessed=2 * 2**20, transcendentals=ROWS * HALF
        ),
        name="last",
    )(conv, own, other, gain, window, res, out_w)


def body(
    noisy_sample,
    timestep,
    noise,
    obs_feat,
    step_w1,
    step_w2,
    film_weight,
    conv_in_w,
    residual_w,
    conv_mid_w,
    out_w,
    gain_one,
    gain_two,
):
    zq, zp, y, core, zl, x = (lax.axis_index(a) for a in AXES)
    zh = 2 * zq + zp

    packed = jnp.concatenate(
        [
            obs_feat,
            noisy_sample.astype(bf16),
            timestep.astype(f32).astype(bf16)[:, None],
            jnp.zeros((OWN, 99), bf16),
        ],
        axis=1,
    )

    stay = lax.dynamic_index_in_dim(film_weight, core, 1, keepdims=False)
    go = lax.dynamic_index_in_dim(film_weight, 1 - core, 1, keepdims=False)
    come = cores(go)

    pair_place = zp.reshape(1).astype(jnp.int32)
    keep, give = split_of(pair_place, conv_mid_w)
    w_own = lax.all_gather(keep, ("y", "core"), axis=0, tiled=False)
    w_up, w_down = z_up(give), z_down(give)

    chip = jnp.where(
        core == 0, jnp.concatenate([stay, come]), jnp.concatenate([come, stay])
    )
    z_a, z_b, z_c = z_up(chip), z_down(chip), z_two(chip)
    line_a, line_b = jnp.stack([chip, z_a]), jnp.stack([z_b, z_c])
    line_a, line_b, packed, w_up, w_down = tie(line_a, line_b, packed, w_up, w_down)
    down_a, up_a, down_b, up_b = y_up(line_a), y_down(line_a), y_up(line_b), y_down(line_b)
    partner = z_pair(packed)
    sibling = [cores(line_a), cores(line_b)]
    down_a, *sibling = tie(down_a, *sibling)
    far_a = y_up(down_a)
    up_b, *sibling = tie(up_b, *sibling)
    far_b = y_down(up_b)
    sibling += [cores(piece) for piece in (down_a, down_b, up_a, up_b)]
    partner, keep = tie(partner, keep)
    w_far = z_two(keep)
    w_near = lax.all_gather(jnp.stack([w_up, w_down]), ("y", "core"), axis=0, tiled=False)

    cond_blocks, window = cond_of(pair_place, packed, partner, step_w1, step_w2, far_a, far_b)
    coarse = lax.reduce_precision(gain_one, 8, 7)
    small = jnp.concatenate(
        [
            conv_in_w.reshape(TAPS * ACT, WIDE),
            coarse[None].astype(bf16),
            (gain_one - coarse)[None].astype(bf16),
            jnp.zeros((WIN - 37, WIDE), bf16),
        ]
    )

    dz = (0, -1, 1, 2)
    order = [((zh + dz[r % 4]) % 4) * 4 + (y + dy) % 4 for dy in (0, -1, 1, 2) for r in range(4)]
    order = jnp.stack(order + [core]).astype(jnp.int32)
    side, step = (0, 0, 1, 0, 1, 0, 1, 1), (0, 1, 0, 2, 1, 3, 2, 3)
    slots = [
        (zl if b == 0 else 1 - zl) * 4 + (x + s * (2 * core - 1)) % 4 for b, s in zip(side, step)
    ]
    early = jnp.stack([zh, y, core] + slots[:7]).astype(jnp.int32)
    late = jnp.stack([zh, y, core] + slots[7:]).astype(jnp.int32)
    order, early, late = tie(order, early, late)
    near_pieces = (line_a, line_b, down_a, down_b, up_a, up_b)
    part = film_of(order, cond_blocks, range(12), near_pieces, sibling)
    far_a, far_b, part, small, window, w_far = tie(far_a, far_b, part, small, window, w_far)
    far_sibling = (cores(far_a), cores(far_b))
    film = film_of(order, cond_blocks, range(12, 16), (far_a, far_b), far_sibling, part, small)

    a_one, b_own = x_ring(film), zl_swap(film)
    far_one, other_far = y_ring(w_far), cores(w_far)
    acts = first_of(0, window, film, None)
    a_one, far_one, acts = tie(a_one, far_one, acts)
    a_two, far_two, other_one = x_ring(a_one), y_ring(far_one), cores(far_one)
    acts = first_of(1, window, a_one, acts)
    b_own, acts = tie(b_own, acts)
    b_one = x_ring(b_own)
    acts = first_of(2, window, b_own, acts)
    a_two, far_two, acts = tie(a_two, far_two, acts)
    a_three, far_three, other_two = x_ring(a_two), y_ring(far_two), cores(far_two)
    acts = first_of(3, window, a_two, acts)
    b_one, acts = tie(b_one, acts)
    b_two = x_ring(b_one)
    acts = first_of(4, window, b_one, acts)
    conv = mid_of(early, EARLY, acts, (w_own, w_near))
    acts = first_of(5, window, a_three, acts, conv)
    b_two, far_three, acts = tie(b_two, far_three, acts)
    b_three, other_three = x_ring(b_two), cores(far_three)
    acts = first_of(6, window, b_two, acts)

    weights = (w_own, w_near, w_far, far_one, far_two, far_three)
    weights += (other_far, other_one, other_two, other_three)
    conv = mid_of(early, 7, acts, weights, conv)
    conv, stats = end_of(late, window, b_three, conv, weights)
    other = z_pair(stats)

    out_h = lax.dynamic_slice_in_dim(out_w, zp * HALF, HALF, 0).T
    out_h = jnp.stack([jnp.pad(out_h, ((7 * h, 25 - 7 * h), (0, 0))) for h in range(HORIZON)])
    res_h = lax.dynamic_slice_in_dim(residual_w, zp * HALF, HALF, 1)
    res_h = jnp.pad(res_h, ((14, WIN - 21), (0, 0)))
    gain_h = lax.dynamic_slice_in_dim(gain_two, zp * HALF, HALF, 0)[None]
    part = last_of(conv, stats, other, gain_h, window, res_h, out_h)

    got = lax.all_to_all(part, ("zp", "zl", "x"), split_axis=0, concat_axis=0, tiled=True)
    eps = jnp.sum(got.astype(f32), axis=0).T[:, :28]

    root_b, root_a, of_start, of_sample, of_noise = denoise_coefficients(timestep)
    start = jnp.clip((noisy_sample - root_b * eps) / root_a, -1.0, 1.0)
    denoised = of_start * start + of_sample * noisy_sample + of_noise * noise
    return (eps, denoised)


def solution(mesh):
    fine = Mesh(mesh.devices.reshape(SIZES), AXES)
    return jax.shard_map(
        body,
        mesh=fine,
        in_specs=(
            P(DP, None),
            P(DP),
            P(DP, None),
            P(DP, None),
            P(),
            P(),
            P(DP, None, TENSOR),
            P(None, None, TENSOR),
            P(None, TENSOR),
            P(None, DP, TENSOR),
            P(TENSOR, None),
            P(TENSOR),
            P(TENSOR),
        ),
        out_specs=(P(DP, None), P(DP, None)),
        check_vma=False,
    )
```
